32 devices in a mesh: section: 2 (over y), dp: 16 (over z, x, core).
Axes of the slice: x: 2, y: 2, z: 4, core: 2. Of those that a mesh axis runs over, the one named last changes fastest.
Arguments:
- inputs: bfloat16 [2, 2, 16, 1024, 512], P('section', None, 'dp'), may hold values from -6 to 6
- positions: float32 [2, 1024, 512], P('section', None, 'dp'), may hold values from -6 to 6
- projections: float32 [2, 4, 512, 512], P('section', None, 'dp'), may hold values from -0.25 to 0.25
- out_projections: float32 [2, 2, 512, 512], P('section', None, 'dp'), may hold values from -0.75 to 0.75
- ffn_up: float32 [2, 512, 2048], P('section', 'dp'), may hold values from -0.25 to 0.25
- ffn_down: float32 [2, 2048, 512], P('section', 'dp'), may hold values from -0.125 to 0.125
- norm_gains: float32 [2, 3, 512], P('section', None, 'dp'), may hold values from 0.5 to 1.5
- segments: int32 [2, 16, 1024], P(None, 'dp'), may hold values from 0 to 31, never falling along the last dimension, each value on 1 to 64 neighbouring positions
- levels: int32 [2, 2, 16, 1024], P(None, None, 'dp'), may hold values from 0 to 7
- cotangent: bfloat16 [2, 16, 1024, 512], P(None, 'dp'), may hold values from -6 to 6
Outputs:
- section_outputs: bfloat16 [2, 2, 16, 1024, 512], P('section', None, 'dp')
- grad_inputs: float32 [2, 2, 16, 1024, 512], P('section', None, 'dp')
- grad_positions: float32 [2, 1024, 512], P('section', None, 'dp')
- grad_projections: float32 [2, 4, 512, 512], P('section', None, 'dp')
- grad_out_projections: float32 [2, 2, 512, 512], P('section', None, 'dp')
- grad_ffn_up: float32 [2, 512, 2048], P('section', 'dp')
- grad_ffn_down: float32 [2, 2048, 512], P('section', 'dp')
- grad_norm_gains: float32 [2, 3, 512], P('section', None, 'dp')
The draws below stay inside these ranges and needn't reach their ends.
Inputs may be any that keep to these rules, and one draw needn't show every extreme that they name: `segments`: in each row of 1024 positions the ids never fall, and each sentence holds 1 to 64 positions. levels[0] is 0 at padded source positions.
All inputs are finite; a program needn't handle non-finite values.
Results may differ from the reference program's by a relative error of at most 0.02.
The reference program's roundings to bfloat16 on the way count: a program that leaves them out, or rounds other values in their place, can miss the bound.
Values may be sent and summed in bfloat16 or wider, within the bound.
A program may use at most 704 MiB of HBM per device.

```python
import math
import jax
import jax.numpy as jnp
import numpy as np
from jax import lax

D = 512
H = 8
DH = 64
FF = 2048
SEQ = 1024
MB = 2
NROWS = 16


def set_ends(drawn, key, least, high):
    index_at = [jax.random.randint(jax.random.fold_in(key, axis), (), 0, length) for axis, length in enumerate(drawn.shape)]
    longest = drawn.shape.index(max(drawn.shape))
    next_to = index_at[:longest] + [(index_at[longest] + 1) % drawn.shape[longest]] + index_at[longest + 1:]
    return drawn.at[tuple(index_at)].set(least).at[tuple(next_to)].set(high)


def block_scale(rng, shape, pieces, smallest, high):
    factor_of = 1.0
    for position, shards_of in pieces:
        heights = jax.random.uniform(jax.random.fold_in(jax.random.fold_in(rng, 6), position), (shards_of,), jnp.float32, smallest / len(pieces), high / len(pieces))
        factor_of = factor_of * jnp.repeat(jnp.exp(heights), shape[position] // shards_of).reshape((-1,) + (1,) * (len(shape) - 1 - position))
    return factor_of


def profile(count, total, limit, skew):
    portions = [(1 << 20) // math.isqrt(grade ** skew) + 1 for grade in range(2, count + 1)]
    rest, given = total - limit - (count - 1), [1] * (count - 1)
    while rest > 0:
        free = [i for i in range(count - 1) if given[i] < limit]
        whole, left = sum([portions[i] for i in free]), rest
        for i in free:
            extra = min(limit - given[i], max(1, left * portions[i] // whole), rest)
            given[i] = given[i] + extra
            rest = rest - extra
    return np.array([limit] + given)


def uneven(stream_key, amount, total, bound, slope):
    if amount == 2:
        one = jax.random.randint(stream_key, (), max(1, total - bound), min(bound, total - 1) + 1)
        return jnp.stack([one, total - one])
    tallies = jnp.asarray(profile(amount, total, bound, slope), jnp.int32)
    couples = (amount - 1) // 2
    donor, receiver = tallies[1:1 + 2 * couples:2], tallies[2:2 + 2 * couples:2]
    slack = jnp.minimum(donor - 1, bound - receiver)
    shifted = jax.random.randint(jax.random.fold_in(stream_key, 1), (couples,), 0, 1 << 20) % (slack + 1)
    tallies = tallies.at[1:1 + 2 * couples:2].set(donor - shifted).at[2:2 + 2 * couples:2].set(receiver + shifted)
    return tallies[jax.random.permutation(jax.random.fold_in(stream_key, 2), amount)]


def bell_draw(key, extent, scale, most, shards=(), kind=jnp.bfloat16):
    values = jax.random.normal(key, extent, jnp.float32) * scale
    if len(shards) > 0:
        values = block_scale(key, extent, shards, -0.22, 0.18) * values
    return jnp.clip(values, min=-most, max=most).astype(kind)


def setup_inputs(seed: int = 0) -> dict:
    key_list = jax.random.split(jax.random.key(seed), 11)
    return {
        "inputs": bell_draw(key_list[0], (2, MB, NROWS, SEQ, D), 1.0, 6.0, ((0, 2), (2, 16))),
        "positions": bell_draw(key_list[1], (2, SEQ, D), 1.0, 6.0, ((0, 2), (2, 16)), jnp.float32),
        "projections": bell_draw(key_list[2], (2, 4, D, D), D ** -0.5, 0.25, ((0, 2), (2, 16)), jnp.float32),
        "out_projections": bell_draw(key_list[3], (2, 2, D, D), (D // 8) ** -0.5, 0.75, ((0, 2), (2, 16)), jnp.float32),
        "ffn_up": bell_draw(key_list[4], (2, D, FF), D ** -0.5, 0.25, ((0, 2), (1, 16)), jnp.float32),
        "ffn_down": bell_draw(key_list[5], (2, FF, D), FF ** -0.5, 0.125, ((0, 2), (1, 16)), jnp.float32),
        "norm_gains": jnp.clip(1.0 + 0.1 * jax.random.normal(key_list[6], (2, 3, D), jnp.float32), 0.5, 1.5),
        "segments": jax.vmap(lambda own: jnp.searchsorted(jnp.cumsum(uneven(own, 32, SEQ, SEQ // 16, 0)), jnp.arange(SEQ), side="right"))(jax.random.split(key_list[7], MB * NROWS)).reshape((MB, NROWS, SEQ)).astype(jnp.int32),
        "levels": set_ends(jax.random.randint(key_list[8], (2, MB, NROWS, SEQ), 0, 8), jax.random.fold_in(key_list[8], 1), 0, 7).astype(jnp.int32),
        "cotangent": bell_draw(key_list[9], (MB, NROWS, SEQ, D), 1.0, 6.0, ((1, 16),)),
    }


@jax.custom_vjp
def low(v):
    return lax.optimization_barrier(v.astype(jnp.bfloat16)).astype(jnp.float32)

@jax.custom_vjp
def low_back(v):
    return v

def low_keep(v):
    return (low(v), None)

def low_pass(kept, grad):
    return (grad,)

def back_keep(v):
    return (v, None)

def back_low(kept, grad):
    return (low(grad),)
low.defvjp(low_keep, low_pass)
low_back.defvjp(back_keep, back_low)
highest = lax.Precision.HIGHEST

def rounded(value):
    return low(low_back(value))

def product(left, right):
    return jnp.dot(left, right, precision=highest, preferred_element_type=jnp.float32)

def layer_norm(stream, gain_vector):
    average = lax.optimization_barrier(jnp.mean(stream, axis=-1, keepdims=True))
    centred = stream - average
    variance = lax.optimization_barrier(jnp.mean(centred * centred, axis=-1, keepdims=True))
    return gain_vector * centred * lax.rsqrt(variance + 1e-05)

def usable_keys(segment_row, level_row):
    starts = jnp.concatenate([jnp.ones((1,), bool), segment_row[1:] != segment_row[:-1]])
    return (level_row > 0) | starts

def attend(queries, key_rows, value_rows, allowed):
    length = queries.shape[0]
    query_heads = queries.reshape(length, H, DH)
    key_heads = key_rows.reshape(-1, H, DH)
    value_heads = value_rows.reshape(-1, H, DH)
    scores = jnp.einsum('qhd,khd->hqk', query_heads, key_heads, precision=highest) * DH ** (-0.5)
    scores = low_back(jnp.where(allowed[None], scores, -1e+30))
    weights = low(jax.nn.softmax(scores, axis=-1))
    mixed_heads = jnp.einsum('hqk,khd->qhd', weights, value_heads, precision=highest)
    return rounded(mixed_heads.reshape(length, H * DH))

def feed(stream, gain_vector, up_weight, down_weight):
    normed = low(layer_norm(stream, gain_vector))
    hidden = low(jax.nn.gelu(low_back(product(normed, up_weight)), approximate=False))
    return low_back(product(hidden, down_weight))

def encode(source, table, segment_row, level_row, inner_weights, outer_weights, up_weight, down_weight, gain_rows):
    stream = source + table
    normed = low(layer_norm(stream, gain_rows[0]))
    queries = rounded(product(normed, inner_weights[0]))
    key_rows = rounded(product(normed, inner_weights[1]))
    value_rows = rounded(product(normed, inner_weights[2]))
    same_segment = segment_row[:, None] == segment_row[None, :]
    allowed = same_segment & usable_keys(segment_row, level_row)[None, :]
    stream = stream + low_back(product(attend(queries, key_rows, value_rows, allowed), outer_weights[0]))
    stream = stream + feed(stream, gain_rows[1], up_weight, down_weight)
    memory = low(layer_norm(stream, gain_rows[2]))
    return (memory, rounded(product(memory, inner_weights[3])), rounded(product(memory, outer_weights[1])))

def decode(target, table, segment_row, source_level, target_level, cross_keys, cross_values, inner_weights, outer_weights, up_weight, down_weight, gain_rows):
    embedded = target + table
    stream = table
    normed = low(layer_norm(stream, gain_rows[0]))
    normed_keys = low(layer_norm(embedded, gain_rows[0]))
    queries = rounded(product(normed, inner_weights[0]))
    key_rows = rounded(product(normed_keys, inner_weights[1]))
    value_rows = rounded(product(normed_keys, inner_weights[2]))
    length = target.shape[0]
    same_segment = segment_row[:, None] == segment_row[None, :]
    visible = (target_level[None, :] < target_level[:, None]) | jnp.eye(length, dtype=bool)
    stream = stream + low_back(product(attend(queries, key_rows, value_rows, same_segment & visible), outer_weights[0]))
    normed_cross = low(layer_norm(stream, gain_rows[1]))
    cross_queries = rounded(product(normed_cross, inner_weights[3]))
    cross_allowed = same_segment & usable_keys(segment_row, source_level)[None, :]
    stream = stream + low_back(product(attend(cross_queries, cross_keys, cross_values, cross_allowed), outer_weights[1]))
    return stream + feed(stream, gain_rows[2], up_weight, down_weight)

def reference(inputs, positions, projections, out_projections, ffn_up, ffn_down, norm_gains, segments, levels, cotangent):
    total_rows = MB * NROWS
    streams = inputs.astype(jnp.float32).reshape(2, total_rows, SEQ, D)
    segment_rows = segments.reshape(total_rows, SEQ)
    level_rows = levels.reshape(2, total_rows, SEQ)

    def forward(streams, positions, projections, out_projections, ffn_up, ffn_down, norm_gains):
        tables = low(positions)
        inner_all = low(projections)
        outer_all = low(out_projections)
        up_weights = low(ffn_up)
        down_weights = low(ffn_down)
        gain_all = low(norm_gains)

        def one_row(running, packed):
            source, target, segment_row, source_level, target_level = packed
            memory, cross_keys, cross_values = encode(source, tables[0], segment_row, source_level, inner_all[0], outer_all[0], up_weights[0], down_weights[0], gain_all[0])
            result = decode(target, tables[1], segment_row, source_level, target_level, cross_keys, cross_values, inner_all[1], outer_all[1], up_weights[1], down_weights[1], gain_all[1])
            return (running, (memory, result))
        _, outputs = lax.scan(jax.checkpoint(one_row), jnp.zeros((), jnp.float32), (streams[0], streams[1], segment_rows, level_rows[0], level_rows[1]))
        return outputs
    (memories, results), pullback = jax.vjp(forward, streams, positions, projections, out_projections, ffn_up, ffn_down, norm_gains)
    gradients = pullback((jnp.zeros_like(memories), cotangent.astype(jnp.float32).reshape(total_rows, SEQ, D)))
    section_outputs = jnp.stack([memories, results]).astype(jnp.bfloat16).reshape(2, MB, NROWS, SEQ, D)
    return (section_outputs, gradients[0].reshape(2, MB, NROWS, SEQ, D), gradients[1], gradients[2], gradients[3], gradients[4], gradients[5], gradients[6])
```

```python
from functools import partial

import jax
import jax.numpy as jnp
from jax import lax
from jax.experimental import pallas as pl
from jax.experimental.pallas import tpu as pltpu
from jax.sharding import PartitionSpec as P

BF = jnp.bfloat16
F32 = jnp.float32
DH = 64
PAIR = 2 * DH
QB = 128
WIN = 256
TB = 256
VMEM_BYTES = 60 * 1024 * 1024


def nn(left, right):
    return jnp.dot(left, right, preferred_element_type=F32)


def nt(left, right):
    return lax.dot_general(left, right, (((1,), (1,)), ((), ())), preferred_element_type=F32)


def tn(left, right):
    return lax.dot_general(left, right, (((0,), (0,)), ((), ())), preferred_element_type=F32)


def norm_parts(stream):
    centred = stream - jnp.mean(stream, axis=-1, keepdims=True)
    scale = lax.rsqrt(jnp.mean(centred * centred, axis=-1, keepdims=True) + 1e-05)
    return centred * scale, scale


def norm_back(grad, unit, scale, gain):
    inner = grad * gain
    first = jnp.mean(inner, axis=-1, keepdims=True)
    second = jnp.mean(inner * unit, axis=-1, keepdims=True)
    return scale * (inner - first - unit * second), jnp.sum(grad * unit, axis=0, keepdims=True)


def block_at(index, size):
    return pl.ds(pl.multiple_of(index * size, size), size)


def lane_halves(scale=1.0):
    lane = lax.broadcasted_iota(jnp.int32, (1, PAIR), 1)
    low = jnp.where(lane < DH, scale, 0.0).astype(BF)
    high = jnp.where(lane < DH, 0.0, scale).astype(BF)
    return low, high


def both_heads(block, halves):
    return jnp.concatenate([block * halves[0], block * halves[1]], axis=0)


def join_heads(stacked):
    lane = lax.broadcasted_iota(jnp.int32, (QB, PAIR), 1)
    return jnp.where(lane < DH, stacked[:QB], stacked[QB:])


def window_start(index, length):
    return pl.multiple_of(jnp.clip(index * QB - DH, 0, length - WIN), DH)


def mask_bias(index, start, cols_ref, rows_ref, causal):
    keys = cols_ref[pl.ds(start, WIN), :]
    query_segment = rows_ref[0, pl.ds(index, 1), :]
    if causal:
        query_level = rows_ref[1, pl.ds(index, 1), :]
        key_id = start + lax.broadcasted_iota(jnp.int32, (WIN, QB), 0)
        query_id = index * QB + lax.broadcasted_iota(jnp.int32, (WIN, QB), 1)
        allowed = (keys[:, 1:2] == query_segment) & (
            (keys[:, 2:3] < query_level) | (key_id == query_id)
        )
    else:
        allowed = keys[:, 0:1] == query_segment
    bias = jnp.where(allowed, 0.0, -1e30)
    return jnp.concatenate([bias, bias], axis=1)


def attend_block(index, q_ref, k_ref, v_ref, cols_ref, rows_ref, weights_ref, mixed_ref, causal):
    length, width = q_ref.shape
    start = window_start(index, length)
    rows = block_at(index, QB)
    bias = mask_bias(index, start, cols_ref, rows_ref, causal)
    halves = lane_halves(DH ** -0.5)
    for pair in range(width // PAIR):
        lanes = slice(pair * PAIR, (pair + 1) * PAIR)
        queries = both_heads(q_ref[rows, lanes], halves)
        scores = nt(k_ref[pl.ds(start, WIN), lanes], queries) + bias
        shifted = jnp.exp(scores - jnp.max(scores, axis=0, keepdims=True))
        weights = (shifted * (1.0 / jnp.sum(shifted, axis=0, keepdims=True))).astype(BF)
        weights_ref[index, pair] = weights
        out = tn(weights, v_ref[pl.ds(start, WIN), lanes])
        mixed_ref[rows, lanes] = join_heads(out).astype(BF)


def attend_back_block(
    index, q_ref, k_ref, v_ref, weights_ref, mixed_ref, dmixed_ref, dq_ref, dk_ref, dv_ref
):
    length, width = q_ref.shape
    start = window_start(index, length)
    rows = block_at(index, QB)
    window = pl.ds(start, WIN)
    plain = lane_halves()
    halves = lane_halves(DH ** -0.5)
    ones = jnp.ones((WIN, PAIR), BF)
    for pair in range(width // PAIR):
        lanes = slice(pair * PAIR, (pair + 1) * PAIR)
        queries = both_heads(q_ref[rows, lanes], halves)
        keys = k_ref[window, lanes]
        values = v_ref[window, lanes]
        weights = weights_ref[index, pair]
        dmixed = dmixed_ref[rows, lanes]
        grads = both_heads(dmixed, plain)
        inner = (dmixed.astype(F32) * mixed_ref[rows, lanes].astype(F32) * -1.0).astype(BF)
        left = jnp.concatenate([values, ones], axis=1)
        right = jnp.concatenate([grads, both_heads(inner, plain)], axis=1)
        centred = nt(left, right)
        dscores = (weights.astype(F32) * centred).astype(BF)
        dv_ref[window, lanes] += nn(weights, grads)
        dk_ref[window, lanes] += nn(dscores, queries)
        dq = tn(dscores, keys) * (DH ** -0.5)
        dq_ref[rows, lanes] = join_heads(dq).astype(BF)


def gelu_parts(value):
    cdf = 0.5 + 0.5 * lax.erf(value * (0.5 ** 0.5))
    density = jnp.exp(value * value * -0.5) * 0.3989422804014327
    return value * cdf, cdf + value * density


def feed_block(normed, up_ref, down_ref, hidden_ref, slope_ref, rows):
    total = None
    width = up_ref.shape[1]
    step = 512
    for at in range(0, width, step):
        hidden, slope = gelu_parts(nn(normed, up_ref[:, at : at + step]))
        hidden = hidden.astype(BF)
        hidden_ref[rows, at : at + step] = hidden
        slope_ref[rows, at : at + step] = slope.astype(BF)
        term = nn(hidden, down_ref[at : at + step, :])
        total = term if total is None else total + term
    return total


def feed_back_block(grad, up_ref, down_ref, slope_ref, rows):
    total = None
    width = up_ref.shape[1]
    step = 512
    for at in range(0, width, step):
        dhidden = nt(grad, down_ref[at : at + step, :])
        dup = (dhidden * slope_ref[rows, at : at + step].astype(F32)).astype(BF)
        slope_ref[rows, at : at + step] = dup
        term = nt(dup, up_ref[:, at : at + step])
        total = term if total is None else total + term
    return total


def loop(count, body):
    def step(index, carry):
        body(index)
        return carry

    lax.fori_loop(0, count, step, 0)


def put_grad(out_ref, index, value, prior_ref):
    if prior_ref is not None:
        value = value + prior_ref[index].astype(F32)
    out_ref[index] = value.astype(BF)


def weight_grad(out_ref, prior_ref, left_t_ref, right_ref, transposed):
    step = 512
    width = right_ref.shape[1]

    def slab(index):
        cols = block_at(index, step)
        value = nn(left_t_ref[...], right_ref[:, cols])
        if transposed:
            put_grad(out_ref, (cols, slice(None)), value.T, prior_ref)
        else:
            put_grad(out_ref, (slice(None), cols), value, prior_ref)

    loop(width // step, slab)


def encode_kernel(
    src, table, gains, mats, up, down, cols, rows_in, mem, qkv, weights, mixed, x1, x2, hidden, slope
):
    length = src.shape[0]

    def project(index):
        rows = block_at(index, TB)
        unit, _ = norm_parts(src[rows, :].astype(F32) + table[rows, :].astype(F32))
        normed = (unit * gains[0:1, :]).astype(BF)
        for which in range(3):
            qkv[which, rows, :] = nn(normed, mats[which]).astype(BF)

    loop(length // TB, project)

    def rest(index):
        for part in range(TB // QB):
            attend_block(
                index * (TB // QB) + part,
                qkv.at[0], qkv.at[1], qkv.at[2], cols, rows_in, weights, mixed, False,
            )
        rows = block_at(index, TB)
        stream = src[rows, :].astype(F32) + table[rows, :].astype(F32)
        stream = stream + nn(mixed[rows, :], mats[3])
        x1[rows, :] = stream
        unit, _ = norm_parts(stream)
        normed = (unit * gains[1:2, :]).astype(BF)
        stream = stream + feed_block(normed, up, down, hidden, slope, rows)
        x2[rows, :] = stream
        unit, _ = norm_parts(stream)
        mem[rows, :] = (unit * gains[2:3, :]).astype(BF)

    loop(length // TB, rest)


def encode_back_kernel(prior, *refs):
    (src, table, gains, mats, up, down, qkv, weights, mixed, x1, x2, hidden, slope_in, dmem) = refs[:14]
    refs = refs[14:]
    if prior:
        p_mats, p_up, p_down, p_table, p_gains = refs[:5]
        refs = refs[5:]
    else:
        p_mats = p_up = p_down = p_table = p_gains = None
    (g_in, g_mats, g_up, g_down, g_table, g_gains) = refs[:6]
    (slope, dy, dy_t, a_t, dx, dmixed, dq, dk, dv) = refs[6:]
    length = src.shape[0]
    slope[...] = slope_in[...]
    g_gains[...] = jnp.zeros_like(g_gains) if p_gains is None else p_gains[...]
    dk[...] = jnp.zeros_like(dk)
    dv[...] = jnp.zeros_like(dv)

    def feed_step(index):
        rows = block_at(index, TB)
        unit, scale = norm_parts(x2[rows, :])
        grad, d_gain = norm_back(dmem[rows, :].astype(F32), unit, scale, gains[2:3, :])
        g_gains[2:3, :] += d_gain
        low = grad.astype(BF)
        dy_t[:, rows] = low.T
        dnormed = feed_back_block(low, up, down, slope, rows)
        unit, scale = norm_parts(x1[rows, :])
        a_t[:, rows] = (unit * gains[1:2, :]).astype(BF).T
        back, d_gain = norm_back(dnormed, unit, scale, gains[1:2, :])
        g_gains[1:2, :] += d_gain
        grad = grad + back
        dx[rows, :] = grad
        low = grad.astype(BF)
        dy[rows, :] = low
        dmixed[rows, :] = nt(low, mats[3]).astype(BF)

    loop(length // TB, feed_step)
    weight_grad(g_up, p_up, a_t, slope, False)
    weight_grad(g_down, p_down, dy_t, hidden, True)
    put_grad(g_mats, 3, tn(mixed[...], dy[...]), p_mats)

    def attend_step(index):
        attend_back_block(
            index, qkv.at[0], qkv.at[1], qkv.at[2], weights, mixed, dmixed, dq, dk, dv
        )

    loop(length // QB, attend_step)

    def project_step(index):
        rows = block_at(index, TB)
        unit, scale = norm_parts(src[rows, :].astype(F32) + table[rows, :].astype(F32))
        a_t[:, rows] = (unit * gains[0:1, :]).astype(BF).T
        dnormed = nt(dq[rows, :], mats[0])
        dnormed += nt(dk[rows, :].astype(BF), mats[1])
        dnormed += nt(dv[rows, :].astype(BF), mats[2])
        back, d_gain = norm_back(dnormed, unit, scale, gains[0:1, :])
        g_gains[0:1, :] += d_gain
        grad = dx[rows, :] + back
        g_in[rows, :] = grad
        put_grad(g_table, (slice(None), rows), grad.T, p_table)

    loop(length // TB, project_step)
    put_grad(g_mats, 0, nn(a_t[...], dq[...]), p_mats)
    put_grad(g_mats, 1, nn(a_t[...], dk[...].astype(BF)), p_mats)
    put_grad(g_mats, 2, nn(a_t[...], dv[...].astype(BF)), p_mats)


def self_kernel(tgt, table, gains, mats, cols, rows_in, qkv, weights, mixed, h1):
    length = tgt.shape[0]

    def project(index):
        rows = block_at(index, TB)
        stream = table[rows, :].astype(F32)
        unit, _ = norm_parts(stream)
        qkv[0, rows, :] = nn((unit * gains[0:1, :]).astype(BF), mats[0]).astype(BF)
        unit, _ = norm_parts(tgt[rows, :].astype(F32) + stream)
        normed = (unit * gains[0:1, :]).astype(BF)
        for which in (1, 2):
            qkv[which, rows, :] = nn(normed, mats[which]).astype(BF)

    loop(length // TB, project)

    def rest(index):
        for part in range(TB // QB):
            attend_block(
                index * (TB // QB) + part,
                qkv.at[0], qkv.at[1], qkv.at[2], cols, rows_in, weights, mixed, True,
            )
        rows = block_at(index, TB)
        h1[rows, :] = table[rows, :].astype(F32) + nn(mixed[rows, :], mats[3])

    loop(length // TB, rest)


def self_back_kernel(prior, *refs):
    (tgt, table, gains, mats, qkv, weights, mixed, dh1) = refs[:8]
    refs = refs[8:]
    if prior:
        p_mats, p_table, p_gains = refs[:3]
        refs = refs[3:]
    else:
        p_mats = p_table = p_gains = None
    (g_in, g_mats, g_table, g_gains) = refs[:4]
    (dy, a_t, b_t, dmixed, dq, dk, dv) = refs[4:]
    length = tgt.shape[0]
    g_gains[...] = jnp.zeros_like(g_gains) if p_gains is None else p_gains[...]
    dk[...] = jnp.zeros_like(dk)
    dv[...] = jnp.zeros_like(dv)

    def out_step(index):
        rows = block_at(index, TB)
        low = dh1[rows, :].astype(BF)
        dy[rows, :] = low
        dmixed[rows, :] = nt(low, mats[3]).astype(BF)

    loop(length // TB, out_step)
    put_grad(g_mats, 3, tn(mixed[...], dy[...]), p_mats)

    def attend_step(index):
        attend_back_block(
            index, qkv.at[0], qkv.at[1], qkv.at[2], weights, mixed, dmixed, dq, dk, dv
        )

    loop(length // QB, attend_step)

    def project_step(index):
        rows = block_at(index, TB)
        stream = table[rows, :].astype(F32)
        unit, scale = norm_parts(stream)
        a_t[:, rows] = (unit * gains[0:1, :]).astype(BF).T
        back, d_gain = norm_back(nt(dq[rows, :], mats[0]), unit, scale, gains[0:1, :])
        dtable = dh1[rows, :] + back
        unit, scale = norm_parts(tgt[rows, :].astype(F32) + stream)
        b_t[:, rows] = (unit * gains[0:1, :]).astype(BF).T
        dnormed = nt(dk[rows, :].astype(BF), mats[1])
        dnormed += nt(dv[rows, :].astype(BF), mats[2])
        back, d_gain_too = norm_back(dnormed, unit, scale, gains[0:1, :])
        g_gains[0:1, :] += d_gain + d_gain_too
        g_in[rows, :] = back
        put_grad(g_table, (slice(None), rows), (dtable + back).T, p_table)

    loop(length // TB, project_step)
    put_grad(g_mats, 0, nn(a_t[...], dq[...]), p_mats)
    put_grad(g_mats, 1, nn(b_t[...], dk[...].astype(BF)), p_mats)
    put_grad(g_mats, 2, nn(b_t[...], dv[...].astype(BF)), p_mats)


def cross_kernel(prior, *refs):
    (h1, mem, cot, gains, mats, up, down, cols, rows_in) = refs[:9]
    refs = refs[9:]
    if prior:
        p_mats, p_up, p_down, p_gains = refs[:4]
        refs = refs[4:]
    else:
        p_mats = p_up = p_down = p_gains = None
    (out, dmem, dh1, g_mats, g_up, g_down, g_gains) = refs[:7]
    (qkv, weights, mixed, h2, hidden, slope, dy, dy_t, a_t, dmixed, dq, dk, dv) = refs[7:]
    length = h1.shape[0]
    g_gains[...] = jnp.zeros_like(g_gains) if p_gains is None else p_gains[...]
    dk[...] = jnp.zeros_like(dk)
    dv[...] = jnp.zeros_like(dv)

    def project(index):
        rows = block_at(index, TB)
        unit, _ = norm_parts(h1[rows, :])
        qkv[0, rows, :] = nn((unit * gains[1:2, :]).astype(BF), mats[0]).astype(BF)
        qkv[1, rows, :] = nn(mem[rows, :], mats[2]).astype(BF)
        qkv[2, rows, :] = nn(mem[rows, :], mats[3]).astype(BF)

    loop(length // TB, project)

    def middle(index):
        for part in range(TB // QB):
            attend_block(
                index * (TB // QB) + part,
                qkv.at[0], qkv.at[1], qkv.at[2], cols, rows_in, weights, mixed, False,
            )
        rows = block_at(index, TB)
        stream = h1[rows, :] + nn(mixed[rows, :], mats[1])
        h2[rows, :] = stream
        unit, scale = norm_parts(stream)
        normed = (unit * gains[2:3, :]).astype(BF)
        a_t[:, rows] = normed.T
        out[rows, :] = (stream + feed_block(normed, up, down, hidden, slope, rows)).astype(BF)
        low = cot[rows, :]
        dy_t[:, rows] = low.T
        dnormed = feed_back_block(low, up, down, slope, rows)
        back, d_gain = norm_back(dnormed, unit, scale, gains[2:3, :])
        g_gains[2:3, :] += d_gain
        grad = low.astype(F32) + back
        h2[rows, :] = grad
        low = grad.astype(BF)
        dy[rows, :] = low
        dmixed[rows, :] = nt(low, mats[1]).astype(BF)

    loop(length // TB, middle)

    def attend_step(index):
        attend_back_block(
            index, qkv.at[0], qkv.at[1], qkv.at[2], weights, mixed, dmixed, dq, dk, dv
        )

    loop(length // QB, attend_step)

    weight_grad(g_up, p_up, a_t, slope, False)
    weight_grad(g_down, p_down, dy_t, hidden, True)
    put_grad(g_mats, 1, tn(mixed[...], dy[...]), p_mats)

    def project_step(index):
        rows = block_at(index, TB)
        unit, scale = norm_parts(h1[rows, :])
        a_t[:, rows] = (unit * gains[1:2, :]).astype(BF).T
        back, d_gain = norm_back(nt(dq[rows, :], mats[0]), unit, scale, gains[1:2, :])
        g_gains[1:2, :] += d_gain
        dh1[rows, :] = h2[rows, :] + back
        dkeys = dk[rows, :].astype(BF)
        dvalues = dv[rows, :].astype(BF)
        dmem[rows, :] = (nt(dkeys, mats[2]) + nt(dvalues, mats[3])).astype(BF)

    loop(length // TB, project_step)
    put_grad(g_mats, 0, nn(a_t[...], dq[...]), p_mats)
    put_grad(g_mats, 2, tn(mem[...], dk[...].astype(BF)), p_mats)
    put_grad(g_mats, 3, tn(mem[...], dv[...].astype(BF)), p_mats)


def shape(dims, kind):
    return jax.ShapeDtypeStruct(dims, kind)


def call(kernel, name, outs, scratch, *args):
    return pl.pallas_call(
        kernel,
        out_shape=outs,
        in_specs=[pl.BlockSpec(memory_space=pltpu.VMEM)] * len(args),
        out_specs=[pl.BlockSpec(memory_space=pltpu.VMEM)] * len(outs),
        scratch_shapes=[pltpu.VMEM(s.shape, s.dtype) for s in scratch],
        compiler_params=pltpu.CompilerParams(vmem_limit_bytes=VMEM_BYTES),
        name=name,
    )(*args)


def sizes(length, width, ff):
    blocks = length // QB
    pairs = width // PAIR
    return dict(
        tok=shape((length, width), BF),
        tok32=shape((length, width), F32),
        qkv=shape((3, length, width), BF),
        weights=shape((blocks, pairs, WIN, 2 * QB), BF),
        hidden=shape((length, ff), BF),
        tokt=shape((width, length), BF),
        mats=shape((4, width, width), BF),
        up=shape((width, ff), BF),
        down=shape((ff, width), BF),
        gains=shape((8, width), F32),
    )


def encode(z, src, table, gains, mats, up, down, cols, rows):
    outs = [z["tok"], z["qkv"], z["weights"], z["tok"], z["tok32"], z["tok32"], z["hidden"], z["hidden"]]
    return call(encode_kernel, "encode", outs, [], src, table, gains, mats, up, down, cols, rows)


def encode_back(z, src, table, gains, mats, up, down, kept, dmem, prior):
    outs = [z["tok32"], z["mats"], z["up"], z["down"], z["tokt"], z["gains"]]
    scratch = [z["hidden"], z["tok"], z["tokt"], z["tokt"], z["tok32"], z["tok"], z["tok"], z["tok32"], z["tok32"]]
    return call(
        partial(encode_back_kernel, len(prior) > 0), "encode_back", outs, scratch,
        src, table, gains, mats, up, down, *kept, dmem, *prior,
    )


def self_forward(z, tgt, table, gains, mats, cols, rows):
    outs = [z["qkv"], z["weights"], z["tok"], z["tok32"]]
    return call(self_kernel, "self_forward", outs, [], tgt, table, gains, mats, cols, rows)


def self_back(z, tgt, table, gains, mats, kept, dh1, prior):
    outs = [z["tok32"], z["mats"], z["tokt"], z["gains"]]
    scratch = [z["tok"], z["tokt"], z["tokt"], z["tok"], z["tok"], z["tok32"], z["tok32"]]
    return call(
        partial(self_back_kernel, len(prior) > 0), "self_back", outs, scratch,
        tgt, table, gains, mats, *kept, dh1, *prior,
    )


def cross(z, h1, mem, cot, gains, mats, up, down, cols, rows, prior):
    outs = [z["tok"], z["tok"], z["tok32"], z["mats"], z["up"], z["down"], z["gains"]]
    scratch = [
        z["qkv"], z["weights"], z["tok"], z["tok32"], z["hidden"], z["hidden"], z["tok"], z["tokt"],
        z["tokt"], z["tok"], z["tok"], z["tok32"], z["tok32"],
    ]
    return call(
        partial(cross_kernel, len(prior) > 0), "cross", outs, scratch,
        h1, mem, cot, gains, mats, up, down, cols, rows, *prior,
    )


def unset(outs):
    return pl.pallas_call(
        lambda *refs: None,
        out_shape=outs,
        out_specs=[pl.BlockSpec(memory_space=pl.ANY)] * len(outs),
        name="unset",
    )()


def to_section(value, source):
    return lax.ppermute(value, "section", [(source, 1 - source)])


def gather(value, axis):
    return lax.all_gather(value, "dp", axis=axis, tiled=True)


def scatter(value, axis):
    return lax.psum_scatter(value, "dp", scatter_dimension=axis, tiled=True)


def mask_arrays(segments, levels):
    first = jnp.concatenate(
        [jnp.ones_like(segments[:, :1], bool), segments[:, 1:] != segments[:, :-1]], axis=1
    )
    usable = jnp.where((levels[0] > 0) | first, segments, -1)
    cols = jnp.stack([usable, segments, levels[1]] + [segments] * 5, axis=-1)
    rows = jnp.stack([segments, levels[1]], axis=1)
    return cols, rows.reshape(rows.shape[0], 2, -1, QB)


def body(
    inputs,
    positions,
    projections,
    out_projections,
    ffn_up,
    ffn_down,
    norm_gains,
    segments,
    levels,
    cotangent,
):
    encoder = lax.axis_index("section") == 0
    own = inputs[0, :, 0]
    cot = cotangent[:, 0]
    micro, length, width = own.shape
    z = sizes(length, width, ffn_up.shape[2])
    cols, rows = mask_arrays(segments[:, 0], levels[:, :, 0])

    proj, outp = projections[0].astype(BF), out_projections[0].astype(BF)
    lent = to_section(jnp.stack([proj[3], outp[1]]), 0)
    own_mats = jnp.stack([proj[0], proj[1], proj[2], outp[0]])
    cross_mats = jnp.concatenate([jnp.stack([proj[3], outp[1]]), lent])
    mats = gather(own_mats, 1)
    mats_b = gather(cross_mats, 1)
    up = gather(ffn_up[0].astype(BF), 0)
    down = gather(ffn_down[0].astype(BF), 0)
    table = gather(positions[0].astype(BF), 1)
    gains = gather(norm_gains[0].astype(BF), 1).astype(F32)
    gains = jnp.concatenate([gains, jnp.zeros((5, width), F32)])

    attn = [z["qkv"], z["weights"], z["tok"], z["tok32"]]
    extra = [z["tok32"], z["hidden"], z["hidden"]]

    def first_encoder(m):
        mem, *kept = encode(z, own[m], table, gains, mats, up, down, cols[m], rows[m])
        return (mem, *kept)

    def first_decoder(m):
        kept = self_forward(z, own[m], table, gains, mats, cols[m], rows[m])
        return (*unset([z["tok"]]), *kept, *unset(extra))

    kept, mems, sent = [], [], []
    for m in range(micro):
        mem, *rest = lax.cond(encoder, partial(first_encoder, m), partial(first_decoder, m))
        kept.append(rest)
        sent.append(mem)
        mems.append(to_section(mem, 0))

    crossed = [z["tok"], z["tok"], z["tok32"], z["mats"], z["up"], z["down"], z["gains"]]
    outs, dmems, dh1s, prior = [], [], [], ()
    for m in range(micro):

        def middle_decoder():
            return tuple(
                cross(z, kept[m][3], mems[m], cot[m], gains, mats_b, up, down, cols[m], rows[m], prior)
            )

        def middle_encoder():
            return tuple(unset(crossed))

        out, dmem, dh1, *prior = lax.cond(encoder, middle_encoder, middle_decoder)
        outs.append(out)
        dmems.append(to_section(dmem, 1))
        dh1s.append(dh1)
    g_cross, g_up, g_down, g_gains = prior

    g_ins, prior = [], ()
    for m in reversed(range(micro)):
        def last_encoder():
            g_in, *grads = encode_back(
                z, own[m], table, gains, mats, up, down, kept[m], dmems[m], prior
            )
            return (g_in, *grads)

        def last_decoder():
            less = (prior[0], prior[3], prior[4]) if prior else ()
            g_in, g_mats, g_table, g_gains = self_back(
                z, own[m], table, gains, mats, kept[m][:3], dh1s[m], less
            )
            return (g_in, g_mats, *unset([z["up"], z["down"]]), g_table, g_gains)

        g_in, *prior = lax.cond(encoder, last_encoder, last_decoder)
        g_ins.insert(0, g_in)
    s_mats, s_up, s_down, s_table, s_gains = prior
    s_up = jnp.where(encoder, s_up, g_up)
    s_down = jnp.where(encoder, s_down, g_down)
    s_gains = s_gains + jnp.where(encoder, 0.0, g_gains)

    r_mats = scatter(s_mats, 1)
    r_cross = scatter(g_cross, 1)
    r_up = scatter(s_up, 0)
    r_down = scatter(s_down, 0)
    r_table = scatter(s_table, 0).T
    r_gains = scatter(s_gains, 1)[:3]
    back = to_section(r_cross[2:], 1)
    own_cross = jnp.where(encoder, back, r_cross[:2])
    d_proj = jnp.concatenate([r_mats[:3], own_cross[:1]]).astype(F32)
    d_out = jnp.concatenate([r_mats[3:], own_cross[1:]]).astype(F32)

    main = [jnp.where(encoder, kept_mem, out) for kept_mem, out in zip(sent, outs)]
    return (
        jnp.stack(main)[None, :, None],
        jnp.stack(g_ins)[None, :, None],
        r_table.astype(F32)[None],
        d_proj[None],
        d_out[None],
        r_up.astype(F32)[None],
        r_down.astype(F32)[None],
        r_gains[None],
    )


def solution(mesh):
    in_specs = (
        P("section", None, "dp", None, None),
        P("section", None, "dp"),
        P("section", None, "dp", None),
        P("section", None, "dp", None),
        P("section", "dp", None),
        P("section", "dp", None),
        P("section", None, "dp"),
        P(None, "dp", None),
        P(None, None, "dp", None),
        P(None, "dp", None, None),
    )
    out_specs = (
        P("section", None, "dp", None, None),
        P("section", None, "dp", None, None),
        P("section", None, "dp"),
        P("section", None, "dp", None),
        P("section", None, "dp", None),
        P("section", "dp", None),
        P("section", "dp", None),
        P("section", None, "dp"),
    )
    return jax.shard_map(body, mesh=mesh, in_specs=in_specs, out_specs=out_specs, check_vma=False)
```

```python
from functools import partial

import jax
import jax.numpy as jnp
from jax import lax
from jax.experimental import pallas as pl
from jax.experimental.pallas import tpu as pltpu
from jax.sharding import PartitionSpec as P

BF = jnp.bfloat16
F32 = jnp.float32
DH = 64
PAIR = 2 * DH
QB = 128
WIN = 256
TB = 256
VMEM_BYTES = 60 * 1024 * 1024


def nn(left, right):
    return jnp.dot(left, right, preferred_element_type=F32)


def nt(left, right):
    return lax.dot_general(left, right, (((1,), (1,)), ((), ())), preferred_element_type=F32)


def tn(left, right):
    return lax.dot_general(left, right, (((0,), (0,)), ((), ())), preferred_element_type=F32)


def norm_parts(stream):
    centred = stream - jnp.mean(stream, axis=-1, keepdims=True)
    scale = lax.rsqrt(jnp.mean(centred * centred, axis=-1, keepdims=True) + 1e-05)
    return centred * scale, scale


def norm_back(grad, unit, scale, gain):
    inner = grad * gain
    first = jnp.mean(inner, axis=-1, keepdims=True)
    second = jnp.mean(inner * unit, axis=-1, keepdims=True)
    return scale * (inner - first - unit * second), jnp.sum(grad * unit, axis=0, keepdims=True)


def block_at(index, size):
    return pl.ds(pl.multiple_of(index * size, size), size)


def lane_halves(scale=1.0):
    lane = lax.broadcasted_iota(jnp.int32, (1, PAIR), 1)
    low = jnp.where(lane < DH, scale, 0.0).astype(BF)
    high = jnp.where(lane < DH, 0.0, scale).astype(BF)
    return low, high


def both_heads(block, halves):
    return jnp.concatenate([block * halves[0], block * halves[1]], axis=0)


def join_heads(stacked):
    lane = lax.broadcasted_iota(jnp.int32, (QB, PAIR), 1)
    return jnp.where(lane < DH, stacked[:QB], stacked[QB:])


def window_start(index, length):
    return pl.multiple_of(jnp.clip(index * QB - DH, 0, length - WIN), DH)


def mask_bias(index, start, cols_ref, rows_ref, causal):
    keys = cols_ref[pl.ds(start, WIN), :]
    query_segment = rows_ref[0, pl.ds(index, 1), :]
    if causal:
        query_level = rows_ref[1, pl.ds(index, 1), :]
        key_id = start + lax.broadcasted_iota(jnp.int32, (WIN, QB), 0)
        query_id = index * QB + lax.broadcasted_iota(jnp.int32, (WIN, QB), 1)
        allowed = (keys[:, 1:2] == query_segment) & (
            (keys[:, 2:3] < query_level) | (key_id == query_id)
        )
    else:
        allowed = keys[:, 0:1] == query_segment
    bias = jnp.where(allowed, 0.0, -1e30)
    return jnp.concatenate([bias, bias], axis=1)


def attend_block(index, q_ref, k_ref, v_ref, cols_ref, rows_ref, weights_ref, mixed_ref, causal):
    length, width = q_ref.shape
    start = window_start(index, length)
    rows = block_at(index, QB)
    bias = mask_bias(index, start, cols_ref, rows_ref, causal)
    halves = lane_halves(DH ** -0.5)
    for pair in range(width // PAIR):
        lanes = slice(pair * PAIR, (pair + 1) * PAIR)
        queries = both_heads(q_ref[rows, lanes], halves)
        scores = nt(k_ref[pl.ds(start, WIN), lanes], queries) + bias
        shifted = jnp.exp(scores - jnp.max(scores, axis=0, keepdims=True))
        weights = (shifted * (1.0 / jnp.sum(shifted, axis=0, keepdims=True))).astype(BF)
        weights_ref[index, pair] = weights
        out = tn(weights, v_ref[pl.ds(start, WIN), lanes])
        mixed_ref[rows, lanes] = join_heads(out).astype(BF)


def attend_back_block(
    index, q_ref, k_ref, v_ref, weights_ref, mixed_ref, dmixed_ref, dq_ref, dk_ref, dv_ref
):
    length, width = q_ref.shape
    start = window_start(index, length)
    rows = block_at(index, QB)
    window = pl.ds(start, WIN)
    plain = lane_halves()
    halves = lane_halves(DH ** -0.5)
    ones = jnp.ones((WIN, PAIR), BF)
    for pair in range(width // PAIR):
        lanes = slice(pair * PAIR, (pair + 1) * PAIR)
        queries = both_heads(q_ref[rows, lanes], halves)
        keys = k_ref[window, lanes]
        values = v_ref[window, lanes]
        weights = weights_ref[index, pair]
        dmixed = dmixed_ref[rows, lanes]
        grads = both_heads(dmixed, plain)
        inner = (dmixed.astype(F32) * mixed_ref[rows, lanes].astype(F32) * -1.0).astype(BF)
        left = jnp.concatenate([values, ones], axis=1)
        right = jnp.concatenate([grads, both_heads(inner, plain)], axis=1)
        centred = nt(left, right)
        dscores = (weights.astype(F32) * centred).astype(BF)
        dv_ref[window, lanes] += nn(weights, grads)
        dk_ref[window, lanes] += nn(dscores, queries)
        dq = tn(dscores, keys) * (DH ** -0.5)
        dq_ref[rows, lanes] = join_heads(dq).astype(BF)


def gelu_parts(value):
    cdf = 0.5 + 0.5 * lax.erf(value * (0.5 ** 0.5))
    density = jnp.exp(value * value * -0.5) * 0.3989422804014327
    return value * cdf, cdf + value * density


def feed_block(normed, up_ref, down_ref, hidden_ref, slope_ref, rows):
    total = None
    width = up_ref.shape[1]
    step = 512
    for at in range(0, width, step):
        hidden, slope = gelu_parts(nn(normed, up_ref[:, at : at + step]))
        hidden = hidden.astype(BF)
        hidden_ref[rows, at : at + step] = hidden
        slope_ref[rows, at : at + step] = slope.astype(BF)
        term = nn(hidden, down_ref[at : at + step, :])
        total = term if total is None else total + term
    return total


def feed_back_block(grad, up_ref, down_ref, slope_ref, rows):
    total = None
    width = up_ref.shape[1]
    step = 512
    for at in range(0, width, step):
        dhidden = nt(grad, down_ref[at : at + step, :])
        dup = (dhidden * slope_ref[rows, at : at + step].astype(F32)).astype(BF)
        slope_ref[rows, at : at + step] = dup
        term = nt(dup, up_ref[:, at : at + step])
        total = term if total is None else total + term
    return total


def loop(count, body):
    def step(index, carry):
        body(index)
        return carry

    lax.fori_loop(0, count, step, 0)


def put_grad(out_ref, index, value, prior_ref):
    if prior_ref is not None:
        value = value + prior_ref[index].astype(F32)
    out_ref[index] = value.astype(BF)


def weight_grad(out_ref, prior_ref, left_t_ref, right_ref, transposed):
    step = 512
    width = right_ref.shape[1]

    def slab(index):
        cols = block_at(index, step)
        value = nn(left_t_ref[...], right_ref[:, cols])
        if transposed:
            put_grad(out_ref, (cols, slice(None)), value.T, prior_ref)
        else:
            put_grad(out_ref, (slice(None), cols), value, prior_ref)

    loop(width // step, slab)


def encode_kernel(
    src, table, gains, mats, up, down, cols, rows_in, mem, qkv, weights, mixed, x1, x2, hidden, slope
):
    length = src.shape[0]

    def project(index):
        rows = block_at(index, TB)
        unit, _ = norm_parts(src[rows, :].astype(F32) + table[rows, :].astype(F32))
        normed = (unit * gains[0:1, :]).astype(BF)
        for which in range(3):
            qkv[which, rows, :] = nn(normed, mats[which]).astype(BF)

    loop(length // TB, project)

    def rest(index):
        for part in range(TB // QB):
            attend_block(
                index * (TB // QB) + part,
                qkv.at[0], qkv.at[1], qkv.at[2], cols, rows_in, weights, mixed, False,
            )
        rows = block_at(index, TB)
        stream = src[rows, :].astype(F32) + table[rows, :].astype(F32)
        stream = stream + nn(mixed[rows, :], mats[3])
        x1[rows, :] = stream
        unit, _ = norm_parts(stream)
        normed = (unit * gains[1:2, :]).astype(BF)
        stream = stream + feed_block(normed, up, down, hidden, slope, rows)
        x2[rows, :] = stream
        unit, _ = norm_parts(stream)
        mem[rows, :] = (unit * gains[2:3, :]).astype(BF)

    loop(length // TB, rest)


def encode_back_kernel(prior, *refs):
    (src, table, gains, mats, up, down, qkv, weights, mixed, x1, x2, hidden, slope_in, dmem) = refs[:14]
    refs = refs[14:]
    if prior:
        p_mats, p_up, p_down, p_table, p_gains = refs[:5]
        refs = refs[5:]
    else:
        p_mats = p_up = p_down = p_table = p_gains = None
    (g_in, g_mats, g_up, g_down, g_table, g_gains) = refs[:6]
    (slope, dy, dy_t, a_t, dx, dmixed, dq, dk, dv) = refs[6:]
    length = src.shape[0]
    slope[...] = slope_in[...]
    g_gains[...] = jnp.zeros_like(g_gains) if p_gains is None else p_gains[...]
    dk[...] = jnp.zeros_like(dk)
    dv[...] = jnp.zeros_like(dv)

    def feed_step(index):
        rows = block_at(index, TB)
        unit, scale = norm_parts(x2[rows, :])
        grad, d_gain = norm_back(dmem[rows, :].astype(F32), unit, scale, gains[2:3, :])
        g_gains[2:3, :] += d_gain
        low = grad.astype(BF)
        dy_t[:, rows] = low.T
        dnormed = feed_back_block(low, up, down, slope, rows)
        unit, scale = norm_parts(x1[rows, :])
        a_t[:, rows] = (unit * gains[1:2, :]).astype(BF).T
        back, d_gain = norm_back(dnormed, unit, scale, gains[1:2, :])
        g_gains[1:2, :] += d_gain
        grad = grad + back
        dx[rows, :] = grad
        low = grad.astype(BF)
        dy[rows, :] = low
        dmixed[rows, :] = nt(low, mats[3]).astype(BF)

    loop(length // TB, feed_step)
    weight_grad(g_up, p_up, a_t, slope, False)
    weight_grad(g_down, p_down, dy_t, hidden, True)
    put_grad(g_mats, 3, tn(mixed[...], dy[...]), p_mats)

    def attend_step(index):
        attend_back_block(
            index, qkv.at[0], qkv.at[1], qkv.at[2], weights, mixed, dmixed, dq, dk, dv
        )

    loop(length // QB, attend_step)

    def project_step(index):
        rows = block_at(index, TB)
        unit, scale = norm_parts(src[rows, :].astype(F32) + table[rows, :].astype(F32))
        a_t[:, rows] = (unit * gains[0:1, :]).astype(BF).T
        dnormed = nt(dq[rows, :], mats[0])
        dnormed += nt(dk[rows, :].astype(BF), mats[1])
        dnormed += nt(dv[rows, :].astype(BF), mats[2])
        back, d_gain = norm_back(dnormed, unit, scale, gains[0:1, :])
        g_gains[0:1, :] += d_gain
        grad = dx[rows, :] + back
        g_in[rows, :] = grad
        put_grad(g_table, (slice(None), rows), grad.T, p_table)

    loop(length // TB, project_step)
    put_grad(g_mats, 0, nn(a_t[...], dq[...]), p_mats)
    put_grad(g_mats, 1, nn(a_t[...], dk[...].astype(BF)), p_mats)
    put_grad(g_mats, 2, nn(a_t[...], dv[...].astype(BF)), p_mats)


def self_kernel(tgt, table, gains, mats, cols, rows_in, qkv, weights, mixed, h1):
    length = tgt.shape[0]

    def project(index):
        rows = block_at(index, TB)
        stream = table[rows, :].astype(F32)
        unit, _ = norm_parts(stream)
        qkv[0, rows, :] = nn((unit * gains[0:1, :]).astype(BF), mats[0]).astype(BF)
        unit, _ = norm_parts(tgt[rows, :].astype(F32) + stream)
        normed = (unit * gains[0:1, :]).astype(BF)
        for which in (1, 2):
            qkv[which, rows, :] = nn(normed, mats[which]).astype(BF)

    loop(length // TB, project)

    def rest(index):
        for part in range(TB // QB):
            attend_block(
                index * (TB // QB) + part,
                qkv.at[0], qkv.at[1], qkv.at[2], cols, rows_in, weights, mixed, True,
            )
        rows = block_at(index, TB)
        h1[rows, :] = table[rows, :].astype(F32) + nn(mixed[rows, :], mats[3])

    loop(length // TB, rest)


def self_back_kernel(prior, *refs):
    (tgt, table, gains, mats, qkv, weights, mixed, dh1) = refs[:8]
    refs = refs[8:]
    if prior:
        p_mats, p_table, p_gains = refs[:3]
        refs = refs[3:]
    else:
        p_mats = p_table = p_gains = None
    (g_in, g_mats, g_table, g_gains) = refs[:4]
    (dy, a_t, b_t, dmixed, dq, dk, dv) = refs[4:]
    length = tgt.shape[0]
    g_gains[...] = jnp.zeros_like(g_gains) if p_gains is None else p_gains[...]
    dk[...] = jnp.zeros_like(dk)
    dv[...] = jnp.zeros_like(dv)

    def out_step(index):
        rows = block_at(index, TB)
        low = dh1[rows, :].astype(BF)
        dy[rows, :] = low
        dmixed[rows, :] = nt(low, mats[3]).astype(BF)

    loop(length // TB, out_step)
    put_grad(g_mats, 3, tn(mixed[...], dy[...]), p_mats)

    def attend_step(index):
        attend_back_block(
            index, qkv.at[0], qkv.at[1], qkv.at[2], weights, mixed, dmixed, dq, dk, dv
        )

    loop(length // QB, attend_step)

    def project_step(index):
        rows = block_at(index, TB)
        stream = table[rows, :].astype(F32)
        unit, scale = norm_parts(stream)
        a_t[:, rows] = (unit * gains[0:1, :]).astype(BF).T
        back, d_gain = norm_back(nt(dq[rows, :], mats[0]), unit, scale, gains[0:1, :])
        dtable = dh1[rows, :] + back
        unit, scale = norm_parts(tgt[rows, :].astype(F32) + stream)
        b_t[:, rows] = (unit * gains[0:1, :]).astype(BF).T
        dnormed = nt(dk[rows, :].astype(BF), mats[1])
        dnormed += nt(dv[rows, :].astype(BF), mats[2])
        back, d_gain_too = norm_back(dnormed, unit, scale, gains[0:1, :])
        g_gains[0:1, :] += d_gain + d_gain_too
        g_in[rows, :] = back
        put_grad(g_table, (slice(None), rows), (dtable + back).T, p_table)

    loop(length // TB, project_step)
    put_grad(g_mats, 0, nn(a_t[...], dq[...]), p_mats)
    put_grad(g_mats, 1, nn(b_t[...], dk[...].astype(BF)), p_mats)
    put_grad(g_mats, 2, nn(b_t[...], dv[...].astype(BF)), p_mats)


def cross_kernel(prior, *refs):
    (h1, mem, cot, gains, mats, up, down, cols, rows_in) = refs[:9]
    refs = refs[9:]
    if prior:
        p_mats, p_up, p_down, p_gains = refs[:4]
        refs = refs[4:]
    else:
        p_mats = p_up = p_down = p_gains = None
    (out, dmem, dh1, g_mats, g_up, g_down, g_gains) = refs[:7]
    (qkv, weights, mixed, h2, hidden, slope, dy, dy_t, a_t, dmixed, dq, dk, dv) = refs[7:]
    length = h1.shape[0]
    g_gains[...] = jnp.zeros_like(g_gains) if p_gains is None else p_gains[...]
    dk[...] = jnp.zeros_like(dk)
    dv[...] = jnp.zeros_like(dv)

    def project(index):
        rows = block_at(index, TB)
        unit, _ = norm_parts(h1[rows, :])
        qkv[0, rows, :] = nn((unit * gains[1:2, :]).astype(BF), mats[0]).astype(BF)
        qkv[1, rows, :] = nn(mem[rows, :], mats[2]).astype(BF)
        qkv[2, rows, :] = nn(mem[rows, :], mats[3]).astype(BF)

    loop(length // TB, project)

    def middle(index):
        for part in range(TB // QB):
            attend_block(
                index * (TB // QB) + part,
                qkv.at[0], qkv.at[1], qkv.at[2], cols, rows_in, weights, mixed, False,
            )
        rows = block_at(index, TB)
        stream = h1[rows, :] + nn(mixed[rows, :], mats[1])
        h2[rows, :] = stream
        unit, scale = norm_parts(stream)
        normed = (unit * gains[2:3, :]).astype(BF)
        a_t[:, rows] = normed.T
        out[rows, :] = (stream + feed_block(normed, up, down, hidden, slope, rows)).astype(BF)
        low = cot[rows, :]
        dy_t[:, rows] = low.T
        dnormed = feed_back_block(low, up, down, slope, rows)
        back, d_gain = norm_back(dnormed, unit, scale, gains[2:3, :])
        g_gains[2:3, :] += d_gain
        grad = low.astype(F32) + back
        h2[rows, :] = grad
        low = grad.astype(BF)
        dy[rows, :] = low
        dmixed[rows, :] = nt(low, mats[1]).astype(BF)

    loop(length // TB, middle)

    def attend_step(index):
        attend_back_block(
            index, qkv.at[0], qkv.at[1], qkv.at[2], weights, mixed, dmixed, dq, dk, dv
        )

    loop(length // QB, attend_step)

    weight_grad(g_up, p_up, a_t, slope, False)
    weight_grad(g_down, p_down, dy_t, hidden, True)
    put_grad(g_mats, 1, tn(mixed[...], dy[...]), p_mats)

    def project_step(index):
        rows = block_at(index, TB)
        unit, scale = norm_parts(h1[rows, :])
        a_t[:, rows] = (unit * gains[1:2, :]).astype(BF).T
        back, d_gain = norm_back(nt(dq[rows, :], mats[0]), unit, scale, gains[1:2, :])
        g_gains[1:2, :] += d_gain
        dh1[rows, :] = h2[rows, :] + back
        dkeys = dk[rows, :].astype(BF)
        dvalues = dv[rows, :].astype(BF)
        dmem[rows, :] = (nt(dkeys, mats[2]) + nt(dvalues, mats[3])).astype(BF)

    loop(length // TB, project_step)
    put_grad(g_mats, 0, nn(a_t[...], dq[...]), p_mats)
    put_grad(g_mats, 2, tn(mem[...], dk[...].astype(BF)), p_mats)
    put_grad(g_mats, 3, tn(mem[...], dv[...].astype(BF)), p_mats)


def shape(dims, kind):
    return jax.ShapeDtypeStruct(dims, kind)


def call(kernel, name, outs, scratch, *args):
    return pl.pallas_call(
        kernel,
        out_shape=outs,
        in_specs=[pl.BlockSpec(memory_space=pltpu.VMEM)] * len(args),
        out_specs=[pl.BlockSpec(memory_space=pltpu.VMEM)] * len(outs),
        scratch_shapes=[pltpu.VMEM(s.shape, s.dtype) for s in scratch],
        compiler_params=pltpu.CompilerParams(vmem_limit_bytes=VMEM_BYTES),
        name=name,
    )(*args)


def sizes(length, width, ff):
    blocks = length // QB
    pairs = width // PAIR
    return dict(
        tok=shape((length, width), BF),
        tok32=shape((length, width), F32),
        qkv=shape((3, length, width), BF),
        weights=shape((blocks, pairs, WIN, 2 * QB), BF),
        hidden=shape((length, ff), BF),
        tokt=shape((width, length), BF),
        mats=shape((4, width, width), BF),
        up=shape((width, ff), BF),
        down=shape((ff, width), BF),
        gains=shape((8, width), F32),
    )


def encode(z, src, table, gains, mats, up, down, cols, rows):
    outs = [z["tok"], z["qkv"], z["weights"], z["tok"], z["tok32"], z["tok32"], z["hidden"], z["hidden"]]
    return call(encode_kernel, "encode", outs, [], src, table, gains, mats, up, down, cols, rows)


def encode_back(z, src, table, gains, mats, up, down, kept, dmem, prior):
    outs = [z["tok32"], z["mats"], z["up"], z["down"], z["tokt"], z["gains"]]
    scratch = [z["hidden"], z["tok"], z["tokt"], z["tokt"], z["tok32"], z["tok"], z["tok"], z["tok32"], z["tok32"]]
    return call(
        partial(encode_back_kernel, len(prior) > 0), "encode_back", outs, scratch,
        src, table, gains, mats, up, down, *kept, dmem, *prior,
    )


def self_forward(z, tgt, table, gains, mats, cols, rows):
    outs = [z["qkv"], z["weights"], z["tok"], z["tok32"]]
    return call(self_kernel, "self_forward", outs, [], tgt, table, gains, mats, cols, rows)


def self_back(z, tgt, table, gains, mats, kept, dh1, prior):
    outs = [z["tok32"], z["mats"], z["tokt"], z["gains"]]
    scratch = [z["tok"], z["tokt"], z["tokt"], z["tok"], z["tok"], z["tok32"], z["tok32"]]
    return call(
        partial(self_back_kernel, len(prior) > 0), "self_back", outs, scratch,
        tgt, table, gains, mats, *kept, dh1, *prior,
    )


def cross(z, h1, mem, cot, gains, mats, up, down, cols, rows, prior):
    outs = [z["tok"], z["tok"], z["tok32"], z["mats"], z["up"], z["down"], z["gains"]]
    scratch = [
        z["qkv"], z["weights"], z["tok"], z["tok32"], z["hidden"], z["hidden"], z["tok"], z["tokt"],
        z["tokt"], z["tok"], z["tok"], z["tok32"], z["tok32"],
    ]
    return call(
        partial(cross_kernel, len(prior) > 0), "cross", outs, scratch,
        h1, mem, cot, gains, mats, up, down, cols, rows, *prior,
    )


LINE = 4
TABLE_ROWS = 48
MESH = pl.DeviceIdType.MESH


def place():
    me = lax.axis_index("dp")
    return me // 4, (me // 2) % 2, me % 2


def rank_of(z, x, core):
    return z * 4 + x * 2 + core


def at_rank(ref, axis, per, rank):
    rows = pl.ds(pl.multiple_of(rank * per, per), per)
    return ref.at[rows, :] if axis == 0 else ref.at[:, rows, :]


def greet(z, x, core):
    barrier = pltpu.get_barrier_semaphore()

    def signal(rank):
        pl.semaphore_signal(barrier, inc=1, device_id={"dp": rank}, device_id_type=MESH)

    signal(rank_of(z, 1 - x, core))
    signal(rank_of(z, x, 1 - core))

    for step in range(1, LINE):
        signal(rank_of((z + step) % LINE, x, core))
    pl.semaphore_wait(barrier, LINE + 1)


def remote(src, dst, send, recv, rank):
    return pltpu.make_async_remote_copy(
        src_ref=src, dst_ref=dst, send_sem=send, recv_sem=recv, device_id={"dp": rank},
        device_id_type=MESH,
    )


def gather_kernel(
    proj, outp, up, down, pos, gain, o_mats, o_up, o_down, o_table, s_mats, s_up, s_down, s_table,
    zsend, zrecv, xsend, xrecv, csend, crecv, here,
):
    z, x, core = place()
    for to, (ref, index) in enumerate(
        ((proj, 0), (proj, 1), (proj, 2), (outp, 0), (proj, 3), (outp, 1))
    ):
        s_mats[to] = ref[index].astype(BF)
    s_up[...] = up[...].astype(BF)
    s_down[...] = down[...].astype(BF)
    per = pos.shape[1]
    s_table[...] = jnp.zeros_like(s_table)
    s_table[:per, :] = pos[...].T.astype(BF)
    s_table[per : per + gain.shape[0], :per] = gain[...].astype(BF)
    greet(z, x, core)

    outs = ((o_mats, 1), (o_up, 0), (o_down, 0), (o_table, 0))
    mine = (s_mats, s_up, s_down, s_table)
    pers = (s_mats.shape[1], s_up.shape[0], s_down.shape[0], s_table.shape[0])
    kinds = range(len(outs))

    def view(kind, rank):
        return at_rank(outs[kind][0], outs[kind][1], pers[kind], rank)

    across = rank_of(z, 1 - x, core)
    sibling = rank_of(z, x, 1 - core)
    own = rank_of(z, x, core)

    def along(kind, way, step, src, rank):
        return remote(
            src, view(kind, rank), zsend.at[kind, way, step], zrecv.at[kind, way, step],
            rank_of(z + (1 - 2 * way), x, core),
        )

    def over(kind, slot, src, rank):
        return remote(src, view(kind, rank), xsend.at[kind, slot], xrecv.at[kind, slot], across)

    def beside(kind, slot, src, rank):
        return remote(src, view(kind, rank), csend.at[kind, slot], crecv.at[kind, slot], sibling)

    def can_send(way):
        return (z > 0) if way else (z < LINE - 1)

    slots = [(0, 0, 0)] + [(1 + way * 3 + step, way, step + 1) for step in range(3) for way in range(2)]

    def begins(way, back):
        return z - back * (1 - 2 * way)

    def exists(way, back):
        if back == 0:
            return None
        return (z <= LINE - 1 - back) if way else (z >= back)

    def when(cond, do):
        if cond is None:
            do()
        else:
            pl.when(cond)(do)

    local = [pltpu.make_async_copy(mine[k], view(k, own), here.at[k]) for k in kinds]
    for kind in kinds:
        for way in range(2):

            @pl.when(can_send(way))
            def _():
                along(kind, way, 0, mine[kind], own).start()

        over(kind, 0, mine[kind], own).start()
    for kind in kinds:
        beside(kind, 0, mine[kind], own).start()
        local[kind].start()

    for slot, way, back in slots[1:]:

        def pass_on():
            rank = rank_of(begins(way, back), x, core)
            for kind in kinds:
                block = view(kind, rank)
                along(kind, way, back - 1, block, rank).wait_recv()
                if back < LINE - 1:

                    @pl.when(can_send(way))
                    def _():
                        along(kind, way, back, block, rank).start()

                over(kind, slot, block, rank).start()
                beside(kind, slot, block, rank).start()

        when(exists(way, back), pass_on)

    for slot, way, back in slots:

        def share():
            rank = rank_of(begins(way, back), 1 - x, core)
            for kind in kinds:
                block = view(kind, rank)
                over(kind, slot, block, rank).wait_recv()
                beside(kind, 7 + slot, block, rank).start()

        when(exists(way, back), share)

    for kind in kinds:
        local[kind].wait()
        for way in range(2):
            for step in range(3):
                sent = can_send(way)
                if step > 0:
                    sent = sent & exists(way, step)

                @pl.when(sent)
                def _():
                    along(kind, way, step, mine[kind], own).wait_send()

    for slot, way, back in slots:

        def finish():
            for kind in kinds:
                over(kind, slot, mine[kind], own).wait_send()
                for part in range(2):
                    copy = beside(kind, slot + 7 * part, mine[kind], own)
                    copy.wait_send()
                    copy.wait_recv()

        when(exists(way, back), finish)


def gather_weights(proj, outp, up, down, pos, gain):
    ranks = lax.axis_size("dp")
    count, per, width = proj.shape[0] + outp.shape[0], proj.shape[1], proj.shape[2]
    length = pos.shape[0]
    if ranks != 4 * LINE or per != pos.shape[1] or per + gain.shape[0] > TABLE_ROWS:
        order = [proj[0], proj[1], proj[2], outp[0], proj[3], outp[1]]
        every = lambda value, axis: lax.all_gather(value.astype(BF), "dp", axis=axis, tiled=True)
        return (
            every(jnp.stack(order), 1), every(up, 0), every(down, 0),
            every(pos, 1), every(gain, 1),
        )
    shards = [
        shape((count, per, width), BF), shape(up.shape, BF), shape(down.shape, BF),
        shape((TABLE_ROWS, length), BF),
    ]
    outs = [
        shape((count, per * ranks, width), BF), shape((up.shape[0] * ranks, up.shape[1]), BF),
        shape((down.shape[0] * ranks, width), BF), shape((TABLE_ROWS * ranks, length), BF),
    ]
    dma = pltpu.SemaphoreType.DMA
    mats, up, down, packed = pl.pallas_call(
        gather_kernel,
        out_shape=outs,
        in_specs=[pl.BlockSpec(memory_space=pltpu.VMEM)] * 6,
        out_specs=[pl.BlockSpec(memory_space=pl.ANY)] * 4,
        scratch_shapes=[pltpu.VMEM(s.shape, s.dtype) for s in shards]
        + [dma((4, 2, 3)), dma((4, 2, 3)), dma((4, 7)), dma((4, 7)), dma((4, 14)), dma((4, 14)), dma((4,))],
        compiler_params=pltpu.CompilerParams(
            collective_id=0, has_side_effects=True, vmem_limit_bytes=VMEM_BYTES
        ),
        name="gather",
    )(proj, outp, up, down, pos, gain)
    packed = packed.reshape(ranks, TABLE_ROWS, length)
    table = packed[:, :per].reshape(ranks * per, length).T
    gains = packed[:, per : per + gain.shape[0], :per].transpose(1, 0, 2).reshape(-1, width)
    return mats, up, down, table, gains


def scatter_kernel(
    g_mats, g_up, g_down, g_table, g_gain, o_mats, o_up, o_down, o_table, o_gain,
    c_mats, c_up, c_down, c_table, x_mats, x_up, x_down, x_table, z_mats, z_up, z_down, z_table,
    gain_buf, csend, crecv, xsend, xrecv, zsend, zrecv, gsend, grecv,
):
    z, x, core = place()
    greet(z, x, core)
    across = rank_of(z, 1 - x, core)
    sibling = rank_of(z, x, 1 - core)
    own = rank_of(z, x, core)
    grads = ((g_mats, 1), (g_up, 0), (g_down, 0), (g_table, 0))
    outs = (o_mats, o_up, o_down, o_table)
    cbuf = (c_mats, c_up, c_down, c_table)
    xbuf = (x_mats, x_up, x_down, x_table)
    zbuf = (z_mats, z_up, z_down, z_table)
    kinds = range(4)
    order = (3, 0, 2, 1)

    def grad(kind, rank):
        ref, axis = grads[kind]
        return at_rank(ref, axis, outs[kind].shape[axis], rank)

    def beside(kind, dest, part):
        target_x = x if part else 1 - x
        return remote(
            grad(kind, rank_of(dest, target_x, 1 - core)), cbuf[kind].at[dest, part],
            csend.at[kind, dest, part], crecv.at[kind, dest, part], sibling,
        )

    def over(kind, dest):
        return remote(
            cbuf[kind].at[dest, 0], xbuf[kind].at[dest], xsend.at[kind, dest], xrecv.at[kind, dest], across
        )

    def along(kind, dest, way):
        return remote(
            cbuf[kind].at[dest, 1], zbuf[kind].at[dest, way], zsend.at[kind, dest, way],
            zrecv.at[kind, dest, way], rank_of(z + (1 - 2 * way), x, core),
        )

    def add(into, *others):
        total = into[...].astype(F32)
        for other in others:
            total = total + other[...].astype(F32)
        into[...] = total.astype(BF)

    for kind in kinds:
        for dest in order:
            for part in range(2):
                beside(kind, dest, part).start()
    for kind in kinds:
        for dest in order:
            beside(kind, dest, 0).wait_recv()
            add(cbuf[kind].at[dest, 0], grad(kind, rank_of(dest, 1 - x, core)))
            over(kind, dest).start()

    for kind in kinds:
        for dest in order:
            beside(kind, dest, 1).wait_recv()
            over(kind, dest).wait_recv()
            add(cbuf[kind].at[dest, 1], grad(kind, rank_of(dest, x, core)), xbuf[kind].at[dest])
            for way in range(2):
                before = (z > dest) if way else (z < dest)
                far = (z == LINE - 1) if way else (z == 0)

                @pl.when(before)
                def _():
                    @pl.when(jnp.logical_not(far))
                    def _():
                        along(kind, dest, way).wait_recv()
                        add(cbuf[kind].at[dest, 1], zbuf[kind].at[dest, way])

                    along(kind, dest, way).start()

    for kind in kinds:
        for dest in range(LINE):

            @pl.when(z == dest)
            def _():
                total = cbuf[kind][dest, 1].astype(F32)
                if dest > 0:
                    along(kind, dest, 0).wait_recv()
                    total = total + zbuf[kind][dest, 0].astype(F32)
                if dest < LINE - 1:
                    along(kind, dest, 1).wait_recv()
                    total = total + zbuf[kind][dest, 1].astype(F32)
                outs[kind][...] = total

    for kind in kinds:
        for dest in order:
            over(kind, dest).wait_send()
            for part in range(2):
                beside(kind, dest, part).wait_send()
            for way in range(2):

                @pl.when((z > dest) if way else (z < dest))
                def _():
                    along(kind, dest, way).wait_send()

    gain_buf[0] = g_gain[...]

    def swap(index, rank):
        return remote(gain_buf.at[0], gain_buf.at[index], gsend.at[index], grecv.at[index], rank)

    for index, rank in ((1, sibling), (2, across)):
        copy = swap(index, rank)
        copy.start()
        copy.wait_send()
        copy.wait_recv()
        gain_buf[0] = gain_buf[0] + gain_buf[index]
    for way in range(2):
        for step in range(1, LINE):
            ahead = z + step * (1 - 2 * way)
            there = (z >= step) if way else (z <= LINE - 1 - step)

            @pl.when(there)
            def _():
                swap(2 + way * 3 + step, rank_of(ahead, x, core)).start()

    for way in range(2):
        for step in range(1, LINE):
            behind = (z <= LINE - 1 - step) if way else (z >= step)

            @pl.when(behind)
            def _():
                swap(2 + way * 3 + step, own).wait_recv()

    for way in range(2):
        for step in range(1, LINE):
            there = (z >= step) if way else (z <= LINE - 1 - step)

            @pl.when(there)
            def _():
                swap(2 + way * 3 + step, own).wait_send()

    o_gain[...] = gain_buf[0]
    for way in range(2):
        for step in range(1, LINE):
            behind = (z <= LINE - 1 - step) if way else (z >= step)

            @pl.when(behind)
            def _():
                o_gain[...] = o_gain[...] + gain_buf[2 + way * 3 + step]


def scatter_grads(mats, up, down, table, gains):
    ranks = lax.axis_size("dp")
    count, width = mats.shape[0], mats.shape[1]
    per = width // ranks
    if ranks != 4 * LINE:
        part = lambda value, axis: lax.psum_scatter(
            value, "dp", scatter_dimension=axis, tiled=True
        ).astype(F32)
        return part(mats, 1), part(up, 0), part(down, 0), part(table, 0).T, part(gains, 1)[:3]
    shards = [
        (count, per, width), (up.shape[0] // ranks, up.shape[1]), (down.shape[0] // ranks, width),
        (table.shape[0] // ranks, table.shape[1]),
    ]
    dma = pltpu.SemaphoreType.DMA
    outs = pl.pallas_call(
        scatter_kernel,
        out_shape=[shape(s, F32) for s in shards] + [shape(gains.shape, F32)],
        in_specs=[pl.BlockSpec(memory_space=pltpu.VMEM)] * 5,
        out_specs=[pl.BlockSpec(memory_space=pltpu.VMEM)] * 5,
        scratch_shapes=[pltpu.VMEM((LINE, 2) + s, BF) for s in shards]
        + [pltpu.VMEM((LINE,) + s, BF) for s in shards]
        + [pltpu.VMEM((LINE, 2) + s, BF) for s in shards]
        + [pltpu.VMEM((9,) + gains.shape, F32)]
        + [
            dma((4, LINE, 2)), dma((4, LINE, 2)), dma((4, LINE)), dma((4, LINE)), dma((4, LINE, 2)),
            dma((4, LINE, 2)), dma((9,)), dma((9,)),
        ],
        compiler_params=pltpu.CompilerParams(
            collective_id=1, has_side_effects=True, vmem_limit_bytes=VMEM_BYTES
        ),
        name="scatter",
    )(mats, up, down, table, gains)
    mats, up, down, table, gains = outs
    gains = lax.dynamic_slice_in_dim(gains, lax.axis_index("dp") * per, per, 1)[:3]
    return mats, up, down, table.T, gains


def unset(outs):
    return pl.pallas_call(
        lambda *refs: None,
        out_shape=outs,
        out_specs=[pl.BlockSpec(memory_space=pl.ANY)] * len(outs),
        name="unset",
    )()


def to_section(value, source):
    return lax.ppermute(value, "section", [(source, 1 - source)])


def mask_arrays(segments, levels):
    first = jnp.concatenate(
        [jnp.ones_like(segments[:, :1], bool), segments[:, 1:] != segments[:, :-1]], axis=1
    )
    usable = jnp.where((levels[0] > 0) | first, segments, -1)
    cols = jnp.stack([usable, segments, levels[1]] + [segments] * 5, axis=-1)
    rows = jnp.stack([segments, levels[1]], axis=1)
    return cols, rows.reshape(rows.shape[0], 2, -1, QB)


def body(
    inputs,
    positions,
    projections,
    out_projections,
    ffn_up,
    ffn_down,
    norm_gains,
    segments,
    levels,
    cotangent,
):
    encoder = lax.axis_index("section") == 0
    own = inputs[0, :, 0]
    cot = cotangent[:, 0]
    micro, length, width = own.shape
    z = sizes(length, width, ffn_up.shape[2])
    cols, rows = mask_arrays(segments[:, 0], levels[:, :, 0])

    mats_all, up, down, table, gains = gather_weights(
        projections[0], out_projections[0], ffn_up[0], ffn_down[0], positions[0], norm_gains[0]
    )
    mats, lent = mats_all[:4], to_section(mats_all[4:], 0)
    mats_b = jnp.concatenate([mats_all[4:], lent])
    gains = jnp.concatenate([gains.astype(F32), jnp.zeros((5, width), F32)])

    attn = [z["qkv"], z["weights"], z["tok"], z["tok32"]]
    extra = [z["tok32"], z["hidden"], z["hidden"]]

    def first_encoder(m):
        mem, *kept = encode(z, own[m], table, gains, mats, up, down, cols[m], rows[m])
        return (mem, *kept)

    def first_decoder(m):
        kept = self_forward(z, own[m], table, gains, mats, cols[m], rows[m])
        return (*unset([z["tok"]]), *kept, *unset(extra))

    kept, mems, sent = [], [], []
    for m in range(micro):
        mem, *rest = lax.cond(encoder, partial(first_encoder, m), partial(first_decoder, m))
        kept.append(rest)
        sent.append(mem)
        mems.append(to_section(mem, 0))

    crossed = [z["tok"], z["tok"], z["tok32"], z["mats"], z["up"], z["down"], z["gains"]]
    outs, dmems, dh1s, prior = [], [], [], ()
    for m in range(micro):

        def middle_decoder():
            return tuple(
                cross(z, kept[m][3], mems[m], cot[m], gains, mats_b, up, down, cols[m], rows[m], prior)
            )

        def middle_encoder():
            return tuple(unset(crossed))

        out, dmem, dh1, *prior = lax.cond(encoder, middle_encoder, middle_decoder)
        outs.append(out)
        dmems.append(to_section(dmem, 1))
        dh1s.append(dh1)
    g_cross, g_up, g_down, g_gains = prior

    g_ins, prior = [], ()
    for m in reversed(range(micro)):
        def last_encoder():
            g_in, *grads = encode_back(
                z, own[m], table, gains, mats, up, down, kept[m], dmems[m], prior
            )
            return (g_in, *grads)

        def last_decoder():
            less = (prior[0], prior[3], prior[4]) if prior else ()
            g_in, g_mats, g_table, g_gains = self_back(
                z, own[m], table, gains, mats, kept[m][:3], dh1s[m], less
            )
            return (g_in, g_mats, *unset([z["up"], z["down"]]), g_table, g_gains)

        g_in, *prior = lax.cond(encoder, last_encoder, last_decoder)
        g_ins.insert(0, g_in)
    s_mats, s_up, s_down, s_table, s_gains = prior
    s_up = jnp.where(encoder, s_up, g_up)
    s_down = jnp.where(encoder, s_down, g_down)
    s_gains = s_gains + jnp.where(encoder, 0.0, g_gains)

    returned = to_section(g_cross[2:], 1)
    s_mats = jnp.concatenate([s_mats, jnp.where(encoder, returned, g_cross[:2])])
    r_mats, r_up, r_down, r_table, r_gains = scatter_grads(s_mats, s_up, s_down, s_table, s_gains)
    d_proj = jnp.stack([r_mats[0], r_mats[1], r_mats[2], r_mats[4]])
    d_out = jnp.stack([r_mats[3], r_mats[5]])

    main = [jnp.where(encoder, kept_mem, out) for kept_mem, out in zip(sent, outs)]
    return (
        jnp.stack(main)[None, :, None],
        jnp.stack(g_ins)[None, :, None],
        r_table[None],
        d_proj[None],
        d_out[None],
        r_up[None],
        r_down[None],
        r_gains[None],
    )


def solution(mesh):
    in_specs = (
        P("section", None, "dp", None, None),
        P("section", None, "dp"),
        P("section", None, "dp", None),
        P("section", None, "dp", None),
        P("section", "dp", None),
        P("section", "dp", None),
        P("section", None, "dp"),
        P(None, "dp", None),
        P(None, None, "dp", None),
        P(None, "dp", None, None),
    )
    out_specs = (
        P("section", None, "dp", None, None),
        P("section", None, "dp", None, None),
        P("section", None, "dp"),
        P("section", None, "dp", None),
        P("section", None, "dp", None),
        P("section", "dp", None),
        P("section", "dp", None),
        P("section", None, "dp"),
    )
    return jax.shard_map(body, mesh=mesh, in_specs=in_specs, out_specs=out_specs, check_vma=False)
```

```python
from functools import partial

import jax
import jax.numpy as jnp
from jax import lax
from jax.experimental import pallas as pl
from jax.experimental.pallas import tpu as pltpu
from jax.sharding import PartitionSpec as P

BF = jnp.bfloat16
F32 = jnp.float32
DH = 64
PAIR = 2 * DH
QB = 128
WIN = 256
TB = 256
VMEM_BYTES = 62 * 1024 * 1024


def nn(left, right):
    return jnp.dot(left, right, preferred_element_type=F32)


def nt(left, right):
    return lax.dot_general(left, right, (((1,), (1,)), ((), ())), preferred_element_type=F32)


def tn(left, right):
    return lax.dot_general(left, right, (((0,), (0,)), ((), ())), preferred_element_type=F32)


def norm_parts(stream):
    centred = stream - jnp.mean(stream, axis=-1, keepdims=True)
    scale = lax.rsqrt(jnp.mean(centred * centred, axis=-1, keepdims=True) + 1e-05)
    return centred * scale, scale


def norm_back(grad, unit, scale, gain):
    inner = grad * gain
    first = jnp.mean(inner, axis=-1, keepdims=True)
    second = jnp.mean(inner * unit, axis=-1, keepdims=True)
    return scale * (inner - first - unit * second), jnp.sum(grad * unit, axis=0, keepdims=True)


def block_at(index, size):
    if isinstance(index, int):
        return pl.ds(index * size, size)
    return pl.ds(pl.multiple_of(index * size, size), size)


def lane_halves(scale=1.0):
    lane = lax.broadcasted_iota(jnp.int32, (1, PAIR), 1)
    low = jnp.where(lane < DH, scale, 0.0).astype(BF)
    high = jnp.where(lane < DH, 0.0, scale).astype(BF)
    return low, high


def both_heads(block, halves):
    return jnp.concatenate([block * halves[0], block * halves[1]], axis=0)


def join_heads(stacked):
    lane = lax.broadcasted_iota(jnp.int32, (QB, PAIR), 1)
    return jnp.where(lane < DH, stacked[:QB], stacked[QB:])


def window_start(index, length):
    return pl.multiple_of(jnp.clip(index * QB - DH, 0, length - WIN), DH)


def make_codes(segments, source_level, target_level, codes_ref, cols_ref):
    segment = segments[...]
    length = segment.shape[1]
    before = pltpu.roll(segment, 1, axis=1)
    lane = lax.broadcasted_iota(jnp.int32, (1, length), 1)
    first = (lane == 0) | (segment != before)
    usable = jnp.where(first | (source_level[...] > 0), segment, -1)
    row = lax.broadcasted_iota(jnp.int32, (8, length), 0)
    codes = jnp.where(row == 0, usable, jnp.where(row == 1, segment, target_level[...]))
    codes_ref[...] = codes
    cols_ref[...] = codes.T


def mask_bias(index, start, codes_ref, cols_ref, causal):
    keys = cols_ref[pl.ds(start, WIN), :]
    queries = codes_ref[:, block_at(index, QB)]
    query_segment = queries[1:2, :]
    if causal:
        key_id = start + lax.broadcasted_iota(jnp.int32, (WIN, QB), 0)
        query_id = index * QB + lax.broadcasted_iota(jnp.int32, (WIN, QB), 1)
        allowed = (keys[:, 1:2] == query_segment) & (
            (keys[:, 2:3] < queries[2:3, :]) | (key_id == query_id)
        )
    else:
        allowed = keys[:, 0:1] == query_segment
    bias = jnp.where(allowed, 0.0, -1e30)
    return jnp.concatenate([bias, bias], axis=1)


def attend_block(index, q_ref, k_ref, v_ref, codes_ref, cols_ref, weights_ref, mixed_ref, causal):
    length, width = q_ref.shape
    start = window_start(index, length)
    rows = block_at(index, QB)
    bias = mask_bias(index, start, codes_ref, cols_ref, causal)
    halves = lane_halves(DH ** -0.5)
    for pair in range(width // PAIR):
        lanes = slice(pair * PAIR, (pair + 1) * PAIR)
        queries = both_heads(q_ref[rows, lanes], halves)
        scores = nt(k_ref[pl.ds(start, WIN), lanes], queries) + bias
        shifted = jnp.exp(scores - jnp.max(scores, axis=0, keepdims=True))
        weights = (shifted * (1.0 / jnp.sum(shifted, axis=0, keepdims=True))).astype(BF)
        weights_ref[index, pair] = weights
        out = tn(weights, v_ref[pl.ds(start, WIN), lanes])
        mixed_ref[rows, lanes] = join_heads(out).astype(BF)


def attend_back_block(
    index, q_ref, k_ref, v_ref, weights_ref, mixed_ref, dmixed_ref, dq_ref, dk_ref, dv_ref
):
    length, width = q_ref.shape
    start = window_start(index, length)
    rows = block_at(index, QB)
    window = pl.ds(start, WIN)
    plain = lane_halves()
    halves = lane_halves(DH ** -0.5)
    ones = jnp.ones((WIN, PAIR), BF)
    for pair in range(width // PAIR):
        lanes = slice(pair * PAIR, (pair + 1) * PAIR)
        queries = both_heads(q_ref[rows, lanes], halves)
        keys = k_ref[window, lanes]
        values = v_ref[window, lanes]
        weights = weights_ref[index, pair]
        dmixed = dmixed_ref[rows, lanes]
        grads = both_heads(dmixed, plain)
        inner = (dmixed.astype(F32) * mixed_ref[rows, lanes].astype(F32) * -1.0).astype(BF)
        left = jnp.concatenate([values, ones], axis=1)
        right = jnp.concatenate([grads, both_heads(inner, plain)], axis=1)
        centred = nt(left, right)
        dscores = (weights.astype(F32) * centred).astype(BF)
        dv_ref[window, lanes] += nn(weights, grads)
        dk_ref[window, lanes] += nn(dscores, queries)
        dq = tn(dscores, keys) * (DH ** -0.5)
        dq_ref[rows, lanes] = join_heads(dq).astype(BF)


def gelu_parts(value):
    cdf = 0.5 + 0.5 * lax.erf(value * (0.5 ** 0.5))
    density = jnp.exp(value * value * -0.5) * 0.3989422804014327
    return value * cdf, cdf + value * density


def feed_block(normed, up_ref, down_ref, hidden_ref, slope_ref, rows):
    total = None
    width = up_ref.shape[1]
    step = 512
    for at in range(0, width, step):
        hidden, slope = gelu_parts(nn(normed, up_ref[:, at : at + step]))
        hidden = hidden.astype(BF)
        hidden_ref[rows, at : at + step] = hidden
        slope_ref[rows, at : at + step] = slope.astype(BF)
        term = nn(hidden, down_ref[at : at + step, :])
        total = term if total is None else total + term
    return total


def feed_back_block(grad, up_ref, down_ref, slope_ref, rows):
    total = None
    width = up_ref.shape[1]
    step = 512
    for at in range(0, width, step):
        dhidden = nt(grad, down_ref[at : at + step, :])
        dup = (dhidden * slope_ref[rows, at : at + step].astype(F32)).astype(BF)
        slope_ref[rows, at : at + step] = dup
        term = nt(dup, up_ref[:, at : at + step])
        total = term if total is None else total + term
    return total


def loop(count, body):
    def step(index, carry):
        body(index)
        return carry

    lax.fori_loop(0, count, step, 0)


def put_grad(out, index, value):
    if out.prior is not None:
        value = value + out.buf[index].astype(F32)
    out.buf[index] = value.astype(BF)


def weight_grad(out, left_t_refs, right_refs, transposed):
    step = 512
    width = right_refs[0].shape[1]

    def slab(index):
        cols = block_at(index, step)
        value = None
        for left_t, right in zip(left_t_refs, right_refs):
            term = nn(left_t[...], right[:, cols])
            value = term if value is None else value + term
        if transposed:
            put_grad(out, (cols, slice(None)), value.T)
        else:
            put_grad(out, (slice(None), cols), value)

    loop(width // step, slab)


def add_gain(out, row, value):
    out.buf[row : row + 1, :] += value


class Source:
    def __init__(self, hbm, buf, sem):
        self.buf, self.copy, self.here = buf, pltpu.make_async_copy(hbm, buf, sem), False
        self.copy.start()

    def __call__(self):
        if not self.here:
            self.copy.wait()
            self.here = True
        return self.buf


class Sink:
    def __init__(self, hbm, buf, sems, first, parts, axis, prior):
        self.hbm, self.buf, self.sems, self.first = hbm, buf, sems, first
        self.parts, self.axis, self.prior = parts, axis, prior

    def copy(self, part):
        view = [slice(None)] * len(self.buf.shape)
        size = self.buf.shape[self.axis] // self.parts
        view[self.axis] = block_at(part, size)
        view = tuple(view)
        return pltpu.make_async_copy(
            self.buf.at[view], self.hbm.at[view], self.sems.at[self.first + part]
        )

    def send(self, part=0):
        self.copy(part).start()

    def wait(self):
        for part in range(self.parts):
            self.copy(part).wait()


def source(array, *index):
    return (array, index)


def sink(full, *index, parts=1, axis=0, prior=None):
    return (full, index, parts, axis, prior)


def inner_shape(dims, index):
    kept = []
    for at, size in enumerate(dims):
        item = index[at] if at < len(index) else slice(None)
        if isinstance(item, slice):
            kept.append(len(range(*item.indices(size))))
    return tuple(kept)


def run(kernel, name, ins, outs, scratch, passes=(), extra=()):
    priors = [(number, out[4]) for number, out in enumerate(outs) if out[4] is not None]
    n_sems = len(ins) + len(priors) + 2 * len(passes) + sum(out[2] for out in outs)

    def body(*refs):
        refs = list(refs)
        take = lambda count: [refs.pop(0) for _ in range(count)]
        r_ins, r_priors, r_passes = take(len(ins)), take(len(priors)), take(len(passes))
        r_outs = take(len(outs) + len(extra))
        b_ins, b_outs, b_passes = take(len(ins)), take(len(outs)), take(len(passes))
        r_scratch = take(len(scratch))
        (sems,) = refs
        view = lambda ref, index: ref.at[index] if index else ref
        sources = [
            Source(view(ref, index), buf, sems.at[at])
            for at, (ref, (_, index), buf) in enumerate(zip(r_ins, ins, b_ins))
        ]
        at = len(ins)
        early = {}
        for ref, (number, _) in zip(r_priors, priors):
            early[number] = Source(ref, b_outs[number], sems.at[at])
            at += 1
        through, onward = [], []
        for ref, buf, (_, number, index) in zip(r_passes, b_passes, passes):
            through.append(Source(ref, buf, sems.at[at]))
            onward.append(pltpu.make_async_copy(buf, view(r_outs[number], index), sems.at[at + 1]))
            at += 2

        def hand_on():
            for item, copy in zip(through, onward):
                item()
                copy.start()

        sinks = []
        for number, (ref, (_, index, parts, axis, _), buf) in enumerate(zip(r_outs, outs, b_outs)):
            sinks.append(Sink(view(ref, index), buf, sems, at, parts, axis, early.get(number)))
            at += parts
        kernel(hand_on, *sources, *sinks, *r_scratch)
        for item in sources:
            item()
        for item in sinks:
            item.wait()
        for copy in onward:
            copy.wait()

    anywhere = pl.BlockSpec(memory_space=pl.ANY)
    arrays = [array for array, _ in ins] + [array for _, array in priors] + [p[0] for p in passes]
    buffers = [shape(inner_shape(array.shape, index), array.dtype) for array, index in ins]
    buffers += [shape(inner_shape(out[0].shape, out[1]), out[0].dtype) for out in outs]
    buffers += [shape(array.shape, array.dtype) for array, _, _ in passes]
    return pl.pallas_call(
        body,
        out_shape=[out[0] for out in outs] + list(extra),
        in_specs=[anywhere] * len(arrays),
        out_specs=[anywhere] * (len(outs) + len(extra)),
        scratch_shapes=[pltpu.VMEM(s.shape, s.dtype) for s in buffers + list(scratch)]
        + [pltpu.SemaphoreType.DMA((n_sems,))],
        compiler_params=pltpu.CompilerParams(vmem_limit_bytes=VMEM_BYTES),
        name=name,
    )(*arrays)


def encode_kernel(
    hand_on, src, table, gains, segments, source_level, target_level, mats, up, down,
    mem, qkv, weights, mixed, x1, x2, hidden, slope, codes, cols,
):
    length = src.buf.shape[0]
    make_codes(segments(), source_level(), target_level(), codes, cols)
    src, table, gains, mats = src(), table(), gains(), mats()

    def project(index):
        rows = block_at(index, TB)
        unit, _ = norm_parts(src[rows, :].astype(F32) + table[rows, :].astype(F32))
        normed = (unit * gains[0:1, :]).astype(BF)
        for which in range(3):
            qkv.buf[which, rows, :] = nn(normed, mats[which]).astype(BF)
        qkv.send(index)

    loop(length // TB, project)
    up, down = up(), down()

    def rest(index):
        for part in range(TB // QB):
            attend_block(
                index * (TB // QB) + part,
                qkv.buf.at[0], qkv.buf.at[1], qkv.buf.at[2], codes, cols, weights.buf, mixed.buf, False,
            )
        weights.send(index)
        mixed.send(index)
        rows = block_at(index, TB)
        stream = src[rows, :].astype(F32) + table[rows, :].astype(F32)
        stream = stream + nn(mixed.buf[rows, :], mats[3])
        x1.buf[rows, :] = stream
        x1.send(index)
        unit, _ = norm_parts(stream)
        normed = (unit * gains[1:2, :]).astype(BF)
        stream = stream + feed_block(normed, up, down, hidden.buf, slope.buf, rows)
        x2.buf[rows, :] = stream
        unit, _ = norm_parts(stream)
        mem.buf[rows, :] = (unit * gains[2:3, :]).astype(BF)
        for item in (mem, x2, hidden, slope):
            item.send(index)

    loop(length // TB, rest)


def encode_back_kernel(
    hand_on, x2, dmem, gains, slope, down, up, x1, mats, hidden, mixed, qkv, weights, src, table,
    g_in, g_mats, g_up, g_down, g_table, g_gains,
    dy, dy_t, a_t, dx, dmixed, dq, dk, dv,
):
    length = src.buf.shape[0]
    if g_gains.prior is None:
        g_gains.buf[...] = jnp.zeros_like(g_gains.buf)
    else:
        g_gains.prior()
    dk[...] = jnp.zeros_like(dk)
    dv[...] = jnp.zeros_like(dv)
    x2, dmem, gains, slope, down, up, x1, mats = (
        x2(), dmem(), gains(), slope(), down(), up(), x1(), mats()
    )

    def feed_step(index):
        rows = block_at(index, TB)
        unit, scale = norm_parts(x2[rows, :])
        grad, d_gain = norm_back(dmem[rows, :].astype(F32), unit, scale, gains[2:3, :])
        add_gain(g_gains, 2, d_gain)
        low = grad.astype(BF)
        dy_t[:, rows] = low.T
        dnormed = feed_back_block(low, up, down, slope, rows)
        unit, scale = norm_parts(x1[rows, :])
        a_t[:, rows] = (unit * gains[1:2, :]).astype(BF).T
        back, d_gain = norm_back(dnormed, unit, scale, gains[1:2, :])
        add_gain(g_gains, 1, d_gain)
        grad = grad + back
        dx[rows, :] = grad
        low = grad.astype(BF)
        dy[rows, :] = low
        dmixed[rows, :] = nt(low, mats[3]).astype(BF)

    loop(length // TB, feed_step)
    for item in (g_up, g_down, g_mats, g_table):
        if item.prior is not None:
            item.prior()
    weight_grad(g_up, [a_t], [slope], False)
    g_up.send()
    weight_grad(g_down, [dy_t], [hidden()], True)
    g_down.send()
    mixed = mixed()
    put_grad(g_mats, 3, tn(mixed[...], dy[...]))
    qkv, weights = qkv(), weights()

    def attend_step(index):
        attend_back_block(
            index, qkv.at[0], qkv.at[1], qkv.at[2], weights, mixed, dmixed, dq, dk, dv
        )

    loop(length // QB, attend_step)
    hand_on()
    src, table = src(), table()

    def project_step(index):
        rows = block_at(index, TB)
        unit, scale = norm_parts(src[rows, :].astype(F32) + table[rows, :].astype(F32))
        a_t[:, rows] = (unit * gains[0:1, :]).astype(BF).T
        dnormed = nt(dq[rows, :], mats[0])
        dnormed += nt(dk[rows, :].astype(BF), mats[1])
        dnormed += nt(dv[rows, :].astype(BF), mats[2])
        back, d_gain = norm_back(dnormed, unit, scale, gains[0:1, :])
        add_gain(g_gains, 0, d_gain)
        grad = dx[rows, :] + back
        g_in.buf[rows, :] = grad
        g_in.send(index)
        put_grad(g_table, (slice(None), rows), grad.T)

    loop(length // TB, project_step)
    g_table.send()
    g_gains.send()
    put_grad(g_mats, 0, nn(a_t[...], dq[...]))
    put_grad(g_mats, 1, nn(a_t[...], dk[...].astype(BF)))
    put_grad(g_mats, 2, nn(a_t[...], dv[...].astype(BF)))
    g_mats.send()


def self_kernel(
    hand_on, tgt, table, gains, segments, source_level, target_level, mats, qkv, weights, mixed, h1, codes, cols
):
    length = tgt.buf.shape[0]
    make_codes(segments(), source_level(), target_level(), codes, cols)
    tgt, table, gains, mats = tgt(), table(), gains(), mats()

    def project(index):
        rows = block_at(index, TB)
        stream = table[rows, :].astype(F32)
        unit, _ = norm_parts(stream)
        qkv.buf[0, rows, :] = nn((unit * gains[0:1, :]).astype(BF), mats[0]).astype(BF)
        unit, _ = norm_parts(tgt[rows, :].astype(F32) + stream)
        normed = (unit * gains[0:1, :]).astype(BF)
        for which in (1, 2):
            qkv.buf[which, rows, :] = nn(normed, mats[which]).astype(BF)
        qkv.send(index)

    loop(length // TB, project)

    def rest(index):
        for part in range(TB // QB):
            attend_block(
                index * (TB // QB) + part,
                qkv.buf.at[0], qkv.buf.at[1], qkv.buf.at[2], codes, cols, weights.buf, mixed.buf, True,
            )
        rows = block_at(index, TB)
        h1.buf[rows, :] = table[rows, :].astype(F32) + nn(mixed.buf[rows, :], mats[3])
        for item in (weights, mixed, h1):
            item.send(index)

    loop(length // TB, rest)


def self_back_kernel(late, hand_on, *refs):
    refs = list(refs)
    (dh1, mats, mixed, qkv, weights, tgt, table, gains) = refs[:8]
    refs = refs[8:]
    rows_kept = late // 4
    kept = [refs[4 * at : 4 * at + 4] for at in range(rows_kept)]
    refs = refs[late:]
    (g_in, g_mats, g_table, g_gains) = refs[:4]
    refs = refs[4:]
    if late:
        (g_up, g_down) = refs[:2]
        refs = refs[2:]
    (dy, a_t, b_t, dmixed, dq, dk, dv) = refs[:7]
    length = tgt.buf.shape[0]
    g_gains.prior()
    dk[...] = jnp.zeros_like(dk)
    dv[...] = jnp.zeros_like(dv)
    dh1, mats, mixed = dh1(), mats(), mixed()

    def out_step(index):
        rows = block_at(index, TB)
        low = dh1[rows, :].astype(BF)
        dy[rows, :] = low
        dmixed[rows, :] = nt(low, mats[3]).astype(BF)

    loop(length // TB, out_step)
    for item in (g_mats, g_table):
        if item.prior is not None:
            item.prior()
    put_grad(g_mats, 3, tn(mixed[...], dy[...]))
    qkv, weights = qkv(), weights()

    def attend_step(index):
        attend_back_block(
            index, qkv.at[0], qkv.at[1], qkv.at[2], weights, mixed, dmixed, dq, dk, dv
        )

    loop(length // QB, attend_step)
    hand_on()
    tgt, table, gains = tgt(), table(), gains()

    def project_step(index):
        rows = block_at(index, TB)
        stream = table[rows, :].astype(F32)
        unit, scale = norm_parts(stream)
        a_t[:, rows] = (unit * gains[0:1, :]).astype(BF).T
        back, d_gain = norm_back(nt(dq[rows, :], mats[0]), unit, scale, gains[0:1, :])
        dtable = dh1[rows, :] + back
        unit, scale = norm_parts(tgt[rows, :].astype(F32) + stream)
        b_t[:, rows] = (unit * gains[0:1, :]).astype(BF).T
        dnormed = nt(dk[rows, :].astype(BF), mats[1])
        dnormed += nt(dv[rows, :].astype(BF), mats[2])
        back, d_gain_too = norm_back(dnormed, unit, scale, gains[0:1, :])
        add_gain(g_gains, 0, d_gain + d_gain_too)
        g_in.buf[rows, :] = back
        g_in.send(index)
        put_grad(g_table, (slice(None), rows), (dtable + back).T)

    loop(length // TB, project_step)
    g_table.send()
    g_gains.send()
    put_grad(g_mats, 0, nn(a_t[...], dq[...]))
    put_grad(g_mats, 1, nn(b_t[...], dk[...].astype(BF)))
    put_grad(g_mats, 2, nn(b_t[...], dv[...].astype(BF)))
    g_mats.send()
    if late:
        weight_grad(g_up, [one[0]() for one in kept], [one[1]() for one in kept], False)
        g_up.send()
        cot_t = refs[7:]
        for one, flat in zip(kept, cot_t):
            flat[...] = one[2]()[...].T
        weight_grad(g_down, cot_t, [one[3]() for one in kept], True)
        g_down.send()


def cross_kernel(
    hand_on, h1, gains, segments, source_level, target_level, mats, mem, lent, up, down, cot,
    out, dmem, dh1, g_mats, g_gains, a_t, dup, hidden,
    codes, cols, qkv, weights, mixed, h2, dy, b_t, dmixed, dq, dk, dv,
):
    length = h1.buf.shape[0]
    make_codes(segments(), source_level(), target_level(), codes, cols)
    if g_gains.prior is None:
        g_gains.buf[...] = jnp.zeros_like(g_gains.buf)
    else:
        g_gains.prior()
    dk[...] = jnp.zeros_like(dk)
    dv[...] = jnp.zeros_like(dv)
    h1, gains, mats, mem, lent = h1(), gains(), mats(), mem(), lent()

    def project(index):
        rows = block_at(index, TB)
        unit, _ = norm_parts(h1[rows, :])
        qkv[0, rows, :] = nn((unit * gains[1:2, :]).astype(BF), mats[0]).astype(BF)
        qkv[1, rows, :] = nn(mem[rows, :], lent[0]).astype(BF)
        qkv[2, rows, :] = nn(mem[rows, :], lent[1]).astype(BF)

    loop(length // TB, project)
    up, down, cot = up(), down(), cot()

    def middle(index):
        for part in range(TB // QB):
            attend_block(
                index * (TB // QB) + part,
                qkv.at[0], qkv.at[1], qkv.at[2], codes, cols, weights, mixed, False,
            )
        rows = block_at(index, TB)
        stream = h1[rows, :] + nn(mixed[rows, :], mats[1])
        unit, scale = norm_parts(stream)
        normed = (unit * gains[2:3, :]).astype(BF)
        a_t.buf[:, rows] = normed.T
        fed = feed_block(normed, up, down, hidden.buf, dup.buf, rows)
        out.buf[rows, :] = (stream + fed).astype(BF)
        low = cot[rows, :]
        dnormed = feed_back_block(low, up, down, dup.buf, rows)
        back, d_gain = norm_back(dnormed, unit, scale, gains[2:3, :])
        add_gain(g_gains, 2, d_gain)
        grad = low.astype(F32) + back
        h2[rows, :] = grad
        low = grad.astype(BF)
        dy[rows, :] = low
        dmixed[rows, :] = nt(low, mats[1]).astype(BF)
        for item in (out, hidden, dup):
            item.send(index)

    loop(length // TB, middle)
    a_t.send()

    def attend_step(index):
        attend_back_block(
            index, qkv.at[0], qkv.at[1], qkv.at[2], weights, mixed, dmixed, dq, dk, dv
        )

    loop(length // QB, attend_step)
    if g_mats.prior is not None:
        g_mats.prior()

    def project_step(index):
        rows = block_at(index, TB)
        dkeys = dk[rows, :].astype(BF)
        dvalues = dv[rows, :].astype(BF)
        dmem.buf[rows, :] = (nt(dkeys, lent[0]) + nt(dvalues, lent[1])).astype(BF)
        dmem.send(index)
        unit, scale = norm_parts(h1[rows, :])
        b_t[:, rows] = (unit * gains[1:2, :]).astype(BF).T
        back, d_gain = norm_back(nt(dq[rows, :], mats[0]), unit, scale, gains[1:2, :])
        add_gain(g_gains, 1, d_gain)
        dh1.buf[rows, :] = h2[rows, :] + back
        dh1.send(index)

    loop(length // TB, project_step)
    g_gains.send()
    put_grad(g_mats, 0, nn(b_t[...], dq[...]))
    put_grad(g_mats, 1, tn(mixed[...], dy[...]))
    put_grad(g_mats, 2, tn(mem[...], dk[...].astype(BF)))
    put_grad(g_mats, 3, tn(mem[...], dv[...].astype(BF)))
    g_mats.send()


def shape(dims, kind):
    return jax.ShapeDtypeStruct(dims, kind)


def sizes(length, width, ff, micro):
    blocks = length // QB
    pairs = width // PAIR
    return dict(
        tok=shape((length, width), BF),
        tok32=shape((length, width), F32),
        outputs=shape((micro, length, width), BF),
        g_in=shape((micro, length, width), F32),
        qkv=shape((3, length, width), BF),
        weights=shape((blocks, pairs, WIN, 2 * QB), BF),
        hidden=shape((length, ff), BF),
        tokt=shape((width, length), BF),
        mats=shape((4, width, width), BF),
        up=shape((width, ff), BF),
        down=shape((ff, width), BF),
        gains=shape((8, width), F32),
        codes=shape((8, length), jnp.int32),
        cols=shape((length, 8), jnp.int32),
    )


def code_sources(w, m):
    return [
        source(w["segments"], m), source(w["levels"], 0, m), source(w["levels"], 1, m),
    ]


def encode(z, w, m):
    parts = z["tok"].shape[0] // TB
    ins = [
        source(w["own"], m), source(w["table"]), source(w["gains"]), *code_sources(w, m),
        source(w["mats"], slice(0, 4)), source(w["up"]), source(w["down"]),
    ]
    outs = [
        sink(z["tok"], parts=parts), sink(z["qkv"], parts=parts, axis=1),
        sink(z["weights"], parts=parts), sink(z["tok"], parts=parts), sink(z["tok32"], parts=parts),
        sink(z["tok32"], parts=parts), sink(z["hidden"], parts=parts), sink(z["hidden"], parts=parts),
    ]
    return run(encode_kernel, "encode", ins, outs, [z["codes"], z["cols"]])


def encode_back(z, w, m, kept, dmem, prior, last):
    parts = z["tok"].shape[0] // TB
    qkv, weights, mixed, x1, x2, hidden, slope = kept
    ins = [
        source(x2), source(dmem), source(w["gains"]), source(slope), source(w["down"]),
        source(w["up"]), source(x1), source(w["mats"], slice(0, 4)), source(hidden), source(mixed),
        source(qkv), source(weights), source(w["own"], m), source(w["table"]),
    ]
    g_mats, g_up, g_down, g_table, g_gains = prior if prior else [None] * 5
    outs, passes = last_outs(z, m, parts, last)
    outs += [
        sink(z["mats"], prior=g_mats), sink(z["up"], prior=g_up), sink(z["down"], prior=g_down),
        sink(z["tokt"], prior=g_table), sink(z["gains"], prior=g_gains),
    ]
    scratch = [
        z["tok"], z["tokt"], z["tokt"], z["tok32"], z["tok"], z["tok"], z["tok32"], z["tok32"],
    ]
    return run(encode_back_kernel, "encode_back", ins, outs, scratch, passes, [z["outputs"]] if last else [])


def last_outs(z, m, parts, last):
    if last is None:
        return [sink(z["tok32"], parts=parts)], []
    mains, grads = last
    passes = [(main, -1, (at,)) for at, main in enumerate(mains)]
    passes += [(grad, 0, (at,)) for at, grad in enumerate(grads)]
    return [sink(z["g_in"], m, parts=parts)], passes


def self_forward(z, w, m):
    parts = z["tok"].shape[0] // TB
    ins = [
        source(w["own"], m), source(w["table"]), source(w["gains"]), *code_sources(w, m),
        source(w["mats"], slice(0, 4)),
    ]
    outs = [
        sink(z["qkv"], parts=parts, axis=1), sink(z["weights"], parts=parts),
        sink(z["tok"], parts=parts), sink(z["tok32"], parts=parts),
    ]
    return run(self_kernel, "self_forward", ins, outs, [z["codes"], z["cols"]])


def self_back(z, w, m, kept, dh1, prior, g_gains, last, feeds=()):
    parts = z["tok"].shape[0] // TB
    qkv, weights, mixed = kept
    ins = [
        source(dh1), source(w["mats"], slice(0, 4)), source(mixed), source(qkv), source(weights),
        source(w["own"], m), source(w["table"]), source(w["gains"]),
    ]
    for at, (a_t, dup, hidden) in enumerate(feeds):
        ins += [source(a_t), source(dup), source(w["cot"], at), source(hidden)]
    g_mats, g_table = prior if prior else [None] * 2
    outs, passes = last_outs(z, m, parts, last)
    outs += [
        sink(z["mats"], prior=g_mats), sink(z["tokt"], prior=g_table), sink(z["gains"], prior=g_gains),
    ]
    if feeds:
        outs += [sink(z["up"]), sink(z["down"])]
    scratch = [
        z["tok"], z["tokt"], z["tokt"], z["tok"], z["tok"], z["tok32"], z["tok32"],
    ] + [z["tokt"]] * len(feeds)
    return run(
        partial(self_back_kernel, 4 * len(feeds)), "self_back", ins, outs, scratch, passes,
        [z["outputs"]] if last else [],
    )


def cross(z, w, m, h1, mem, prior):
    parts = z["tok"].shape[0] // TB
    ins = [
        source(h1), source(w["gains"]), *code_sources(w, m), source(w["mats"], slice(4, 6)),
        source(mem), source(w["lent"]), source(w["up"]), source(w["down"]), source(w["cot"], m),
    ]
    g_mats, g_gains = prior if prior else [None] * 2
    outs = [
        sink(z["tok"], parts=parts), sink(z["tok"], parts=parts), sink(z["tok32"], parts=parts),
        sink(z["mats"], prior=g_mats), sink(z["gains"], prior=g_gains), sink(z["tokt"]),
        sink(z["hidden"], parts=parts), sink(z["hidden"], parts=parts),
    ]
    scratch = [
        z["codes"], z["cols"], z["qkv"], z["weights"], z["tok"], z["tok32"], z["tok"], z["tokt"],
        z["tok"], z["tok"], z["tok32"], z["tok32"],
    ]
    return run(cross_kernel, "cross", ins, outs, scratch)


LINE = 4
TABLE_ROWS = 48
KINDS = 5
MESH = pl.DeviceIdType.MESH


def place():
    me = lax.axis_index("dp")
    return me // 4, (me // 2) % 2, me % 2


def rank_of(z, x, core):
    return z * 4 + x * 2 + core


def at_rank(ref, axis, per, rank):
    rows = pl.ds(pl.multiple_of(rank * per, per), per)
    return ref.at[rows, :] if axis == 0 else ref.at[:, rows, :]


def greet(z, x, core):
    barrier = pltpu.get_barrier_semaphore()

    def signal(rank):
        pl.semaphore_signal(barrier, inc=1, device_id={"dp": rank}, device_id_type=MESH)

    signal(rank_of(z, 1 - x, core))
    signal(rank_of(z, x, 1 - core))

    for step in range(1, LINE):
        signal(rank_of((z + step) % LINE, x, core))
    pl.semaphore_wait(barrier, LINE + 1)


def remote(src, dst, send, recv, rank):
    return pltpu.make_async_remote_copy(
        src_ref=src, dst_ref=dst, send_sem=send, recv_sem=recv, device_id={"dp": rank},
        device_id_type=MESH,
    )


def gather_kernel(
    proj, outp, up, down, pos, gain, o_mats, o_up, o_down, o_table, o_gain,
    packed, s_mats, s_up, s_down, s_table, zsend, zrecv, xsend, xrecv, csend, crecv, here,
):
    z, x, core = place()
    per = pos.shape[1]
    s_table[...] = jnp.zeros_like(s_table)
    s_table[:per, :] = pos[...].T.astype(BF)
    s_table[per : per + gain.shape[0], :per] = gain[...].astype(BF)
    for to, (ref, index) in enumerate(
        ((proj, 0), (proj, 1), (proj, 2), (outp, 0), (proj, 3), (outp, 1))
    ):
        s_mats[to] = ref[index].astype(BF)
    s_up[...] = up[...].astype(BF)
    s_down[...] = down[...].astype(BF)
    greet(z, x, core)

    outs = ((packed, 0), (o_mats, 1), (o_up, 0), (o_down, 0))
    mine = (s_table, s_mats, s_up, s_down)
    kinds = range(len(outs))
    pers = [mine[kind].shape[outs[kind][1]] for kind in kinds]

    def view(kind, rank):
        return at_rank(outs[kind][0], outs[kind][1], pers[kind], rank)

    across = rank_of(z, 1 - x, core)
    sibling = rank_of(z, x, 1 - core)
    own = rank_of(z, x, core)

    def along(kind, way, step, src, rank):
        return remote(
            src, view(kind, rank), zsend.at[kind, way, step], zrecv.at[kind, way, step],
            rank_of(z + (1 - 2 * way), x, core),
        )

    def over(kind, slot, src, rank):
        return remote(src, view(kind, rank), xsend.at[kind, slot], xrecv.at[kind, slot], across)

    def beside(kind, slot, src, rank):
        return remote(src, view(kind, rank), csend.at[kind, slot], crecv.at[kind, slot], sibling)

    def can_send(way):
        return (z > 0) if way else (z < LINE - 1)

    slots = [(0, 0, 0)] + [(1 + way * 3 + step, way, step + 1) for step in range(3) for way in range(2)]

    def begins(way, back):
        return z - back * (1 - 2 * way)

    def exists(way, back):
        if back == 0:
            return None
        return (z <= LINE - 1 - back) if way else (z >= back)

    def when(cond, do):
        if cond is None:
            do()
        else:
            pl.when(cond)(do)

    local = [pltpu.make_async_copy(mine[k], view(k, own), here.at[k]) for k in kinds]

    def begin(kind):
        for way in range(2):

            @pl.when(can_send(way))
            def _():
                along(kind, way, 0, mine[kind], own).start()

        over(kind, 0, mine[kind], own).start()
        beside(kind, 0, mine[kind], own).start()
        local[kind].start()

    def pass_on(kind):
        for slot, way, back in slots[1:]:

            def one():
                rank = rank_of(begins(way, back), x, core)
                block = view(kind, rank)
                along(kind, way, back - 1, block, rank).wait_recv()
                if back < LINE - 1:

                    @pl.when(can_send(way))
                    def _():
                        along(kind, way, back, block, rank).start()

                over(kind, slot, block, rank).start()
                beside(kind, slot, block, rank).start()

            when(exists(way, back), one)

    def share(kind):
        for slot, way, back in slots:

            def one():
                rank = rank_of(begins(way, back), 1 - x, core)
                block = view(kind, rank)
                over(kind, slot, block, rank).wait_recv()
                beside(kind, 7 + slot, block, rank).start()

            when(exists(way, back), one)

    def finish(kind):
        local[kind].wait()
        for way in range(2):
            for step in range(3):
                sent = can_send(way)
                if step > 0:
                    sent = sent & exists(way, step)

                @pl.when(sent)
                def _():
                    along(kind, way, step, mine[kind], own).wait_send()

        for slot, way, back in slots:

            def one():
                over(kind, slot, mine[kind], own).wait_send()
                for part in range(2):
                    copy = beside(kind, slot + 7 * part, mine[kind], own)
                    copy.wait_send()
                    copy.wait_recv()

            when(exists(way, back), one)

    begin(0)
    begin(1)
    pass_on(0)
    begin(2)
    pass_on(1)
    share(0)
    begin(3)
    pass_on(2)
    share(1)
    finish(0)
    o_gain[...] = jnp.zeros_like(o_gain)
    ranks = packed.shape[0] // TABLE_ROWS
    group = 4
    for first in range(0, ranks, group):
        blocks = [packed[rank * TABLE_ROWS : (rank + 1) * TABLE_ROWS, :] for rank in range(first, first + group)]
        lanes = slice(first * per, (first + group) * per)
        o_table[:, lanes] = jnp.concatenate([block[:per] for block in blocks], axis=0).T
        o_gain[: gain.shape[0], lanes] = jnp.concatenate(
            [block[per : per + gain.shape[0], :per] for block in blocks], axis=1
        ).astype(F32)
    pass_on(3)
    share(2)
    share(3)
    for kind in kinds[1:]:
        finish(kind)


def gather_weights(proj, outp, up, down, pos, gain):
    ranks = lax.axis_size("dp")
    count, per, width = proj.shape[0] + outp.shape[0], proj.shape[1], proj.shape[2]
    length = pos.shape[0]
    if ranks != 4 * LINE or per != pos.shape[1] or per + gain.shape[0] > TABLE_ROWS or per * 4 != 128:
        order = [proj[0], proj[1], proj[2], outp[0], proj[3], outp[1]]
        every = lambda value, axis: lax.all_gather(value.astype(BF), "dp", axis=axis, tiled=True)
        gains = every(gain, 1).astype(F32)
        return (
            every(jnp.stack(order), 1), every(up, 0), every(down, 0), every(pos, 1),
            jnp.concatenate([gains, jnp.zeros((8 - gain.shape[0], width), F32)]),
        )
    shards = [
        shape((TABLE_ROWS * ranks, length), BF), shape((count, per, width), BF), shape(up.shape, BF),
        shape(down.shape, BF), shape((TABLE_ROWS, length), BF),
    ]
    outs = [
        shape((count, width, width), BF), shape((width, up.shape[1]), BF),
        shape((down.shape[0] * ranks, width), BF), shape((length, width), BF), shape((8, width), F32),
    ]
    dma = pltpu.SemaphoreType.DMA
    in_vmem, anywhere = pl.BlockSpec(memory_space=pltpu.VMEM), pl.BlockSpec(memory_space=pl.ANY)
    return pl.pallas_call(
        gather_kernel,
        out_shape=outs,
        in_specs=[in_vmem] * 6,
        out_specs=[anywhere] * 3 + [in_vmem] * 2,
        scratch_shapes=[pltpu.VMEM(s.shape, s.dtype) for s in shards]
        + [dma((4, 2, 3)), dma((4, 2, 3)), dma((4, 7)), dma((4, 7)), dma((4, 14)), dma((4, 14)), dma((4,))],
        compiler_params=pltpu.CompilerParams(
            collective_id=0, has_side_effects=True, vmem_limit_bytes=VMEM_BYTES
        ),
        name="gather",
    )(proj, outp, up, down, pos, gain)


def scatter_kernel(
    *refs,
):
    take = lambda count: [refs.pop(0) for _ in range(count)]
    refs = list(refs)
    grads, g_gain = take(KINDS), refs.pop(0)
    outs, o_gain = take(KINDS), refs.pop(0)
    cbuf, xbuf, zbuf = take(KINDS), take(KINDS), take(KINDS)
    gain_buf, csend, crecv, xsend, xrecv, zsend, zrecv, gsend, grecv = refs
    z, x, core = place()
    greet(z, x, core)
    across = rank_of(z, 1 - x, core)
    sibling = rank_of(z, x, 1 - core)
    own = rank_of(z, x, core)
    kinds = range(KINDS)
    order = (3, 0, 2, 1)

    def grad(kind, rank):
        ref, axis = grads[kind], len(grads[kind].shape) - 2
        return at_rank(ref, axis, outs[kind].shape[axis], rank)

    def beside(kind, dest, part):
        target_x = x if part else 1 - x
        return remote(
            grad(kind, rank_of(dest, target_x, 1 - core)), cbuf[kind].at[dest, part],
            csend.at[kind, dest, part], crecv.at[kind, dest, part], sibling,
        )

    def over(kind, dest):
        return remote(
            cbuf[kind].at[dest, 0], xbuf[kind].at[dest], xsend.at[kind, dest], xrecv.at[kind, dest], across
        )

    def along(kind, dest, way):
        return remote(
            cbuf[kind].at[dest, 1], zbuf[kind].at[dest, way], zsend.at[kind, dest, way],
            zrecv.at[kind, dest, way], rank_of(z + (1 - 2 * way), x, core),
        )

    def add(into, *others):
        total = into[...].astype(F32)
        for other in others:
            total = total + other[...].astype(F32)
        into[...] = total.astype(BF)

    for kind in kinds:
        for dest in order:
            for part in range(2):
                beside(kind, dest, part).start()
    for kind in kinds:
        for dest in order:
            beside(kind, dest, 0).wait_recv()
            add(cbuf[kind].at[dest, 0], grad(kind, rank_of(dest, 1 - x, core)))
            over(kind, dest).start()

    for kind in kinds:
        for dest in order:
            beside(kind, dest, 1).wait_recv()
            over(kind, dest).wait_recv()
            add(cbuf[kind].at[dest, 1], grad(kind, rank_of(dest, x, core)), xbuf[kind].at[dest])
            for way in range(2):
                before = (z > dest) if way else (z < dest)
                far = (z == LINE - 1) if way else (z == 0)

                @pl.when(before)
                def _():
                    @pl.when(jnp.logical_not(far))
                    def _():
                        along(kind, dest, way).wait_recv()
                        add(cbuf[kind].at[dest, 1], zbuf[kind].at[dest, way])

                    along(kind, dest, way).start()

    for kind in kinds:
        for dest in range(LINE):

            @pl.when(z == dest)
            def _():
                total = cbuf[kind][dest, 1].astype(F32)
                if dest > 0:
                    along(kind, dest, 0).wait_recv()
                    total = total + zbuf[kind][dest, 0].astype(F32)
                if dest < LINE - 1:
                    along(kind, dest, 1).wait_recv()
                    total = total + zbuf[kind][dest, 1].astype(F32)
                outs[kind][...] = total

    for kind in kinds:
        for dest in order:
            over(kind, dest).wait_send()
            for part in range(2):
                beside(kind, dest, part).wait_send()
            for way in range(2):

                @pl.when((z > dest) if way else (z < dest))
                def _():
                    along(kind, dest, way).wait_send()

    gain_buf[0] = g_gain[...]

    def swap(index, rank):
        return remote(gain_buf.at[0], gain_buf.at[index], gsend.at[index], grecv.at[index], rank)

    for index, rank in ((1, sibling), (2, across)):
        copy = swap(index, rank)
        copy.start()
        copy.wait_send()
        copy.wait_recv()
        gain_buf[0] = gain_buf[0] + gain_buf[index]
    for way in range(2):
        for step in range(1, LINE):
            ahead = z + step * (1 - 2 * way)
            there = (z >= step) if way else (z <= LINE - 1 - step)

            @pl.when(there)
            def _():
                swap(2 + way * 3 + step, rank_of(ahead, x, core)).start()

    for way in range(2):
        for step in range(1, LINE):
            behind = (z <= LINE - 1 - step) if way else (z >= step)

            @pl.when(behind)
            def _():
                swap(2 + way * 3 + step, own).wait_recv()

    for way in range(2):
        for step in range(1, LINE):
            there = (z >= step) if way else (z <= LINE - 1 - step)

            @pl.when(there)
            def _():
                swap(2 + way * 3 + step, own).wait_send()

    o_gain[...] = gain_buf[0]
    for way in range(2):
        for step in range(1, LINE):
            behind = (z <= LINE - 1 - step) if way else (z >= step)

            @pl.when(behind)
            def _():
                o_gain[...] = o_gain[...] + gain_buf[2 + way * 3 + step]


def scatter_grads(mats, more, up, down, table, gains):
    ranks = lax.axis_size("dp")
    width = mats.shape[1]
    per = width // ranks
    if ranks != 4 * LINE:
        part = lambda value, axis: lax.psum_scatter(
            value, "dp", scatter_dimension=axis, tiled=True
        ).astype(F32)
        return (
            part(mats, 1), part(more, 1), part(up, 0), part(down, 0), part(table, 0).T,
            part(gains, 1)[:3],
        )
    grads = (mats, more, up, down, table)
    shards = []
    for grad in grads:
        dims = list(grad.shape)
        dims[-2] //= ranks
        shards.append(tuple(dims))
    dma = pltpu.SemaphoreType.DMA
    outs = pl.pallas_call(
        scatter_kernel,
        out_shape=[shape(s, F32) for s in shards] + [shape(gains.shape, F32)],
        in_specs=[pl.BlockSpec(memory_space=pltpu.VMEM)] * (KINDS + 1),
        out_specs=[pl.BlockSpec(memory_space=pltpu.VMEM)] * (KINDS + 1),
        scratch_shapes=[pltpu.VMEM((LINE, 2) + s, BF) for s in shards]
        + [pltpu.VMEM((LINE,) + s, BF) for s in shards]
        + [pltpu.VMEM((LINE, 2) + s, BF) for s in shards]
        + [pltpu.VMEM((9,) + gains.shape, F32)]
        + [
            dma((KINDS, LINE, 2)), dma((KINDS, LINE, 2)), dma((KINDS, LINE)), dma((KINDS, LINE)),
            dma((KINDS, LINE, 2)), dma((KINDS, LINE, 2)), dma((9,)), dma((9,)),
        ],
        compiler_params=pltpu.CompilerParams(
            collective_id=1, has_side_effects=True, vmem_limit_bytes=VMEM_BYTES
        ),
        name="scatter",
    )(*grads, gains)
    mats, more, up, down, table, gains = outs
    gains = lax.dynamic_slice_in_dim(gains, lax.axis_index("dp") * per, per, 1)[:3]
    return mats, more, up, down, table.T, gains


def unset(*outs):
    return tuple(
        pl.pallas_call(
            lambda *refs: None,
            out_shape=list(outs),
            out_specs=[pl.BlockSpec(memory_space=pl.ANY)] * len(outs),
            name="unset",
        )()
    )


def to_section(value, source):
    return lax.ppermute(value, "section", [(source, 1 - source)])


def body(
    inputs,
    positions,
    projections,
    out_projections,
    ffn_up,
    ffn_down,
    norm_gains,
    segments,
    levels,
    cotangent,
):
    encoder = lax.axis_index("section") == 0
    micro, _, length, width = inputs.shape[1:]
    z = sizes(length, width, ffn_up.shape[2], micro)
    mats, up, down, table, gains = gather_weights(
        projections[0], out_projections[0], ffn_up[0], ffn_down[0], positions[0], norm_gains[0]
    )
    w = dict(
        own=inputs[0, :, 0], cot=cotangent[:, 0], segments=segments, levels=levels, mats=mats, up=up,
        down=down, table=table, gains=gains, lent=to_section(mats[4:], 0),
    )

    kept, sent, mems = [], [], []
    for m in range(micro):

        def first_encoder():
            return tuple(encode(z, w, m))

        def first_decoder():
            (none,) = unset(z["tok"])
            return (none, *self_forward(z, w, m), *unset(z["tok32"], z["hidden"], z["hidden"]))

        mem, *rest = lax.cond(encoder, first_encoder, first_decoder)
        kept.append(rest)
        sent.append(mem)
        mems.append(to_section(mem, 0))

    outs, dmems, dh1s, feeds, prior = [], [], [], [], ()
    for m in range(micro):

        def middle_decoder():
            return tuple(cross(z, w, m, kept[m][3], mems[m], prior))

        def middle_encoder():
            return unset(
                z["tok"], z["tok"], z["tok32"], z["mats"], z["gains"], z["tokt"], z["hidden"], z["hidden"]
            )

        out, dmem, dh1, g_cross, g_gains, *feed = lax.cond(encoder, middle_encoder, middle_decoder)
        prior = (g_cross, g_gains)
        outs.append(out)
        dmems.append(to_section(dmem, 1))
        dh1s.append(dh1)
        feeds.append(feed)
    returned = to_section(g_cross[2:], 1)

    g_ins, prior = [], ()
    for m in range(micro):
        at_end = m == micro - 1

        def last_encoder():
            last = (sent, g_ins) if at_end else None
            return tuple(encode_back(z, w, m, kept[m], dmems[m], prior, last))

        def last_decoder():
            last = (outs, g_ins) if at_end else None
            less = (prior[0], prior[3]) if prior else ()
            g_in, g_mats, g_table, gain_sum, *rest = self_back(
                z, w, m, kept[m][:3], dh1s[m], less, prior[4] if prior else g_gains, last,
                feeds if at_end else (),
            )
            g_up, g_down, *whole = rest if at_end else unset(z["up"], z["down"])
            return (g_in, g_mats, g_up, g_down, g_table, gain_sum, *whole)

        g_in, *prior = lax.cond(encoder, last_encoder, last_decoder)
        g_ins.append(g_in)
    g_mats, g_up, g_down, g_table, g_gains, whole = prior

    more = jnp.where(encoder, returned, g_cross[:2])
    r_mats, r_more, r_up, r_down, r_table, r_gains = scatter_grads(
        g_mats, more, g_up, g_down, g_table, g_gains
    )
    return (
        whole[None, :, None],
        g_in[None, :, None],
        r_table[None],
        jnp.concatenate([r_mats[:3], r_more[:1]])[None],
        jnp.concatenate([r_mats[3:], r_more[1:]])[None],
        r_up[None],
        r_down[None],
        r_gains[None],
    )


def solution(mesh):
    in_specs = (
        P("section", None, "dp", None, None),
        P("section", None, "dp"),
        P("section", None, "dp", None),
        P("section", None, "dp", None),
        P("section", "dp", None),
        P("section", "dp", None),
        P("section", None, "dp"),
        P(None, "dp", None),
        P(None, None, "dp", None),
        P(None, "dp", None, None),
    )
    out_specs = (
        P("section", None, "dp", None, None),
        P("section", None, "dp", None, None),
        P("section", None, "dp"),
        P("section", None, "dp", None),
        P("section", None, "dp", None),
        P("section", "dp", None),
        P("section", "dp", None),
        P("section", None, "dp"),
    )
    return jax.shard_map(body, mesh=mesh, in_specs=in_specs, out_specs=out_specs, check_vma=False)
```

```python
from functools import partial

import jax
import jax.numpy as jnp
from jax import lax
from jax.experimental import pallas as pl
from jax.experimental.pallas import tpu as pltpu
from jax.sharding import PartitionSpec as P

BF = jnp.bfloat16
F32 = jnp.float32
DH = 64
PAIR = 2 * DH
QB = 128
WIN = 256
TB = 256
MESH = pl.DeviceIdType.MESH
VMEM_BYTES = 62 * 1024 * 1024


def nn(left, right):
    return jnp.dot(left, right, preferred_element_type=F32)


def nt(left, right):
    return lax.dot_general(left, right, (((1,), (1,)), ((), ())), preferred_element_type=F32)


def tn(left, right):
    return lax.dot_general(left, right, (((0,), (0,)), ((), ())), preferred_element_type=F32)


def norm_parts(stream):
    centred = stream - jnp.mean(stream, axis=-1, keepdims=True)
    scale = lax.rsqrt(jnp.mean(centred * centred, axis=-1, keepdims=True) + 1e-05)
    return centred * scale, scale


def norm_back(grad, unit, scale, gain):
    inner = grad * gain
    first = jnp.mean(inner, axis=-1, keepdims=True)
    second = jnp.mean(inner * unit, axis=-1, keepdims=True)
    return scale * (inner - first - unit * second), jnp.sum(grad * unit, axis=0, keepdims=True)


def block_at(index, size):
    if isinstance(index, int):
        return pl.ds(index * size, size)
    return pl.ds(pl.multiple_of(index * size, size), size)


def lane_halves(scale=1.0):
    lane = lax.broadcasted_iota(jnp.int32, (1, PAIR), 1)
    low = jnp.where(lane < DH, scale, 0.0).astype(BF)
    high = jnp.where(lane < DH, 0.0, scale).astype(BF)
    return low, high


def both_heads(block, halves):
    return jnp.concatenate([block * halves[0], block * halves[1]], axis=0)


def join_heads(stacked):
    lane = lax.broadcasted_iota(jnp.int32, (QB, PAIR), 1)
    return jnp.where(lane < DH, stacked[:QB], stacked[QB:])


def window_start(index, length):
    return pl.multiple_of(jnp.clip(index * QB - DH, 0, length - WIN), DH)


def make_codes(segments, source_level, target_level, codes_ref, cols_ref):
    segment = segments[...]
    length = segment.shape[1]
    before = pltpu.roll(segment, 1, axis=1)
    lane = lax.broadcasted_iota(jnp.int32, (1, length), 1)
    first = (lane == 0) | (segment != before)
    usable = jnp.where(first | (source_level[...] > 0), segment, -1)
    row = lax.broadcasted_iota(jnp.int32, (8, length), 0)
    codes = jnp.where(row == 0, usable, jnp.where(row == 1, segment, target_level[...]))
    codes_ref[...] = codes
    cols_ref[...] = codes.T


def mask_bias(index, start, codes_ref, cols_ref, causal):
    keys = cols_ref[pl.ds(start, WIN), :]
    queries = codes_ref[:, block_at(index, QB)]
    query_segment = queries[1:2, :]
    if causal:
        key_id = start + lax.broadcasted_iota(jnp.int32, (WIN, QB), 0)
        query_id = index * QB + lax.broadcasted_iota(jnp.int32, (WIN, QB), 1)
        allowed = (keys[:, 1:2] == query_segment) & (
            (keys[:, 2:3] < queries[2:3, :]) | (key_id == query_id)
        )
    else:
        allowed = keys[:, 0:1] == query_segment
    bias = jnp.where(allowed, 0.0, -1e30)
    return jnp.concatenate([bias, bias], axis=1)


def attend_block(index, q_ref, k_ref, v_ref, codes_ref, cols_ref, weights_ref, mixed_ref, causal):
    length, width = q_ref.shape
    start = window_start(index, length)
    rows = block_at(index, QB)
    bias = mask_bias(index, start, codes_ref, cols_ref, causal)
    halves = lane_halves(DH ** -0.5)
    for pair in range(width // PAIR):
        lanes = slice(pair * PAIR, (pair + 1) * PAIR)
        queries = both_heads(q_ref[rows, lanes], halves)
        scores = nt(k_ref[pl.ds(start, WIN), lanes], queries) + bias
        shifted = jnp.exp(scores - jnp.max(scores, axis=0, keepdims=True))
        weights = (shifted * (1.0 / jnp.sum(shifted, axis=0, keepdims=True))).astype(BF)
        weights_ref[index, pair] = weights
        out = tn(weights, v_ref[pl.ds(start, WIN), lanes])
        mixed_ref[rows, lanes] = join_heads(out).astype(BF)


def attend_back_block(
    index, q_ref, k_ref, v_ref, weights_ref, mixed_ref, dmixed_ref, dq_ref, dk_ref, dv_ref
):
    length, width = q_ref.shape
    start = window_start(index, length)
    rows = block_at(index, QB)
    window = pl.ds(start, WIN)
    plain = lane_halves()
    halves = lane_halves(DH ** -0.5)
    ones = jnp.ones((WIN, PAIR), BF)
    for pair in range(width // PAIR):
        lanes = slice(pair * PAIR, (pair + 1) * PAIR)
        queries = both_heads(q_ref[rows, lanes], halves)
        keys = k_ref[window, lanes]
        values = v_ref[window, lanes]
        weights = weights_ref[index, pair]
        dmixed = dmixed_ref[rows, lanes]
        grads = both_heads(dmixed, plain)
        inner = (dmixed.astype(F32) * mixed_ref[rows, lanes].astype(F32) * -1.0).astype(BF)
        left = jnp.concatenate([values, ones], axis=1)
        right = jnp.concatenate([grads, both_heads(inner, plain)], axis=1)
        centred = nt(left, right)
        dscores = (weights.astype(F32) * centred).astype(BF)
        dv_ref[window, lanes] += nn(weights, grads)
        dk_ref[window, lanes] += nn(dscores, queries)
        dq = tn(dscores, keys) * (DH ** -0.5)
        dq_ref[rows, lanes] = join_heads(dq).astype(BF)


def gelu_parts(value):
    cdf = 0.5 + 0.5 * lax.erf(value * (0.5 ** 0.5))
    density = jnp.exp(value * value * -0.5) * 0.3989422804014327
    return value * cdf, cdf + value * density


def feed_block(normed, up_ref, down_ref, hidden_ref, slope_ref, rows):
    total = None
    width = up_ref.shape[1]
    step = 512
    for at in range(0, width, step):
        hidden, slope = gelu_parts(nn(normed, up_ref[:, at : at + step]))
        hidden = hidden.astype(BF)
        hidden_ref[rows, at : at + step] = hidden
        slope_ref[rows, at : at + step] = slope.astype(BF)
        term = nn(hidden, down_ref[at : at + step, :])
        total = term if total is None else total + term
    return total


def feed_back_block(grad, up_ref, down_ref, slope_ref, rows):
    total = None
    width = up_ref.shape[1]
    step = 512
    for at in range(0, width, step):
        dhidden = nt(grad, down_ref[at : at + step, :])
        dup = (dhidden * slope_ref[rows, at : at + step].astype(F32)).astype(BF)
        slope_ref[rows, at : at + step] = dup
        term = nt(dup, up_ref[:, at : at + step])
        total = term if total is None else total + term
    return total


def loop(count, body):
    def step(index, carry):
        body(index)
        return carry

    lax.fori_loop(0, count, step, 0)


def put_grad(out, index, value):
    if out.prior is not None:
        value = value + out.buf[index].astype(F32)
    out.buf[index] = value.astype(BF)


def weight_grad(out, left_t_refs, right_refs, transposed):
    step = 512
    width = right_refs[0].shape[1]

    def slab(index):
        cols = block_at(index, step)
        value = None
        for left_t, right in zip(left_t_refs, right_refs):
            term = nn(left_t[...], right[:, cols])
            value = term if value is None else value + term
        if transposed:
            put_grad(out, (cols, slice(None)), value.T)
        else:
            put_grad(out, (slice(None), cols), value)

    loop(width // step, slab)


def add_gain(out, row, value):
    out.buf[row : row + 1, :] += value


class Source:
    def __init__(self, hbm, buf, sem):
        self.buf, self.copy, self.here = buf, pltpu.make_async_copy(hbm, buf, sem), False
        self.copy.start()

    def __call__(self):
        if not self.here:
            self.copy.wait()
            self.here = True
        return self.buf


class Sink:
    def __init__(self, hbm, buf, sems, first, parts, axis, prior):
        self.hbm, self.buf, self.sems, self.first = hbm, buf, sems, first
        self.parts, self.axis, self.prior = parts, axis, prior

    def copy(self, part):
        view = [slice(None)] * len(self.buf.shape)
        size = self.buf.shape[self.axis] // self.parts
        view[self.axis] = block_at(part, size)
        view = tuple(view)
        return pltpu.make_async_copy(
            self.buf.at[view], self.hbm.at[view], self.sems.at[self.first + part]
        )

    def send(self, part=0):
        self.copy(part).start()

    def wait(self):
        for part in range(self.parts):
            self.copy(part).wait()


class Ready:
    def __init__(self, buf):
        self.buf = buf

    def __call__(self):
        return self.buf


class Total:
    def __init__(self, buf, hbm, sem, first, last):
        self.buf, self.last = buf, last
        self.copy = pltpu.make_async_copy(buf, hbm, sem) if last else None
        self.prior = None if first else (lambda: None)

    def send(self):
        if self.last:
            self.copy.start()

    def wait(self):
        if self.last:
            self.copy.wait()


class Link:
    def __init__(self, outbox, inbox, send, recv, parts):
        self.buf, self.inbox, self.sems, self.parts = outbox, inbox, (send, recv), parts

    def copy(self, part):
        size = self.buf.shape[0] // self.parts
        rows = block_at(part, size)
        return pltpu.make_async_remote_copy(
            src_ref=self.buf.at[rows, :], dst_ref=self.inbox.at[rows, :],
            send_sem=self.sems[0].at[part], recv_sem=self.sems[1].at[part],
            device_id={"section": 1 - lax.axis_index("section")}, device_id_type=MESH,
        )

    def send(self, part):
        self.copy(part).start()

    def wait(self):
        for part in range(self.parts):
            self.copy(part).wait_send()

    def __call__(self):
        for part in range(self.parts):
            self.copy(part).wait_recv()
        return self.inbox


def encode_kernel(
    src, table, gains, segments, source_level, target_level, mats, up, down,
    mem, qkv, weights, mixed, x1, x2, hidden, slope, codes, cols,
):
    length = src.buf.shape[0]
    make_codes(segments(), source_level(), target_level(), codes, cols)
    src, table, gains, mats = src(), table(), gains(), mats()

    def project(index):
        rows = block_at(index, TB)
        unit, _ = norm_parts(src[rows, :].astype(F32) + table[rows, :].astype(F32))
        normed = (unit * gains[0:1, :]).astype(BF)
        for which in range(3):
            qkv.buf[which, rows, :] = nn(normed, mats[which]).astype(BF)
        qkv.send(index)

    loop(length // TB, project)
    up, down = up(), down()

    def rest(index):
        for part in range(TB // QB):
            attend_block(
                index * (TB // QB) + part,
                qkv.buf.at[0], qkv.buf.at[1], qkv.buf.at[2], codes, cols, weights.buf, mixed.buf, False,
            )
        weights.send(index)
        mixed.send(index)
        rows = block_at(index, TB)
        stream = src[rows, :].astype(F32) + table[rows, :].astype(F32)
        stream = stream + nn(mixed.buf[rows, :], mats[3])
        x1.buf[rows, :] = stream
        x1.send(index)
        unit, _ = norm_parts(stream)
        normed = (unit * gains[1:2, :]).astype(BF)
        stream = stream + feed_block(normed, up, down, hidden.buf, slope.buf, rows)
        x2.buf[rows, :] = stream
        unit, _ = norm_parts(stream)
        mem.buf[rows, :] = (unit * gains[2:3, :]).astype(BF)
        for item in (mem, x2, hidden, slope):
            item.send(index)

    loop(length // TB, rest)


def encode_back_kernel(
    x2, dmem, gains, slope, down, up, x1, mats, hidden, mixed, qkv, weights, src, table,
    g_in, g_mats, g_up, g_down, g_table, g_gains,
    dy, dy_t, a_t, dx, dmixed, dq, dk, dv,
):
    length = src.buf.shape[0]
    if g_gains.prior is None:
        g_gains.buf[...] = jnp.zeros_like(g_gains.buf)
    else:
        g_gains.prior()
    dk[...] = jnp.zeros_like(dk)
    dv[...] = jnp.zeros_like(dv)
    x2, dmem, gains, slope, down, up, x1, mats = (
        x2(), dmem(), gains(), slope(), down(), up(), x1(), mats()
    )

    def feed_step(index):
        rows = block_at(index, TB)
        unit, scale = norm_parts(x2[rows, :])
        grad, d_gain = norm_back(dmem[rows, :].astype(F32), unit, scale, gains[2:3, :])
        add_gain(g_gains, 2, d_gain)
        low = grad.astype(BF)
        dy_t[:, rows] = low.T
        dnormed = feed_back_block(low, up, down, slope, rows)
        unit, scale = norm_parts(x1[rows, :])
        a_t[:, rows] = (unit * gains[1:2, :]).astype(BF).T
        back, d_gain = norm_back(dnormed, unit, scale, gains[1:2, :])
        add_gain(g_gains, 1, d_gain)
        grad = grad + back
        dx[rows, :] = grad
        low = grad.astype(BF)
        dy[rows, :] = low
        dmixed[rows, :] = nt(low, mats[3]).astype(BF)

    loop(length // TB, feed_step)
    for item in (g_up, g_down, g_mats, g_table):
        if item.prior is not None:
            item.prior()
    weight_grad(g_up, [a_t], [slope], False)
    g_up.send()
    weight_grad(g_down, [dy_t], [hidden()], True)
    g_down.send()
    mixed = mixed()
    put_grad(g_mats, 3, tn(mixed[...], dy[...]))
    qkv, weights = qkv(), weights()

    def attend_step(index):
        attend_back_block(
            index, qkv.at[0], qkv.at[1], qkv.at[2], weights, mixed, dmixed, dq, dk, dv
        )

    loop(length // QB, attend_step)
    src, table = src(), table()

    def project_step(index):
        rows = block_at(index, TB)
        unit, scale = norm_parts(src[rows, :].astype(F32) + table[rows, :].astype(F32))
        a_t[:, rows] = (unit * gains[0:1, :]).astype(BF).T
        dnormed = nt(dq[rows, :], mats[0])
        dnormed += nt(dk[rows, :].astype(BF), mats[1])
        dnormed += nt(dv[rows, :].astype(BF), mats[2])
        back, d_gain = norm_back(dnormed, unit, scale, gains[0:1, :])
        add_gain(g_gains, 0, d_gain)
        grad = dx[rows, :] + back
        g_in.buf[rows, :] = grad
        g_in.send(index)
        put_grad(g_table, (slice(None), rows), grad.T)

    loop(length // TB, project_step)
    g_table.send()
    g_gains.send()
    put_grad(g_mats, 0, nn(a_t[...], dq[...]))
    put_grad(g_mats, 1, nn(a_t[...], dk[...].astype(BF)))
    put_grad(g_mats, 2, nn(a_t[...], dv[...].astype(BF)))
    g_mats.send()


def self_kernel(
    tgt, table, gains, segments, source_level, target_level, mats, qkv, weights, mixed, h1, codes, cols
):
    length = tgt.buf.shape[0]
    make_codes(segments(), source_level(), target_level(), codes, cols)
    tgt, table, gains, mats = tgt(), table(), gains(), mats()

    def project(index):
        rows = block_at(index, TB)
        stream = table[rows, :].astype(F32)
        unit, _ = norm_parts(stream)
        qkv.buf[0, rows, :] = nn((unit * gains[0:1, :]).astype(BF), mats[0]).astype(BF)
        unit, _ = norm_parts(tgt[rows, :].astype(F32) + stream)
        normed = (unit * gains[0:1, :]).astype(BF)
        for which in (1, 2):
            qkv.buf[which, rows, :] = nn(normed, mats[which]).astype(BF)
        qkv.send(index)

    loop(length // TB, project)

    def rest(index):
        for part in range(TB // QB):
            attend_block(
                index * (TB // QB) + part,
                qkv.buf.at[0], qkv.buf.at[1], qkv.buf.at[2], codes, cols, weights.buf, mixed.buf, True,
            )
        rows = block_at(index, TB)
        h1.buf[rows, :] = table[rows, :].astype(F32) + nn(mixed.buf[rows, :], mats[3])
        for item in (weights, mixed, h1):
            item.send(index)

    loop(length // TB, rest)


def self_back_kernel(
    dh1, mats, mixed, qkv, weights, tgt, table, gains,
    g_in, g_mats, g_table, g_gains,
    dy, a_t, b_t, dmixed, dq, dk, dv,
):
    length = tgt.buf.shape[0]
    g_gains.prior()
    dk[...] = jnp.zeros_like(dk)
    dv[...] = jnp.zeros_like(dv)
    dh1, mats, mixed = dh1(), mats(), mixed()

    def out_step(index):
        rows = block_at(index, TB)
        low = dh1[rows, :].astype(BF)
        dy[rows, :] = low
        dmixed[rows, :] = nt(low, mats[3]).astype(BF)

    loop(length // TB, out_step)
    for item in (g_mats, g_table):
        if item.prior is not None:
            item.prior()
    put_grad(g_mats, 3, tn(mixed[...], dy[...]))
    qkv, weights = qkv(), weights()

    def attend_step(index):
        attend_back_block(
            index, qkv.at[0], qkv.at[1], qkv.at[2], weights, mixed, dmixed, dq, dk, dv
        )

    loop(length // QB, attend_step)
    tgt, table, gains = tgt(), table(), gains()

    def project_step(index):
        rows = block_at(index, TB)
        stream = table[rows, :].astype(F32)
        unit, scale = norm_parts(stream)
        a_t[:, rows] = (unit * gains[0:1, :]).astype(BF).T
        back, d_gain = norm_back(nt(dq[rows, :], mats[0]), unit, scale, gains[0:1, :])
        dtable = dh1[rows, :] + back
        unit, scale = norm_parts(tgt[rows, :].astype(F32) + stream)
        b_t[:, rows] = (unit * gains[0:1, :]).astype(BF).T
        dnormed = nt(dk[rows, :].astype(BF), mats[1])
        dnormed += nt(dv[rows, :].astype(BF), mats[2])
        back, d_gain_too = norm_back(dnormed, unit, scale, gains[0:1, :])
        add_gain(g_gains, 0, d_gain + d_gain_too)
        g_in.buf[rows, :] = back
        g_in.send(index)
        put_grad(g_table, (slice(None), rows), (dtable + back).T)

    loop(length // TB, project_step)
    g_table.send()
    g_gains.send()
    put_grad(g_mats, 0, nn(a_t[...], dq[...]))
    put_grad(g_mats, 1, nn(b_t[...], dk[...].astype(BF)))
    put_grad(g_mats, 2, nn(b_t[...], dv[...].astype(BF)))
    g_mats.send()


def feed_grads_kernel(a_t, dup, cot, hidden, g_up, g_down, cot_t):
    cot_t[...] = cot()[...].T
    weight_grad(g_up, [a_t()], [dup()], False)
    g_up.send()
    weight_grad(g_down, [cot_t], [hidden()], True)
    g_down.send()


def cross_kernel(
    h1, gains, segments, source_level, target_level, mats, mem, lent, up, down, cot,
    out, dmem, dh1, g_mats, g_gains, a_t, dup, hidden,
    codes, cols, qkv, weights, mixed, h2, dy, b_t, dmixed, dq, dk, dv,
):
    length = h1.buf.shape[0]
    make_codes(segments(), source_level(), target_level(), codes, cols)
    if g_gains.prior is None:
        g_gains.buf[...] = jnp.zeros_like(g_gains.buf)
    else:
        g_gains.prior()
    dk[...] = jnp.zeros_like(dk)
    dv[...] = jnp.zeros_like(dv)
    h1, gains, mats, mem, lent = h1(), gains(), mats(), mem(), lent()

    def project(index):
        rows = block_at(index, TB)
        unit, _ = norm_parts(h1[rows, :])
        qkv[0, rows, :] = nn((unit * gains[1:2, :]).astype(BF), mats[0]).astype(BF)
        qkv[1, rows, :] = nn(mem[rows, :], lent[0]).astype(BF)
        qkv[2, rows, :] = nn(mem[rows, :], lent[1]).astype(BF)

    loop(length // TB, project)
    up, down, cot = up(), down(), cot()

    def middle(index):
        for part in range(TB // QB):
            attend_block(
                index * (TB // QB) + part,
                qkv.at[0], qkv.at[1], qkv.at[2], codes, cols, weights, mixed, False,
            )
        rows = block_at(index, TB)
        stream = h1[rows, :] + nn(mixed[rows, :], mats[1])
        unit, scale = norm_parts(stream)
        normed = (unit * gains[2:3, :]).astype(BF)
        a_t.buf[:, rows] = normed.T
        fed = feed_block(normed, up, down, hidden.buf, dup.buf, rows)
        out.buf[rows, :] = (stream + fed).astype(BF)
        low = cot[rows, :]
        dnormed = feed_back_block(low, up, down, dup.buf, rows)
        back, d_gain = norm_back(dnormed, unit, scale, gains[2:3, :])
        add_gain(g_gains, 2, d_gain)
        grad = low.astype(F32) + back
        h2[rows, :] = grad
        low = grad.astype(BF)
        dy[rows, :] = low
        dmixed[rows, :] = nt(low, mats[1]).astype(BF)
        for item in (out, hidden, dup):
            item.send(index)

    loop(length // TB, middle)
    a_t.send()

    def attend_step(index):
        attend_back_block(
            index, qkv.at[0], qkv.at[1], qkv.at[2], weights, mixed, dmixed, dq, dk, dv
        )

    loop(length // QB, attend_step)
    if g_mats.prior is not None:
        g_mats.prior()

    def project_step(index):
        rows = block_at(index, TB)
        dkeys = dk[rows, :].astype(BF)
        dvalues = dv[rows, :].astype(BF)
        dmem.buf[rows, :] = (nt(dkeys, lent[0]) + nt(dvalues, lent[1])).astype(BF)
        dmem.send(index)
        unit, scale = norm_parts(h1[rows, :])
        b_t[:, rows] = (unit * gains[1:2, :]).astype(BF).T
        back, d_gain = norm_back(nt(dq[rows, :], mats[0]), unit, scale, gains[1:2, :])
        add_gain(g_gains, 1, d_gain)
        dh1.buf[rows, :] = h2[rows, :] + back
        dh1.send(index)

    loop(length // TB, project_step)
    g_gains.send()
    put_grad(g_mats, 0, nn(b_t[...], dq[...]))
    put_grad(g_mats, 1, tn(mixed[...], dy[...]))
    put_grad(g_mats, 2, tn(mem[...], dk[...].astype(BF)))
    put_grad(g_mats, 3, tn(mem[...], dv[...].astype(BF)))
    g_mats.send()


def shape(dims, kind):
    return jax.ShapeDtypeStruct(dims, kind)


def sizes(length, width, ff, micro):
    blocks = length // QB
    pairs = width // PAIR
    return dict(
        tok=shape((length, width), BF),
        tok32=shape((length, width), F32),
        outputs=shape((micro, length, width), BF),
        g_in=shape((micro, length, width), F32),
        qkv=shape((3, length, width), BF),
        weights=shape((blocks, pairs, WIN, 2 * QB), BF),
        hidden=shape((length, ff), BF),
        tokt=shape((width, length), BF),
        mats=shape((4, width, width), BF),
        up=shape((width, ff), BF),
        down=shape((ff, width), BF),
        gains=shape((8, width), F32),
        pair=shape((2, width, width), BF),
        row=shape((1, length), jnp.int32),
        codes=shape((8, length), jnp.int32),
        cols=shape((length, 8), jnp.int32),
    )


def stage_pool(z):
    return [
        ("row", 3), ("tok", 6), ("tok32", 6), ("tokt", 2), ("qkv", 1), ("weights", 1), ("hidden", 2),
    ]


KEPT = ("qkv", "weights", "tok", "tok32", "tok32", "hidden", "hidden", "tokt")
PERSISTENT = (
    "tok", "gains", "mats", "up", "down", "pair", "pair", "mats", "mats", "up", "down", "tokt", "gains",
    "codes", "cols", "outputs", "outputs",
)


def section_kernel(z, *refs):
    refs = list(refs)
    take = lambda count: [refs.pop(0) for _ in range(count)]
    own, cot, segments, levels, mats, up, down, table, gains = take(9)
    whole, g_in, o_mats, o_more, o_up, o_down, o_table, o_gains = take(8)
    micro, length = own.shape[:2]
    parts = length // TB
    kept = [take(len(KEPT)) for _ in range(micro)]
    (
        v_table, v_gains, v_mats, v_up, v_down, v_cross, v_lent, s_mats, s_cross, s_up, s_down, s_table,
        s_gains, codes, cols, inbox, outbox,
    ) = take(len(PERSISTENT))
    pool = {name: take(count) for name, count in stage_pool(z)}
    local, ysend, yrecv, lsend, lrecv, bsend, brecv = refs
    section, core = lax.axis_index("section"), lax.axis_index("dp") % 2
    partner, sibling = {"section": 1 - section}, {"dp": lax.axis_index("dp") + 1 - 2 * core}

    barrier = pltpu.get_barrier_semaphore()
    for other in (partner, sibling):
        pl.semaphore_signal(barrier, inc=1, device_id=other, device_id_type=MESH)
    pl.semaphore_wait(barrier, 2)

    count = [0]

    def sems(number):
        count[0] += number
        return count[0] - number

    def load(hbm, buf):
        return Source(hbm, buf, local.at[sems(1)])

    def store(hbm, buf, axis=0, split=True):
        number = parts if split else 1
        return Sink(hbm, buf, local, sems(number), number, axis, None)

    def box(m):
        return Link(outbox.at[m], inbox.at[m], ysend.at[m], yrecv.at[m], parts)

    def totals(m, *names):
        all_of = dict(
            mats=(s_mats, o_mats), up=(s_up, o_up), down=(s_down, o_down), table=(s_table, o_table),
            gains=(s_gains, o_gains),
        )
        return [Total(*all_of[name], local.at[sems(1)], m == 0, m == micro - 1) for name in names]

    def code_loads(m):
        hbm = (segments.at[m], levels.at[0, m], levels.at[1, m])
        return [load(ref, buf) for ref, buf in zip(hbm, pool["row"])]

    def lend(hop):
        if hop == 0:
            src, where = mats.at[4 + core], partner
        else:
            src, where = v_lent.at[core], sibling
        return pltpu.make_async_remote_copy(
            src_ref=src, dst_ref=v_lent.at[core], send_sem=lsend.at[hop], recv_sem=lrecv.at[hop],
            device_id=where, device_id_type=MESH,
        )

    def lent_by_sibling():
        return pltpu.make_async_remote_copy(
            src_ref=v_lent.at[1 - core], dst_ref=v_lent.at[1 - core], send_sem=lsend.at[1],
            recv_sem=lrecv.at[1], device_id=sibling, device_id_type=MESH,
        )

    give_back = pltpu.make_async_remote_copy(
        src_ref=s_cross.at[2:4], dst_ref=o_more, send_sem=bsend.at[0], recv_sem=brecv.at[0],
        device_id=partner, device_id_type=MESH,
    )

    @pl.when(section == 0)
    def _():
        count[0] = 0
        lend(0).start()
        first_table, first_gains = load(table, v_table), load(gains, v_gains)
        first_mats = load(mats.at[0:4], v_mats)
        first_up, first_down = load(up, v_up), load(down, v_down)
        base = count[0]
        for m in range(micro):
            count[0] = base
            k_qkv, k_weights, k_mixed, k_x1, k_x2, k_hidden, k_slope, _ = kept[m]
            src, mixed = pool["tok"][:2]
            x1, x2 = pool["tok32"][:2]
            hidden, slope = pool["hidden"]
            sinks = [
                store(k_qkv, pool["qkv"][0], axis=1), store(k_weights, pool["weights"][0]),
                store(k_mixed, mixed), store(k_x1, x1), store(k_x2, x2), store(k_hidden, hidden),
                store(k_slope, slope),
            ]
            encode_kernel(
                load(own.at[m], src), first_table, first_gains, *code_loads(m), first_mats, first_up,
                first_down, box(m), *sinks, codes, cols,
            )
            mem = pltpu.make_async_copy(outbox.at[m], whole.at[m], local.at[sems(1)])
            mem.start()
            for item in sinks:
                item.wait()
            mem.wait()
        for m in range(micro):
            count[0] = base
            k_qkv, k_weights, k_mixed, k_x1, k_x2, k_hidden, k_slope, _ = kept[m]
            src, mixed, dy, dmixed, dq = pool["tok"][:5]
            x1, x2, grad, dx, dk, dv = pool["tok32"][:6]
            hidden, slope = pool["hidden"]
            dy_t, a_t = pool["tokt"]
            x2, slope = load(k_x2, x2), load(k_slope, slope)
            x1, hidden = load(k_x1, x1), load(k_hidden, hidden)
            mixed, qkv = load(k_mixed, mixed), load(k_qkv, pool["qkv"][0])
            weights, src = load(k_weights, pool["weights"][0]), load(own.at[m], src)
            sinks = [store(g_in.at[m], grad)] + totals(m, "mats", "up", "down", "table", "gains")
            encode_back_kernel(
                x2, box(m), first_gains, slope, first_down, first_up, x1, first_mats, hidden, mixed, qkv,
                weights, src, first_table, *sinks, dy, dy_t, a_t, dx, dmixed, dq, dk, dv,
            )
            for item in sinks:
                item.wait()
        lend(0).wait_send()
        give_back.wait_recv()

    @pl.when(section == 1)
    def _():
        count[0] = 0
        first_table, first_gains = load(table, v_table), load(gains, v_gains)
        first_mats, first_cross = load(mats.at[0:4], v_mats), load(mats.at[4:6], v_cross)
        first_up, first_down = load(up, v_up), load(down, v_down)
        base = count[0]
        for m in range(micro):
            count[0] = base
            k_qkv, k_weights, k_mixed, k_h1 = kept[m][:4]
            tgt, mixed = pool["tok"][:2]
            sinks = [
                store(k_qkv, pool["qkv"][0], axis=1), store(k_weights, pool["weights"][0]),
                store(k_mixed, mixed), store(k_h1, pool["tok32"][0]),
            ]
            self_kernel(
                load(own.at[m], tgt), first_table, first_gains, *code_loads(m), first_mats, *sinks, codes,
                cols,
            )
            for item in sinks:
                item.wait()
            if m == 0:
                lend(0).wait_recv()
                lend(1).start()
        lent_by_sibling().wait_recv()
        for m in range(micro):
            count[0] = base
            k_h1, k_dh1, k_hidden, k_dup, k_a = kept[m][3:8]
            v_cot, out, mixed, dy, dmixed, dq = pool["tok"]
            h1, dh1, h2, dk, dv = pool["tok32"][:5]
            hidden, dup = pool["hidden"]
            a_t, b_t = pool["tokt"]
            gain_sum = Total(s_gains, o_gains, local.at[sems(1)], m == 0, False)
            cross_sum = Total(s_cross.at[0:4], o_mats, local.at[sems(1)], m == 0, False)
            sinks = [store(whole.at[m], out), store(k_dh1, dh1)]
            feeds = [store(k_a, a_t, split=False), store(k_dup, dup), store(k_hidden, hidden)]
            cross_kernel(
                load(k_h1, h1), first_gains, *code_loads(m), first_cross, box(m), Ready(v_lent), first_up,
                first_down, load(cot.at[m], v_cot), sinks[0], box(m), sinks[1], cross_sum, gain_sum,
                *feeds, codes, cols, pool["qkv"][0], pool["weights"][0], mixed, h2, dy, b_t, dmixed, dq,
                dk, dv,
            )
            for item in sinks + feeds:
                item.wait()
        give_back.start()
        keep_own = pltpu.make_async_copy(s_cross.at[0:2], o_more, local.at[sems(1)])
        keep_own.start()
        base = count[0]
        for m in range(micro):
            count[0] = base
            k_dh1, k_hidden, k_dup, k_a = kept[m][4:8]
            sums = totals(m, "up", "down")
            feed_grads_kernel(
                load(k_a, pool["tokt"][0]), load(k_dup, pool["hidden"][1]), load(cot.at[m], pool["tok"][0]),
                load(k_hidden, pool["hidden"][0]), *sums, pool["tokt"][1],
            )
            for item in sums:
                item.wait()
        for m in range(micro):
            count[0] = base
            k_qkv, k_weights, k_mixed, _, k_dh1 = kept[m][:5]
            tgt, mixed, dy, dmixed, dq = pool["tok"][:5]
            dh1, grad, dk, dv = pool["tok32"][:4]
            a_t, b_t = pool["tokt"]
            dh1, mixed = load(k_dh1, dh1), load(k_mixed, mixed)
            qkv, weights = load(k_qkv, pool["qkv"][0]), load(k_weights, pool["weights"][0])
            sinks = [store(g_in.at[m], grad)] + totals(m, "mats", "table", "gains")
            sinks[-1].prior = lambda: None
            self_back_kernel(
                dh1, first_mats, mixed, qkv, weights, load(own.at[m], tgt), first_table, first_gains,
                *sinks, dy, a_t, b_t, dmixed, dq, dk, dv,
            )
            for item in sinks:
                item.wait()
        keep_own.wait()
        lend(1).wait_send()
        give_back.wait_send()

    for m in range(micro):
        box(m).wait()


def run_sections(z, own, cot, segments, levels, mats, up, down, table, gains):
    micro = own.shape[0]
    args = [own, cot, segments, levels, mats, up, down, table, gains]
    outs = [
        z["outputs"], z["g_in"], z["mats"], z["pair"], z["up"], z["down"], z["tokt"], z["gains"],
    ] + [z[name] for _ in range(micro) for name in KEPT]
    scratch = [z[name] for name in PERSISTENT]
    scratch += [z[name] for name, number in stage_pool(z) for _ in range(number)]
    parts = own.shape[1] // TB
    dma = pltpu.SemaphoreType.DMA
    anywhere = pl.BlockSpec(memory_space=pl.ANY)
    outs = pl.pallas_call(
        partial(section_kernel, z),
        out_shape=outs,
        in_specs=[anywhere] * len(args),
        out_specs=[anywhere] * len(outs),
        scratch_shapes=[pltpu.VMEM(s.shape, s.dtype) for s in scratch]
        + [
            dma((64,)), dma((micro, parts)), dma((micro, parts)), dma((2,)), dma((2,)), dma((1,)),
            dma((1,)),
        ],
        compiler_params=pltpu.CompilerParams(
            collective_id=2, has_side_effects=True, vmem_limit_bytes=VMEM_BYTES
        ),
        name="sections",
    )(*args)
    return outs[:8]


LINE = 4
TABLE_ROWS = 48


def place():
    me = lax.axis_index("dp")
    return me // 4, (me // 2) % 2, me % 2


def rank_of(z, x, core):
    return z * 4 + x * 2 + core


def when(cond, do):
    if cond is None:
        do()
    else:
        pl.when(cond)(do)


def can_send(way, z):
    return (z > 0) if way else (z < LINE - 1)


def greet(z, x, core):
    barrier = pltpu.get_barrier_semaphore()

    def signal(rank):
        pl.semaphore_signal(barrier, inc=1, device_id={"dp": rank}, device_id_type=MESH)

    signal(rank_of(z, 1 - x, core))
    signal(rank_of(z, x, 1 - core))
    for way in range(2):
        pl.when(can_send(way, z))(lambda: signal(rank_of(z + 1 - 2 * way, x, core)))
    pl.semaphore_wait(barrier, 2 + jnp.minimum(z, 1) + jnp.minimum(LINE - 1 - z, 1))


def remote(src, dst, send, recv, rank):
    return pltpu.make_async_remote_copy(
        src_ref=src, dst_ref=dst, send_sem=send, recv_sem=recv, device_id={"dp": rank},
        device_id_type=MESH,
    )


def at_rank(ref, per, rank):
    axis = len(ref.shape) - 2
    view = [slice(None)] * len(ref.shape)
    view[axis] = pl.ds(pl.multiple_of(rank * per, 16), per)
    return ref.at[tuple(view)]


SLOTS = [(0, 0, 0)] + [(1 + way * 3 + step, way, step + 1) for step in range(3) for way in range(2)]


def gather_kernel(
    proj, outp, up, down, pos, gain, o_mats, o_up, o_down, o_table, o_gain,
    packed, s_mats, s_up, s_down, s_table, zsend, zrecv, xsend, xrecv, csend, crecv, here,
):
    z, x, core = place()
    per = pos.shape[0]
    count = gain.shape[0]
    s_table[:per, :] = pos[...].astype(BF)
    s_table[per:, :] = jnp.zeros((TABLE_ROWS - per, pos.shape[1]), BF)
    s_table[per : per + count, :per] = gain[...].reshape(count, per).astype(BF)
    for to, (ref, index) in enumerate(
        ((proj, 0), (proj, 1), (proj, 2), (outp, 0), (proj, 3), (outp, 1))
    ):
        s_mats[to] = ref[index].astype(BF)
    s_up[...] = up[...].astype(BF)
    s_down[...] = down[...].astype(BF)
    greet(z, x, core)

    outs = (packed, o_mats, o_up, o_down)
    mine = (s_table, s_mats, s_up, s_down)
    pers = [ref.shape[-2] for ref in mine]
    along_first = (1, 2, 3)
    across, sibling = rank_of(z, 1 - x, core), rank_of(z, x, 1 - core)

    def origin(way, back, other):
        return rank_of(z - back * (1 - 2 * way), 1 - x if other else x, core)

    def block(kind, way, back, other):
        return at_rank(outs[kind], pers[kind], origin(way, back, other))

    def begin_block(kind, way, back, other):
        return mine[kind] if back == 0 and not other else block(kind, way, back, other)

    def along(kind, other, way, hop):
        return remote(
            begin_block(kind, way, hop, other), block(kind, way, hop, other),
            zsend.at[kind, other, way, hop], zrecv.at[kind, other, way, hop],
            rank_of(z + 1 - 2 * way, x, core),
        )

    def over(kind, slot):
        at, way, back = SLOTS[slot]
        return remote(
            begin_block(kind, way, back, 0), block(kind, way, back, 0), xsend.at[kind, at],
            xrecv.at[kind, at], across,
        )

    def beside(kind, slot, other):
        at, way, back = SLOTS[slot]
        at += other * len(SLOTS)
        return remote(
            begin_block(kind, way, back, other), block(kind, way, back, other), csend.at[kind, at],
            crecv.at[kind, at], sibling,
        )

    def exists(way, back):
        if back == 0:
            return None
        return (z <= LINE - 1 - back) if way else (z >= back)

    def begin_along(kind, other):
        for way in range(2):
            pl.when(can_send(way, z))(lambda: along(kind, other, way, 0).start())

    def pass_on(kind, other):
        for slot in range(1, len(SLOTS)):
            _, way, back = SLOTS[slot]

            def one():
                along(kind, other, way, back - 1).wait_recv()
                if back < LINE - 1:
                    pl.when(can_send(way, z))(lambda: along(kind, other, way, back).start())
                if kind in along_first:
                    over(kind, slot).start()
                beside(kind, slot, other).start()

            when(exists(way, back), one)

    def share(kind):
        for slot in range(len(SLOTS)):
            _, way, back = SLOTS[slot]

            def one():
                over(kind, slot).wait_recv()
                beside(kind, slot, 1).start()

            when(exists(way, back), one)

    def finish(kind):
        local[kind].wait()
        for other in range(1 if kind in along_first else 2):
            for way in range(2):
                for hop in range(LINE - 1):
                    sent = can_send(way, z)
                    if hop:
                        sent = sent & exists(way, hop)
                    pl.when(sent)(lambda: along(kind, other, way, hop).wait_send())
        for slot in range(len(SLOTS)):
            _, way, back = SLOTS[slot]

            def one():
                if kind in along_first or slot == 0:
                    over(kind, slot).wait_send()
                for other in range(2):
                    copy = beside(kind, slot, other)
                    copy.wait_send()
                    copy.wait_recv()

            when(exists(way, back), one)

    local = [
        pltpu.make_async_copy(mine[kind], block(kind, 0, 0, 0), here.at[kind])
        for kind in range(len(outs))
    ]
    over(0, 0).start()
    begin_along(1, 0)
    over(1, 0).start()
    begin_along(0, 0)
    begin_along(2, 0)
    over(2, 0).start()
    for kind in range(len(outs)):
        beside(kind, 0, 0).start()
        local[kind].start()
    over(0, 0).wait_recv()
    begin_along(0, 1)
    beside(0, 0, 1).start()
    pass_on(1, 0)
    begin_along(3, 0)
    over(3, 0).start()
    pass_on(0, 0)
    pass_on(0, 1)
    pass_on(2, 0)
    share(1)
    finish(0)
    o_gain[...] = jnp.zeros_like(o_gain)
    ranks = packed.shape[0] // TABLE_ROWS
    group = 4
    for first in range(0, ranks, group):
        blocks = [packed[rank * TABLE_ROWS : (rank + 1) * TABLE_ROWS, :] for rank in range(first, first + group)]
        lanes = slice(first * per, (first + group) * per)
        o_table[:, lanes] = jnp.concatenate([one[:per] for one in blocks], axis=0).T
        o_gain[:count, lanes] = jnp.concatenate(
            [one[per : per + count, :per] for one in blocks], axis=1
        ).astype(F32)
    pass_on(3, 0)
    share(2)
    share(3)
    for kind in along_first:
        finish(kind)


def line_fits(ranks, per, length):
    return ranks == 4 * LINE and per * 4 == 128 and length % 128 == 0


def gather_weights(proj, outp, up, down, pos, gain):
    ranks = lax.axis_size("dp")
    count, per, width = proj.shape[0] + outp.shape[0], proj.shape[1], proj.shape[2]
    length = pos.shape[1]
    if not line_fits(ranks, per, length):
        order = [proj[0], proj[1], proj[2], outp[0], proj[3], outp[1]]
        every = lambda value, axis: lax.all_gather(value.astype(BF), "dp", axis=axis, tiled=True)
        gains = every(gain[:, 0], 1).astype(F32)
        return (
            every(jnp.stack(order), 1), every(up, 0), every(down, 0), every(pos, 0).T,
            jnp.concatenate([gains, jnp.zeros((8 - gain.shape[0], width), F32)]),
        )
    shards = [
        shape((TABLE_ROWS * ranks, length), BF), shape((count, per, width), BF), shape(up.shape, BF),
        shape(down.shape, BF), shape((TABLE_ROWS, length), BF),
    ]
    outs = [
        shape((count, width, width), BF), shape((width, up.shape[1]), BF),
        shape((down.shape[0] * ranks, width), BF), shape((length, width), BF), shape((8, width), F32),
    ]
    dma = pltpu.SemaphoreType.DMA
    slots = len(SLOTS)
    hops = (4, 2, 2, LINE - 1)
    in_vmem, anywhere = pl.BlockSpec(memory_space=pltpu.VMEM), pl.BlockSpec(memory_space=pl.ANY)
    return pl.pallas_call(
        gather_kernel,
        out_shape=outs,
        in_specs=[in_vmem] * 6,
        out_specs=[anywhere] * 3 + [in_vmem] * 2,
        scratch_shapes=[pltpu.VMEM(s.shape, s.dtype) for s in shards]
        + [
            dma(hops), dma(hops), dma((4, slots)), dma((4, slots)), dma((4, 2 * slots)),
            dma((4, 2 * slots)), dma((4,)),
        ],
        compiler_params=pltpu.CompilerParams(
            collective_id=0, has_side_effects=True, vmem_limit_bytes=VMEM_BYTES
        ),
        name="gather",
    )(proj, outp, up, down, pos, gain)


KINDS = 5
FAR_FIRST = (3, 0, 2, 1)


def scatter_kernel(*refs):
    refs = list(refs)
    take = lambda count: [refs.pop(0) for _ in range(count)]
    g_mats, g_more, g_up, g_down, g_table, g_gain = take(6)
    o_proj, o_out, o_up, o_down, o_table, o_gain = take(6)
    grads, cbuf, xbuf, zbuf = take(KINDS), take(KINDS), take(KINDS), take(KINDS)
    here, csend, crecv, xsend, xrecv, zsend, zrecv = refs
    z, x, core = place()
    over_first, table = (0, 1, 2, 3), 4
    pers = [ref.shape[-2] for ref in cbuf]
    across, sibling = rank_of(z, 1 - x, core), rank_of(z, x, 1 - core)
    ranks = 4 * LINE
    per = o_table.shape[0]
    count = o_gain.shape[0]

    loads = [
        pltpu.make_async_copy(ref, grads[kind], here.at[kind])
        for kind, ref in enumerate((g_mats, g_more, g_up, g_down))
    ]
    loads += [
        pltpu.make_async_copy(
            g_table.at[rank * per : (rank + 1) * per, :],
            grads[table].at[rank * TABLE_ROWS : rank * TABLE_ROWS + per, :],
            here.at[table + rank],
        )
        for rank in range(ranks)
    ]
    for copy in loads:
        copy.start()
    for rank in range(ranks):
        first = rank * TABLE_ROWS + per
        part = jnp.concatenate(
            [g_gain[:, rank * per : (rank + 1) * per], jnp.zeros((8, per), F32)], axis=0
        )
        grads[table][first : first + 16, :] = jnp.zeros((16, grads[table].shape[1]), BF)
        grads[table][first : first + 16, :per] = part.astype(BF)
    greet(z, x, core)

    def grad(kind, dest, line, its_core):
        return at_rank(grads[kind], pers[kind], rank_of(dest, line, its_core))

    def line_of(part):
        return x if part else 1 - x

    def beside(kind, dest, part):
        return remote(
            grad(kind, dest, line_of(part), 1 - core), cbuf[kind].at[dest, part],
            csend.at[kind, dest, part], crecv.at[kind, dest, part], sibling,
        )

    def over(kind, dest):
        return remote(
            cbuf[kind].at[dest, 0], xbuf[kind].at[dest], xsend.at[kind, dest], xrecv.at[kind, dest], across
        )

    def along(kind, dest, part, way):
        return remote(
            cbuf[kind].at[dest, part], zbuf[kind].at[dest, part, way], zsend.at[kind, dest, part, way],
            zrecv.at[kind, dest, part, way], rank_of(z + 1 - 2 * way, x, core),
        )

    def total(*terms):
        value = terms[0][...].astype(F32)
        for term in terms[1:]:
            value = value + term[...].astype(F32)
        return value

    def add(into, *terms):
        into[...] = total(into, *terms).astype(BF)

    def from_sibling(kind, dest, part):
        beside(kind, dest, part).wait_recv()
        add(cbuf[kind].at[dest, part], grad(kind, dest, line_of(part), core))

    def before(dest, way):
        return (z > dest) if way else (z < dest)

    def chain(kind, dest, part):
        for way in range(2):

            def one():
                def came():
                    along(kind, dest, part, way).wait_recv()
                    add(cbuf[kind].at[dest, part], zbuf[kind].at[dest, part, way])

                pl.when(can_send(1 - way, z))(came)
                along(kind, dest, part, way).start()

            pl.when(before(dest, way))(one)

    def line_total(kind, dest, part):
        terms = [cbuf[kind].at[dest, part]]
        for way in range(2):
            if 0 <= dest - 1 + 2 * way < LINE:
                along(kind, dest, part, way).wait_recv()
                terms.append(zbuf[kind].at[dest, part, way])
        return total(*terms)

    for copy in loads:
        copy.wait()
    for kind in over_first:
        for dest in FAR_FIRST:
            beside(kind, dest, 0).start()
    for dest in FAR_FIRST:
        for part in range(2):
            beside(table, dest, part).start()
    for kind in over_first:
        for dest in FAR_FIRST:
            beside(kind, dest, 1).start()

    for kind in over_first:
        for dest in FAR_FIRST:
            from_sibling(kind, dest, 0)
            over(kind, dest).start()
    for dest in FAR_FIRST:
        for part in range(2):
            from_sibling(table, dest, part)
            chain(table, dest, part)
    for kind in over_first:
        for dest in FAR_FIRST:
            from_sibling(kind, dest, 1)
            over(kind, dest).wait_recv()
            add(cbuf[kind].at[dest, 1], xbuf[kind].at[dest])
            chain(kind, dest, 1)

    for dest in range(LINE):

        def last():
            cbuf[table][dest, 0] = line_total(table, dest, 0).astype(BF)
            over(table, dest).start()
            done = line_total(0, dest, 1)
            o_proj[0:3] = done[0:3]
            o_out[0] = done[3]
            done = line_total(1, dest, 1)
            o_proj[3] = done[0]
            o_out[1] = done[1]
            o_up[...] = line_total(2, dest, 1)
            o_down[...] = line_total(3, dest, 1)
            done = line_total(table, dest, 1)
            over(table, dest).wait_recv()
            done = done + xbuf[table][dest].astype(F32)
            o_table[...] = done[:per]
            o_gain[...] = done[per : per + count, :per].reshape(count, 1, per)
            over(table, dest).wait_send()

        pl.when(z == dest)(last)

    for kind in range(KINDS):
        for dest in range(LINE):
            if kind in over_first:
                over(kind, dest).wait_send()
            for part in range(2):
                beside(kind, dest, part).wait_send()
                if kind == table or part:
                    for way in range(2):
                        pl.when(before(dest, way))(lambda: along(kind, dest, part, way).wait_send())


def scatter_grads(mats, more, up, down, table, gains, count):
    ranks = lax.axis_size("dp")
    width, length = mats.shape[1], table.shape[1]
    per = width // ranks
    if not line_fits(ranks, per, length):
        part = lambda value, axis: lax.psum_scatter(
            value, "dp", scatter_dimension=axis, tiled=True
        ).astype(F32)
        mats, more = part(mats, 1), part(more, 1)
        return (
            jnp.concatenate([mats[:3], more[:1]]), jnp.concatenate([mats[3:], more[1:]]),
            part(up, 0), part(down, 0), part(table, 0), part(gains, 1)[:count, None],
        )
    shards = [
        (4, per, width), (2, per, width), (per, up.shape[1]), (down.shape[0] // ranks, width),
        (TABLE_ROWS, length),
    ]
    wholes = [mats.shape, more.shape, up.shape, down.shape, (TABLE_ROWS * ranks, length)]
    dma = pltpu.SemaphoreType.DMA
    in_vmem, anywhere = pl.BlockSpec(memory_space=pltpu.VMEM), pl.BlockSpec(memory_space=pl.ANY)
    vmem = lambda dims: pltpu.VMEM(dims, BF)
    return pl.pallas_call(
        scatter_kernel,
        out_shape=[
            shape((4, per, width), F32), shape((2, per, width), F32), shape(shards[2], F32),
            shape(shards[3], F32), shape((per, length), F32), shape((count, 1, per), F32),
        ],
        in_specs=[anywhere] * 5 + [in_vmem],
        out_specs=[in_vmem] * 6,
        scratch_shapes=[vmem(s) for s in wholes]
        + [vmem((LINE, 2) + s) for s in shards]
        + [vmem((LINE,) + s) for s in shards]
        + [vmem((LINE, 2, 2) + s) for s in shards]
        + [
            dma((KINDS + ranks,)), dma((KINDS, LINE, 2)), dma((KINDS, LINE, 2)), dma((KINDS, LINE)),
            dma((KINDS, LINE)), dma((KINDS, LINE, 2, 2)), dma((KINDS, LINE, 2, 2)),
        ],
        compiler_params=pltpu.CompilerParams(
            collective_id=1, has_side_effects=True, vmem_limit_bytes=VMEM_BYTES
        ),
        name="scatter",
    )(mats, more, up, down, table, gains)


def body(
    inputs,
    positions,
    projections,
    out_projections,
    ffn_up,
    ffn_down,
    norm_gains,
    segments,
    levels,
    cotangent,
):
    micro, _, length, width = inputs.shape[1:]
    z = sizes(length, width, ffn_up.shape[2], micro)
    mats, up, down, table, gains = gather_weights(
        projections[0], out_projections[0], ffn_up[0], ffn_down[0], positions[0].T,
        norm_gains.transpose(1, 0, 2),
    )
    whole, g_in, g_mats, g_more, g_up, g_down, g_table, g_gains = run_sections(
        z, inputs[0, :, 0], cotangent[:, 0], segments, levels, mats, up, down, table, gains
    )
    d_proj, d_out, d_up, d_down, d_table, d_gains = scatter_grads(
        g_mats, g_more, g_up, g_down, g_table, g_gains, norm_gains.shape[1]
    )
    return (
        whole[None, :, None],
        g_in[None, :, None],
        d_table.T[None],
        d_proj[None],
        d_out[None],
        d_up[None],
        d_down[None],
        d_gains.transpose(1, 0, 2),
    )


def solution(mesh):
    in_specs = (
        P("section", None, "dp", None, None),
        P("section", None, "dp"),
        P("section", None, "dp", None),
        P("section", None, "dp", None),
        P("section", "dp", None),
        P("section", "dp", None),
        P("section", None, "dp"),
        P(None, "dp", None),
        P(None, None, "dp", None),
        P(None, "dp", None, None),
    )
    out_specs = (
        P("section", None, "dp", None, None),
        P("section", None, "dp", None, None),
        P("section", None, "dp"),
        P("section", None, "dp", None),
        P("section", None, "dp", None),
        P("section", "dp", None),
        P("section", "dp", None),
        P("section", None, "dp"),
    )
    return jax.shard_map(body, mesh=mesh, in_specs=in_specs, out_specs=out_specs, check_vma=False)
```

```python
from functools import partial

import jax
import jax.numpy as jnp
from jax import lax
from jax.experimental import pallas as pl
from jax.experimental.pallas import tpu as pltpu
from jax.sharding import PartitionSpec as P

BF = jnp.bfloat16
F32 = jnp.float32
DH = 64
PAIR = 2 * DH
QB = 128
WIN = 256
TB = 256
MESH = pl.DeviceIdType.MESH
VMEM_BYTES = 62 * 1024 * 1024


def nn(left, right):
    return jnp.dot(left, right, preferred_element_type=F32)


def nt(left, right):
    return lax.dot_general(left, right, (((1,), (1,)), ((), ())), preferred_element_type=F32)


def tn(left, right):
    return lax.dot_general(left, right, (((0,), (0,)), ((), ())), preferred_element_type=F32)


def norm_parts(stream):
    centred = stream - jnp.mean(stream, axis=-1, keepdims=True)
    scale = lax.rsqrt(jnp.mean(centred * centred, axis=-1, keepdims=True) + 1e-05)
    return centred * scale, scale


def norm_back(grad, unit, scale, gain):
    inner = grad * gain
    first = jnp.mean(inner, axis=-1, keepdims=True)
    second = jnp.mean(inner * unit, axis=-1, keepdims=True)
    return scale * (inner - first - unit * second), jnp.sum(grad * unit, axis=0, keepdims=True)


def block_at(index, size):
    if isinstance(index, int):
        return pl.ds(index * size, size)
    return pl.ds(pl.multiple_of(index * size, size), size)


def lane_halves(scale=1.0):
    lane = lax.broadcasted_iota(jnp.int32, (1, PAIR), 1)
    low = jnp.where(lane < DH, scale, 0.0).astype(BF)
    high = jnp.where(lane < DH, 0.0, scale).astype(BF)
    return low, high


def both_heads(block, halves):
    return jnp.concatenate([block * halves[0], block * halves[1]], axis=0)


def join_heads(stacked):
    lane = lax.broadcasted_iota(jnp.int32, (QB, PAIR), 1)
    return jnp.where(lane < DH, stacked[:QB], stacked[QB:])


def window_start(index, length):
    return pl.multiple_of(jnp.clip(index * QB - DH, 0, length - WIN), DH)


def make_codes(segments, source_level, target_level, codes_ref, cols_ref):
    segment = segments[...]
    length = segment.shape[1]
    before = pltpu.roll(segment, 1, axis=1)
    lane = lax.broadcasted_iota(jnp.int32, (1, length), 1)
    first = (lane == 0) | (segment != before)
    usable = jnp.where(first | (source_level[...] > 0), segment, -1)
    row = lax.broadcasted_iota(jnp.int32, (8, length), 0)
    codes = jnp.where(row == 0, usable, jnp.where(row == 1, segment, target_level[...]))
    codes_ref[...] = codes
    cols_ref[...] = codes.T


def mask_bias(index, start, codes_ref, cols_ref, causal):
    keys = cols_ref[pl.ds(start, WIN), :]
    queries = codes_ref[:, block_at(index, QB)]
    query_segment = queries[1:2, :]
    if causal:
        key_id = start + lax.broadcasted_iota(jnp.int32, (WIN, QB), 0)
        query_id = index * QB + lax.broadcasted_iota(jnp.int32, (WIN, QB), 1)
        allowed = (keys[:, 1:2] == query_segment) & (
            (keys[:, 2:3] < queries[2:3, :]) | (key_id == query_id)
        )
    else:
        allowed = keys[:, 0:1] == query_segment
    bias = jnp.where(allowed, 0.0, -1e30)
    return jnp.concatenate([bias, bias], axis=1)


def attend_block(index, q_ref, k_ref, v_ref, codes_ref, cols_ref, weights_ref, mixed_ref, causal):
    length, width = q_ref.shape
    start = window_start(index, length)
    rows = block_at(index, QB)
    bias = mask_bias(index, start, codes_ref, cols_ref, causal)
    halves = lane_halves(DH ** -0.5)
    for pair in range(width // PAIR):
        lanes = slice(pair * PAIR, (pair + 1) * PAIR)
        queries = both_heads(q_ref[rows, lanes], halves)
        scores = nt(k_ref[pl.ds(start, WIN), lanes], queries) + bias
        shifted = jnp.exp(scores - jnp.max(scores, axis=0, keepdims=True))
        weights = (shifted * (1.0 / jnp.sum(shifted, axis=0, keepdims=True))).astype(BF)
        weights_ref[index, pair] = weights
        out = tn(weights, v_ref[pl.ds(start, WIN), lanes])
        mixed_ref[rows, lanes] = join_heads(out).astype(BF)


def attend_back_block(
    index, q_ref, k_ref, v_ref, weights_ref, mixed_ref, dmixed_ref, dq_ref, dk_ref, dv_ref
):
    length, width = q_ref.shape
    start = window_start(index, length)
    rows = block_at(index, QB)
    window = pl.ds(start, WIN)
    plain = lane_halves()
    halves = lane_halves(DH ** -0.5)
    ones = jnp.ones((WIN, PAIR), BF)
    for pair in range(width // PAIR):
        lanes = slice(pair * PAIR, (pair + 1) * PAIR)
        queries = both_heads(q_ref[rows, lanes], halves)
        keys = k_ref[window, lanes]
        values = v_ref[window, lanes]
        weights = weights_ref[index, pair]
        dmixed = dmixed_ref[rows, lanes]
        grads = both_heads(dmixed, plain)
        inner = (dmixed.astype(F32) * mixed_ref[rows, lanes].astype(F32) * -1.0).astype(BF)
        left = jnp.concatenate([values, ones], axis=1)
        right = jnp.concatenate([grads, both_heads(inner, plain)], axis=1)
        centred = nt(left, right)
        dscores = (weights.astype(F32) * centred).astype(BF)
        dv_ref[window, lanes] += nn(weights, grads)
        dk_ref[window, lanes] += nn(dscores, queries)
        dq = tn(dscores, keys) * (DH ** -0.5)
        dq_ref[rows, lanes] = join_heads(dq).astype(BF)


def gelu_parts(value):
    cdf = 0.5 + 0.5 * lax.erf(value * (0.5 ** 0.5))
    density = jnp.exp(value * value * -0.5) * 0.3989422804014327
    return value * cdf, cdf + value * density


def feed_block(normed, up_ref, down_ref, hidden_ref, slope_ref, rows):
    total = None
    width = up_ref.shape[1]
    step = 512
    for at in range(0, width, step):
        hidden, slope = gelu_parts(nn(normed, up_ref[:, at : at + step]))
        hidden = hidden.astype(BF)
        hidden_ref[rows, at : at + step] = hidden
        slope_ref[rows, at : at + step] = slope.astype(BF)
        term = nn(hidden, down_ref[at : at + step, :])
        total = term if total is None else total + term
    return total


def feed_back_block(grad, up_ref, down_ref, slope_ref, rows):
    total = None
    width = up_ref.shape[1]
    step = 512
    for at in range(0, width, step):
        dhidden = nt(grad, down_ref[at : at + step, :])
        dup = (dhidden * slope_ref[rows, at : at + step].astype(F32)).astype(BF)
        slope_ref[rows, at : at + step] = dup
        term = nt(dup, up_ref[:, at : at + step])
        total = term if total is None else total + term
    return total


class Queue:
    def __init__(self):
        self.steps = []

    def add(self, *groups):
        self.steps.extend(groups)

    def next(self):
        return self.steps.pop(0) if self.steps else None

    def flush(self):
        while self.steps:
            self.next()()


def loop(count, body, queue=None):
    hooks = [queue.next() if queue else None for _ in range(count)]

    def step(index, carry):
        body(index)
        for turn, hook in enumerate(hooks):
            if hook is not None:
                pl.when(index == turn)(hook)
        return carry

    lax.fori_loop(0, count, step, 0)


def put_grad(out, index, value):
    if out.prior is not None:
        value = value + out.buf[index].astype(F32)
    out.buf[index] = value.astype(BF)


def weight_grad(out, left_t_refs, right_refs, transposed):
    step = 512
    width = right_refs[0].shape[1]

    def slab(index):
        cols = block_at(index, step)
        value = None
        for left_t, right in zip(left_t_refs, right_refs):
            term = nn(left_t[...], right[:, cols])
            value = term if value is None else value + term
        if transposed:
            put_grad(out, (cols, slice(None)), value.T)
        else:
            put_grad(out, (slice(None), cols), value)

    loop(width // step, slab)


def put_table(out, rows, value):
    value = value.T.reshape(out.buf.shape[:2] + (value.shape[0],))
    put_grad(out, (slice(None), slice(None), rows), value)


def add_gain(out, row, value):
    out.buf[row : row + 1, :] += value


class Source:
    def __init__(self, hbm, buf, sem):
        self.buf, self.copy, self.here = buf, pltpu.make_async_copy(hbm, buf, sem), False
        self.copy.start()

    def __call__(self):
        if not self.here:
            self.copy.wait()
            self.here = True
        return self.buf


class Sink:
    def __init__(self, hbm, buf, sems, first, parts, axis, prior):
        self.hbm, self.buf, self.sems, self.first = hbm, buf, sems, first
        self.parts, self.axis, self.prior = parts, axis, prior

    def copy(self, part):
        view = [slice(None)] * len(self.buf.shape)
        size = self.buf.shape[self.axis] // self.parts
        view[self.axis] = block_at(part, size)
        view = tuple(view)
        return pltpu.make_async_copy(
            self.buf.at[view], self.hbm.at[view], self.sems.at[self.first + part]
        )

    def send(self, part=0):
        self.copy(part).start()

    def wait(self):
        for part in range(self.parts):
            self.copy(part).wait()


class Ready:
    def __init__(self, buf, before=None):
        self.buf, self.before = buf, before

    def __call__(self):
        if self.before is not None:
            self.before()
            self.before = None
        return self.buf


class Total:
    def __init__(self, buf, first):
        self.buf = buf
        self.prior = None if first else buf


class Link:
    def __init__(self, outbox, inbox, send, recv, parts):
        self.buf, self.inbox, self.sems, self.parts = outbox, inbox, (send, recv), parts

    def copy(self, part):
        size = self.buf.shape[0] // self.parts
        rows = block_at(part, size)
        return pltpu.make_async_remote_copy(
            src_ref=self.buf.at[rows, :], dst_ref=self.inbox.at[rows, :],
            send_sem=self.sems[0].at[part], recv_sem=self.sems[1].at[part],
            device_id={"section": 1 - lax.axis_index("section")}, device_id_type=MESH,
        )

    def send(self, part):
        self.copy(part).start()

    def wait(self):
        for part in range(self.parts):
            self.copy(part).wait_send()

    def come(self, part):
        self.copy(part).wait_recv()


def encode_attend(src, table, gains, segments, source_level, target_level, mats, qkv, weights, mixed, codes, cols, queue):
    length = src.buf.shape[0]
    make_codes(segments(), source_level(), target_level(), codes, cols)
    src, table, gains, mats = src(), table(), gains(), mats()

    def project(index):
        rows = block_at(index, TB)
        unit, _ = norm_parts(src[rows, :].astype(F32) + table[rows, :].astype(F32))
        normed = (unit * gains[0:1, :]).astype(BF)
        for which in range(3):
            qkv.buf[which, rows, :] = nn(normed, mats[which]).astype(BF)
        qkv.send(index)

    loop(length // TB, project, queue)

    def attend(index):
        for part in range(TB // QB):
            attend_block(
                index * (TB // QB) + part,
                qkv.buf.at[0], qkv.buf.at[1], qkv.buf.at[2], codes, cols, weights.buf, mixed.buf, False,
            )
        weights.send(index)
        mixed.send(index)

    loop(length // TB, attend, queue)


def encode_feed(src, mixed, table, gains, mats, up, down, mem, x1, x2, hidden, slope):
    length = src.buf.shape[0]
    table, gains, mats, up, down = table(), gains(), mats(), up(), down()
    src, mixed = src(), mixed()

    def rest(index):
        rows = block_at(index, TB)
        stream = src[rows, :].astype(F32) + table[rows, :].astype(F32)
        stream = stream + nn(mixed[rows, :], mats[3])
        x1.buf[rows, :] = stream
        x1.send(index)
        unit, _ = norm_parts(stream)
        normed = (unit * gains[1:2, :]).astype(BF)
        stream = stream + feed_block(normed, up, down, hidden.buf, slope.buf, rows)
        x2.buf[rows, :] = stream
        unit, _ = norm_parts(stream)
        mem.buf[rows, :] = (unit * gains[2:3, :]).astype(BF)
        for item in (mem, x2, hidden, slope):
            item.send(index)

    loop(length // TB, rest)


def encode_back(
    x2, dmem, gains, slope, down, up, x1, mats, hidden, mixed, qkv, weights, src, table,
    g_in, g_mats, g_up, g_down, g_table, g_gains,
    dy, dy_t, a_t, dx, dmixed, dq, dk, dv, queue, fed,
):
    length = src.buf.shape[0]
    if g_gains.prior is None:
        g_gains.buf[...] = jnp.zeros_like(g_gains.buf)
    x2, gains, slope, down, up, x1, mats = x2(), gains(), slope(), down(), up(), x1(), mats()

    def feed_step(index):
        rows = block_at(index, TB)
        dmem.come(index)
        unit, scale = norm_parts(x2[rows, :])
        grad, d_gain = norm_back(dmem.inbox[rows, :].astype(F32), unit, scale, gains[2:3, :])
        add_gain(g_gains, 2, d_gain)
        low = grad.astype(BF)
        dy_t[:, rows] = low.T
        dnormed = feed_back_block(low, up, down, slope, rows)
        unit, scale = norm_parts(x1[rows, :])
        a_t[:, rows] = (unit * gains[1:2, :]).astype(BF).T
        back, d_gain = norm_back(dnormed, unit, scale, gains[1:2, :])
        add_gain(g_gains, 1, d_gain)
        grad = grad + back
        dx[rows, :] = grad
        low = grad.astype(BF)
        dy[rows, :] = low
        dmixed[rows, :] = nt(low, mats[3]).astype(BF)

    loop(length // TB, feed_step)
    weight_grad(g_up, [a_t], [slope], False)
    weight_grad(g_down, [dy_t], [hidden()], True)
    mixed = mixed()
    put_grad(g_mats, 3, tn(mixed[...], dy[...]))
    fed()
    qkv, weights = qkv(), weights()
    dk[...] = jnp.zeros_like(dk)
    dv[...] = jnp.zeros_like(dv)

    def attend_step(index):
        attend_back_block(
            index, qkv.at[0], qkv.at[1], qkv.at[2], weights, mixed, dmixed, dq, dk, dv
        )

    loop(length // QB, attend_step, queue)
    src, table = src(), table()

    def project_step(index):
        rows = block_at(index, TB)
        unit, scale = norm_parts(src[rows, :].astype(F32) + table[rows, :].astype(F32))
        a_t[:, rows] = (unit * gains[0:1, :]).astype(BF).T
        dnormed = nt(dq[rows, :], mats[0])
        dnormed += nt(dk[rows, :].astype(BF), mats[1])
        dnormed += nt(dv[rows, :].astype(BF), mats[2])
        back, d_gain = norm_back(dnormed, unit, scale, gains[0:1, :])
        add_gain(g_gains, 0, d_gain)
        grad = dx[rows, :] + back
        g_in.buf[rows, :] = grad
        g_in.send(index)
        put_table(g_table, rows, grad)

    loop(length // TB, project_step, queue)
    put_grad(g_mats, 0, nn(a_t[...], dq[...]))
    put_grad(g_mats, 1, nn(a_t[...], dk[...].astype(BF)))
    put_grad(g_mats, 2, nn(a_t[...], dv[...].astype(BF)))


def self_forward(tgt, table, gains, segments, source_level, target_level, mats, qkv, weights, mixed, h1, codes, cols, queue):
    length = tgt.buf.shape[0]
    make_codes(segments(), source_level(), target_level(), codes, cols)
    tgt, table, gains, mats = tgt(), table(), gains(), mats()

    def project(index):
        rows = block_at(index, TB)
        stream = table[rows, :].astype(F32)
        unit, _ = norm_parts(stream)
        qkv.buf[0, rows, :] = nn((unit * gains[0:1, :]).astype(BF), mats[0]).astype(BF)
        unit, _ = norm_parts(tgt[rows, :].astype(F32) + stream)
        normed = (unit * gains[0:1, :]).astype(BF)
        for which in (1, 2):
            qkv.buf[which, rows, :] = nn(normed, mats[which]).astype(BF)
        qkv.send(index)

    loop(length // TB, project, queue)

    def rest(index):
        for part in range(TB // QB):
            attend_block(
                index * (TB // QB) + part,
                qkv.buf.at[0], qkv.buf.at[1], qkv.buf.at[2], codes, cols, weights.buf, mixed.buf, True,
            )
        rows = block_at(index, TB)
        h1.buf[rows, :] = table[rows, :].astype(F32) + nn(mixed.buf[rows, :], mats[3])
        for item in (weights, mixed, h1):
            item.send(index)

    loop(length // TB, rest, queue)


def self_back(
    dh1, mats, mixed, qkv, weights, tgt, table, gains,
    g_in, g_mats, g_table, g_gains,
    dy, a_t, b_t, dmixed, dq, dk, dv, queue,
):
    length = tgt.buf.shape[0]
    dk[...] = jnp.zeros_like(dk)
    dv[...] = jnp.zeros_like(dv)
    dh1, mats, mixed = dh1(), mats(), mixed()

    def out_step(index):
        rows = block_at(index, TB)
        low = dh1[rows, :].astype(BF)
        dy[rows, :] = low
        dmixed[rows, :] = nt(low, mats[3]).astype(BF)

    loop(length // TB, out_step)
    put_grad(g_mats, 3, tn(mixed[...], dy[...]))
    qkv, weights = qkv(), weights()

    def attend_step(index):
        attend_back_block(
            index, qkv.at[0], qkv.at[1], qkv.at[2], weights, mixed, dmixed, dq, dk, dv
        )

    loop(length // QB, attend_step, queue)
    tgt, table, gains = tgt(), table(), gains()

    def project_step(index):
        rows = block_at(index, TB)
        stream = table[rows, :].astype(F32)
        unit, scale = norm_parts(stream)
        a_t[:, rows] = (unit * gains[0:1, :]).astype(BF).T
        back, d_gain = norm_back(nt(dq[rows, :], mats[0]), unit, scale, gains[0:1, :])
        dtable = dh1[rows, :] + back
        unit, scale = norm_parts(tgt[rows, :].astype(F32) + stream)
        b_t[:, rows] = (unit * gains[0:1, :]).astype(BF).T
        dnormed = nt(dk[rows, :].astype(BF), mats[1])
        dnormed += nt(dv[rows, :].astype(BF), mats[2])
        back, d_gain_too = norm_back(dnormed, unit, scale, gains[0:1, :])
        add_gain(g_gains, 0, d_gain + d_gain_too)
        g_in.buf[rows, :] = back
        g_in.send(index)
        put_table(g_table, rows, dtable + back)

    loop(length // TB, project_step, queue)
    put_grad(g_mats, 0, nn(a_t[...], dq[...]))
    put_grad(g_mats, 1, nn(b_t[...], dk[...].astype(BF)))
    put_grad(g_mats, 2, nn(b_t[...], dv[...].astype(BF)))


def feed_grads(a_t, dup, cot, hidden, g_up, g_down, cot_t):
    cot_t[...] = cot()[...].T
    weight_grad(g_up, [a_t()], [dup()], False)
    weight_grad(g_down, [cot_t], [hidden()], True)


def cross(
    h1, gains, segments, source_level, target_level, mats, mem, up, down, cot,
    out, dmem, dh1, g_mats, g_gains, a_t, dup, hidden,
    codes, cols, qkv, weights, mixed, h2, dy, b_t, dmixed, dq, dk, dv,
):
    length = h1.buf.shape[0]
    make_codes(segments(), source_level(), target_level(), codes, cols)
    if g_gains.prior is None:
        g_gains.buf[...] = jnp.zeros_like(g_gains.buf)
    dk[...] = jnp.zeros_like(dk)
    dv[...] = jnp.zeros_like(dv)
    h1, gains, mats = h1(), gains(), mats()
    memory = mem.inbox

    def project(index):
        rows = block_at(index, TB)
        unit, _ = norm_parts(h1[rows, :])
        qkv[0, rows, :] = nn((unit * gains[1:2, :]).astype(BF), mats[0]).astype(BF)
        mem.come(index)
        qkv[1, rows, :] = nn(memory[rows, :], mats[2]).astype(BF)
        qkv[2, rows, :] = nn(memory[rows, :], mats[3]).astype(BF)

    loop(length // TB, project)
    up, down, cot = up(), down(), cot()

    def middle(index):
        for part in range(TB // QB):
            attend_block(
                index * (TB // QB) + part,
                qkv.at[0], qkv.at[1], qkv.at[2], codes, cols, weights, mixed, False,
            )
        rows = block_at(index, TB)
        stream = h1[rows, :] + nn(mixed[rows, :], mats[1])
        unit, scale = norm_parts(stream)
        normed = (unit * gains[2:3, :]).astype(BF)
        a_t.buf[:, rows] = normed.T
        fed = feed_block(normed, up, down, hidden.buf, dup.buf, rows)
        out.buf[rows, :] = (stream + fed).astype(BF)
        low = cot[rows, :]
        dnormed = feed_back_block(low, up, down, dup.buf, rows)
        back, d_gain = norm_back(dnormed, unit, scale, gains[2:3, :])
        add_gain(g_gains, 2, d_gain)
        grad = low.astype(F32) + back
        h2[rows, :] = grad
        low = grad.astype(BF)
        dy[rows, :] = low
        dmixed[rows, :] = nt(low, mats[1]).astype(BF)
        for item in (out, hidden, dup):
            item.send(index)

    loop(length // TB, middle)
    a_t.send()

    def attend_step(index):
        def one(at):
            attend_back_block(at, qkv.at[0], qkv.at[1], qkv.at[2], weights, mixed, dmixed, dq, dk, dv)

        steps = TB // QB
        last = length // TB - 1
        pl.when(index == 0)(lambda: one(0))
        for part in range(1, steps):
            one(index * steps + part)
        pl.when(index < last)(lambda: one((index + 1) * steps))
        rows = block_at(index, TB)
        dkeys = dk[rows, :].astype(BF)
        dvalues = dv[rows, :].astype(BF)
        dmem.buf[rows, :] = (nt(dkeys, mats[2]) + nt(dvalues, mats[3])).astype(BF)
        dmem.send(index)

    loop(length // TB, attend_step)

    def project_step(index):
        rows = block_at(index, TB)
        unit, scale = norm_parts(h1[rows, :])
        b_t[:, rows] = (unit * gains[1:2, :]).astype(BF).T
        back, d_gain = norm_back(nt(dq[rows, :], mats[0]), unit, scale, gains[1:2, :])
        add_gain(g_gains, 1, d_gain)
        dh1.buf[rows, :] = h2[rows, :] + back
        dh1.send(index)

    loop(length // TB, project_step)
    put_grad(g_mats, 0, nn(b_t[...], dq[...]))
    put_grad(g_mats, 1, tn(mixed[...], dy[...]))
    put_grad(g_mats, 2, tn(memory[...], dk[...].astype(BF)))
    put_grad(g_mats, 3, tn(memory[...], dv[...].astype(BF)))


def shape(dims, kind):
    return jax.ShapeDtypeStruct(dims, kind)


def sizes(length, width, ff, micro, ranks):
    blocks = length // QB
    pairs = width // PAIR
    return dict(
        tok=shape((length, width), BF),
        tok32=shape((length, width), F32),
        outputs=shape((micro, length, width), BF),
        g_in=shape((micro, length, width), F32),
        qkv=shape((3, length, width), BF),
        weights=shape((blocks, pairs, WIN, 2 * QB), BF),
        hidden=shape((length, ff), BF),
        tokt=shape((width, length), BF),
        packed=shape((ranks, width // ranks, length), BF),
        packed_gains=shape((ranks, 16, PAIR), BF),
        mats=shape((4, width, width), BF),
        up=shape((width, ff), BF),
        down=shape((ff, width), BF),
        gains=shape((8, width), F32),
        pair=shape((2, width, width), BF),
        row=shape((1, length), jnp.int32),
        codes=shape((8, length), jnp.int32),
        cols=shape((length, 8), jnp.int32),
    )


LINE = 4
AHEAD = (2, 1, 3, 0)
TABLE, GAIN, MATS, UP, DOWN, CROSS, OUT = range(7)
KINDS = 7


def rank_of(z, x, core):
    return z * 4 + x * 2 + core


def remote(src, dst, send, recv, to):
    return pltpu.make_async_remote_copy(
        src_ref=src, dst_ref=dst, send_sem=send, recv_sem=recv, device_id=to, device_id_type=MESH
    )


def rows_at(ref, per, rank):
    view = [slice(None)] * len(ref.shape)
    view[-2] = pl.ds(pl.multiple_of(rank * per, 16), per)
    return ref.at[tuple(view)]


class Place:
    def __init__(self):
        me = lax.axis_index("dp")
        self.z, self.x, self.core = me // 4, (me // 2) % 2, me % 2
        self.rank = me
        self.section = lax.axis_index("section")
        self.partner = {"section": 1 - self.section}
        self.across = {"dp": rank_of(self.z, 1 - self.x, self.core)}
        self.sibling = {"dp": rank_of(self.z, self.x, 1 - self.core)}

    def ahead(self, step):
        return (self.z + step) % LINE

    def on_line(self, step):
        return {"dp": rank_of(self.ahead(step), self.x, self.core)}

    def line(self, other):
        return 1 - self.x if other else self.x

    def meet(self, semaphore, also=()):
        devices = [self.across, self.sibling, *also] + [self.on_line(step) for step in range(1, LINE)]
        for device in devices:
            pl.semaphore_signal(semaphore, inc=1, device_id=device, device_id_type=MESH)
        pl.semaphore_wait(semaphore, len(devices))


class Gather:
    def __init__(self, place, kind, view, sems):
        self.place, self.kind, self.view = place, kind, view
        self.zsend, self.zrecv, self.xsend, self.xrecv, self.csend, self.crecv = sems

    def block(self, back, other):
        place = self.place
        return self.view(rank_of(place.ahead(LINE - back), place.line(other), place.core))

    def along(self, step):
        at, block = (self.kind, step - 1), self.block(0, 0)
        return remote(block, block, self.zsend.at[at], self.zrecv.at[at], self.place.on_line(step))

    def over(self, back):
        at, block = (self.kind, back), self.block(back, 0)
        return remote(block, block, self.xsend.at[at], self.xrecv.at[at], self.place.across)

    def beside(self, back, other):
        at, block = (self.kind, back + LINE * other), self.block(back, other)
        return remote(block, block, self.csend.at[at], self.crecv.at[at], self.place.sibling)

    def begin_along(self):
        for step in (1, 3, 2):
            self.along(step).start()

    def begin_over(self):
        self.over(0).start()
        self.beside(0, 0).start()

    def pass_on(self, back):
        self.along(back).wait_recv()
        self.over(back).start()
        self.beside(back, 0).start()

    def share(self, back):
        self.over(back).wait_recv()
        self.beside(back, 1).start()

    def finish(self):
        for step in range(1, LINE):
            self.along(step).wait_send()
        for back in range(LINE):
            self.over(back).wait_send()
            for other in range(2):
                copy = self.beside(back, other)
                copy.wait_send()
                copy.wait_recv()


def passing(arrays):
    return [partial(array.pass_on, back) for back in (1, 3, 2) for array in arrays]


def sharing(arrays):
    return [partial(array.share, back) for back in (0, 1, 3, 2) for array in arrays]


def in_groups(steps, size):
    def group(some):
        return lambda: [step() for step in some] and None

    return [group(steps[at : at + size]) for at in range(0, len(steps), size)]


class Scatter:
    def __init__(self, place, kind, view, slots, sems):
        self.place, self.kind, self.view, self.slots = place, kind, view, slots
        self.zsend, self.zrecv, self.xsend, self.xrecv, self.csend, self.crecv = sems

    def from_core(self, step, part):
        return self.slots(step * 2 + part)

    def from_x(self, step):
        return self.slots(2 * LINE + step)

    def from_z(self, step):
        return self.slots(3 * LINE + step - 1)

    def own(self, step, part, its_core):
        return self.view(rank_of(self.place.ahead(step), self.place.line(1 - part), its_core))

    def beside(self, step, part):
        at = (self.kind, step, part)
        return remote(
            self.own(step, part, 1 - self.place.core), self.from_core(step, part), self.csend.at[at],
            self.crecv.at[at], self.place.sibling,
        )

    def over(self, step):
        at = (self.kind, step)
        return remote(
            self.from_core(step, 0), self.from_x(step), self.xsend.at[at], self.xrecv.at[at],
            self.place.across,
        )

    def along(self, step):
        at = (self.kind, step - 1)
        return remote(
            self.from_core(step, 1), self.from_z(step), self.zsend.at[at], self.zrecv.at[at],
            self.place.on_line(step),
        )

    def total(self, *terms):
        value = terms[0][...].astype(F32)
        for term in terms[1:]:
            value = value + term[...].astype(F32)
        return value

    def begin(self):
        for part in range(2):
            for step in AHEAD:
                self.beside(step, part).start()

    def first(self, step):
        self.beside(step, 0).wait_recv()
        both = self.from_core(step, 0)
        both[...] = self.total(both, self.own(step, 0, self.place.core)).astype(BF)
        self.over(step).start()

    def second(self, step):
        self.beside(step, 1).wait_recv()
        self.over(step).wait_recv()
        four = self.from_core(step, 1)
        four[...] = self.total(four, self.own(step, 1, self.place.core), self.from_x(step)).astype(BF)
        if step:
            self.along(step).start()

    def finish(self, put):
        for step in range(1, LINE):
            self.along(step).wait_recv()
        put(self.total(self.from_core(0, 1), *[self.from_z(step) for step in range(1, LINE)]))
        for step in range(LINE):
            self.over(step).wait_send()
            if step:
                self.along(step).wait_send()
            for part in range(2):
                self.beside(step, part).wait_send()


def firsts(arrays):
    return [partial(array.first, step) for step in AHEAD for array in arrays]


def seconds(arrays):
    return [partial(array.second, step) for step in AHEAD for array in arrays]


POOL = (("row", 3), ("tok", 6), ("tok32", 4), ("tokt", 2), ("qkv", 1), ("weights", 1), ("hidden", 2))
KEPT = ("qkv", "weights", "tok", "tok32", "tok32", "hidden", "hidden", "tokt")
PERSISTENT = (
    "tok", "gains", "mats", "up", "down", "mats", "mats", "mats", "up", "down", "packed", "gains", "codes",
    "cols", "outputs", "outputs",
)


def step_kernel(z, line, *refs):
    refs = list(refs)
    take = lambda count: [refs.pop(0) for _ in range(count)]
    given, (own, cot, segments, levels) = take(6), take(4)
    whole, g_in = take(2)
    results = take(6)
    micro, length = own.shape[:2]
    parts = length // TB
    kept = [take(len(KEPT)) for _ in range(micro)]
    (
        v_table, v_gains, v_mats, v_up, v_down, v_cross, s_mats, s_cross, s_up, s_down, s_table, s_gains,
        codes, cols, inbox, outbox,
    ) = take(len(PERSISTENT))
    pool = {name: take(count) for name, count in POOL}
    local, ysend, yrecv = take(3)
    section = lax.axis_index("section")
    count = [0]

    def sems(number):
        count[0] += number
        return count[0] - number

    def load(hbm, buf):
        return Source(hbm, buf, local.at[sems(1)])

    def store(hbm, buf, axis=0, split=True):
        number = parts if split else 1
        return Sink(hbm, buf, local, sems(number), number, axis, None)

    def box(m):
        return Link(outbox.at[m], inbox.at[m], ysend.at[m], yrecv.at[m], parts)

    def code_loads(m):
        hbm = (segments.at[m], levels.at[0, m], levels.at[1, m])
        return [load(ref, buf) for ref, buf in zip(hbm, pool["row"])]

    queue = Queue()
    if line:
        o_proj, o_out, o_up, o_down, o_table, o_gain = results
        r_mats, r_gains, packed_gains, handing, handed = take(5)
        g_sems, s_sems = take(6), take(6)
        ready, shard_sems, hand_sems = refs
        place = Place()
        per, n_gains = o_table.shape[0], o_gain.shape[0]
        ranks = s_table.shape[0]
        rank, lent = place.rank, slice(2, 4)

        view_of = {
            TABLE: lambda at: s_table.at[at],
            GAIN: lambda at: packed_gains.at[at],
            MATS: lambda at: rows_at(v_mats, per, at),
            UP: lambda at: rows_at(v_up, per, at),
            DOWN: lambda at: rows_at(v_down, o_down.shape[0], at),
            CROSS: lambda at: rows_at(v_cross, per, at),
        }
        gathers = {kind: Gather(place, kind, view, g_sems) for kind, view in view_of.items()}
        sum_of = {
            TABLE: lambda at: s_table.at[at],
            GAIN: lambda at: packed_gains.at[at],
            MATS: lambda at: rows_at(s_mats.at[0:3], per, at),
            UP: lambda at: rows_at(s_up, per, at),
            DOWN: lambda at: rows_at(s_down, o_down.shape[0], at),
            CROSS: lambda at: rows_at(s_cross, per, at),
            OUT: lambda at: rows_at(s_mats.at[3], per, at),
        }
        width = v_mats.shape[-1]
        hidden_0, hidden_1 = pool["hidden"]
        slots = 4 * LINE

        def in_hidden(buf, first, tall, wide):
            across = buf.shape[1] // wide

            def slot(number):
                row, lane = first + number // across * tall, number % across * wide
                return buf.at[row : row + tall, lane : lane + wide]

            return slot

        slot_of = {
            TABLE: in_hidden(hidden_0, slots * per, per, length),
            GAIN: lambda number: r_gains.at[number],
            MATS: lambda number: r_mats.at[number, 0:3],
            UP: in_hidden(hidden_0, 0, per, hidden_0.shape[1]),
            DOWN: in_hidden(hidden_1, 0, o_down.shape[0], width),
            CROSS: lambda number: r_mats.at[number],
            OUT: lambda number: r_mats.at[number, 3],
        }
        scatters = {
            kind: Scatter(place, kind, view, slot_of[kind], s_sems) for kind, view in sum_of.items()
        }

        p_proj, p_out, p_up, p_down, p_pos, p_gain = given
        s_table[rank] = p_pos[...].astype(BF)
        gain = jnp.concatenate([p_gain[...].reshape(n_gains, per), jnp.zeros((16 - n_gains, per), F32)], axis=0)
        packed_gains[rank] = jnp.concatenate([gain, jnp.zeros((16, PAIR - per), F32)], axis=1).astype(BF)
        own_mats = rows_at(v_mats, per, rank)
        for to, shard in enumerate((p_proj.at[0], p_proj.at[1], p_proj.at[2], p_out.at[0])):
            own_mats[to] = shard[...].astype(BF)
        own_cross = rows_at(v_cross, per, rank)
        for to, shard in enumerate((p_proj.at[3], p_out.at[1])):
            low = shard[...].astype(BF)
            own_cross[to] = low
            r_mats[0, to] = low
        place.meet(pltpu.get_barrier_semaphore(), (place.partner,))
        early = [gathers[kind] for kind in (GAIN, TABLE, MATS)]
        for item in early:
            item.begin_along()
            item.begin_over()
        lend = remote(
            r_mats.at[0, 0:2], own_cross.at[lent], shard_sems.at[0], shard_sems.at[1], place.partner
        )
        pl.when(section == 0)(lambda: lend.start())
        rows_at(v_up, per, rank)[...] = p_up[...].astype(BF)
        rows_at(v_down, o_down.shape[0], rank)[...] = p_down[...].astype(BF)
        gathers[UP].begin_over()
        for step in passing(early):
            step()
        gathers[UP].begin_along()
        for step in sharing(early):
            step()
        gathers[DOWN].begin_along()
        gathers[DOWN].begin_over()
        for item in early[:2]:
            item.finish()
        v_gains[...] = jnp.zeros_like(v_gains)
        group = PAIR // per
        for first in range(0, ranks, group):
            at = slice(first * per, (first + group) * per)
            v_table[:, at] = jnp.concatenate([s_table[one] for one in range(first, first + group)], axis=0).T
            v_gains[:n_gains, at] = jnp.concatenate(
                [packed_gains[one, :n_gains, :per] for one in range(first, first + group)], axis=1
            ).astype(F32)
        early[2].finish()

        def weights_ready(kinds):
            def before():
                queue.flush()
                for kind in kinds:
                    gathers[kind].finish()

            return before

        def put_mats(value):
            o_proj[0:3] = value

        def put_out(value):
            o_out[0] = value

        def put_up(value):
            o_up[...] = value

        def put_down(value):
            o_down[...] = value

        def put_pos(value):
            o_table[...] = value

        def put_gain(value):
            o_gain[...] = value[:n_gains, :per].reshape(n_gains, 1, per)

        def put_cross(value):
            o_proj[3] = value[0]
            o_out[1] = value[1]
            handing[...] = value[2:4]

        hand = remote(handing, handed, hand_sems.at[0], hand_sems.at[1], place.partner)

        def feed_sums():
            place.meet(ready.at[0])
            for kind in (UP, DOWN):
                scatters[kind].begin()

        def last_sums(late):
            for at in range(ranks):
                gain = s_gains[:, at * per : (at + 1) * per]
                gain = jnp.concatenate([gain, jnp.zeros((8, per), F32)], axis=0)
                packed_gains[at] = jnp.concatenate([gain, jnp.zeros((16, PAIR - per), F32)], axis=1).astype(BF)
            items = [scatters[kind] for kind in late]
            for item in items:
                item.begin()
            for step in firsts(items):
                step()
            queue.flush()
            for step in seconds(items):
                step()
            puts = {
                UP: put_up, DOWN: put_down, OUT: put_out, MATS: put_mats, TABLE: put_pos, GAIN: put_gain,
            }
            for kind, put in puts.items():
                scatters[kind].finish(put)
    else:
        partner = {"section": 1 - section}
        barrier = pltpu.get_barrier_semaphore()
        pl.semaphore_signal(barrier, inc=1, device_id=partner, device_id_type=MESH)
        pl.semaphore_wait(barrier, 1)

    def persistent():
        if line:
            return [Ready(buf) for buf in (v_table, v_gains, v_mats, v_up, v_down, v_cross)]
        order = (4, 5, 0, 2, 3, 1)
        return [
            load(given[at], buf) for at, buf in zip(order, (v_table, v_gains, v_mats, v_up, v_down, v_cross))
        ]

    def finish(items):
        for item in items:
            item.wait()

    @pl.when(section == 0)
    def _():
        count[0] = 0
        w_table, w_gains, w_mats, w_up, w_down, _ = first = persistent()
        if line:
            pair = [gathers[UP], gathers[DOWN]]
            queue.add(None, *passing(pair[:1]), *in_groups(passing(pair[1:]) + sharing(pair), 1))
            w_up.before = weights_ready((UP, DOWN))
        base = count[0]
        src, mixed, dy, dmixed, dq = pool["tok"][:5]
        x1, x2, dx, dv = pool["tok32"]
        hidden, slope = pool["hidden"]
        dy_t, a_t = pool["tokt"]
        v_qkv, v_weights = pool["qkv"][0], pool["weights"][0]
        for m in range(micro):
            count[0] = base
            k_qkv, k_weights, k_mixed = kept[m][:3]
            sinks = [store(k_qkv, v_qkv, axis=1), store(k_weights, v_weights), store(k_mixed, mixed)]
            encode_attend(
                load(own.at[m], src), w_table, w_gains, *code_loads(m), w_mats, *sinks, codes, cols, queue
            )
            finish(sinks)
        if line:
            lend.wait_send()
        for m in range(micro):
            count[0] = base
            _, _, k_mixed, k_x1, k_x2, k_hidden, k_slope, _ = kept[m]
            sinks = [store(k_x1, x1), store(k_x2, x2), store(k_hidden, hidden), store(k_slope, slope)]
            encode_feed(
                load(own.at[m], src), load(k_mixed, mixed), w_table, w_gains, w_mats, w_up, w_down, box(m),
                *sinks,
            )
            memory = pltpu.make_async_copy(outbox.at[m], whole.at[m], local.at[sems(1)])
            memory.start()
            finish(sinks + [memory])
        for m in range(micro):
            count[0] = base
            last = line and m == micro - 1
            k_qkv, k_weights, k_mixed, k_x1, k_x2, k_hidden, k_slope, _ = kept[m]
            loads = [load(k_x2, x2), load(k_slope, slope), load(k_x1, x1), load(k_hidden, hidden)]
            late = [load(k_mixed, mixed), load(k_qkv, v_qkv), load(k_weights, v_weights), load(own.at[m], src)]
            sink = store(g_in.at[m], x2)
            sums = [Total(buf, m == 0) for buf in (s_mats, s_up, s_down, s_table, s_gains)]

            def fed():
                if last:
                    feed_sums()
                    scatters[OUT].begin()
                    up_steps, down_steps = seconds([scatters[UP]]), seconds([scatters[DOWN]])
                    queue.add(*in_groups(firsts([scatters[kind] for kind in (UP, DOWN, OUT)]), 4))
                    queue.add(None, None, up_steps[0], None, None, up_steps[1], None, up_steps[2])
                    queue.add(*up_steps[3:], *down_steps, *seconds([scatters[OUT]]))

            encode_back(
                loads[0], box(m), w_gains, loads[1], w_down, w_up, loads[2], w_mats, loads[3], *late[:3],
                late[3], w_table, sink, *sums, dy, dy_t, a_t, dx, dmixed, dq, x1, dv,
                queue, fed,
            )
            finish([sink])
        if line:
            last_sums((TABLE, GAIN, MATS))
            hand.wait_recv()
            o_proj[3] = handed[0]
            o_out[1] = handed[1]
        for item in first:
            item()

    @pl.when(section == 1)
    def _():
        count[0] = 0
        w_table, w_gains, w_mats, w_up, w_down, w_cross = first = persistent()
        if line:
            lend.wait_recv()
            gathers[CROSS].begin_along()
            gathers[CROSS].begin_over()
            three = [gathers[kind] for kind in (UP, DOWN, CROSS)]
            queue.add(None, *passing(three[:1]), *in_groups(passing(three[1:]) + sharing(three), 2))
            w_cross.before = weights_ready((UP, DOWN, CROSS))
        base = count[0]
        hidden, dup = pool["hidden"]
        a_t, b_t = pool["tokt"]
        v_qkv, v_weights = pool["qkv"][0], pool["weights"][0]
        for m in range(micro):
            count[0] = base
            k_qkv, k_weights, k_mixed, k_h1 = kept[m][:4]
            tgt, mixed = pool["tok"][:2]
            sinks = [
                store(k_qkv, v_qkv, axis=1), store(k_weights, v_weights), store(k_mixed, mixed),
                store(k_h1, pool["tok32"][0]),
            ]
            self_forward(
                load(own.at[m], tgt), w_table, w_gains, *code_loads(m), w_mats, *sinks, codes, cols, queue
            )
            finish(sinks)
        for m in range(micro):
            count[0] = base
            k_h1, k_dh1, k_hidden, k_dup, k_a = kept[m][3:8]
            v_cot, out, mixed, dy, dmixed, dq = pool["tok"]
            h1, h2, dk, dv = pool["tok32"]
            sums = [Total(buf, m == 0) for buf in (s_cross, s_gains)]
            sinks = [store(whole.at[m], out), store(k_dh1, h2)]
            feeds = [store(k_a, a_t, split=False), store(k_dup, dup), store(k_hidden, hidden)]
            cross(
                load(k_h1, h1), w_gains, *code_loads(m), w_cross, box(m), w_up, w_down,
                load(cot.at[m], v_cot), sinks[0], box(m), sinks[1], *sums, *feeds, codes, cols, v_qkv,
                v_weights, mixed, h2, dy, b_t, dmixed, dq, dk, dv,
            )
            finish(sinks + feeds)
        if line:
            scatters[CROSS].begin()
        for m in range(micro):
            count[0] = base
            k_hidden, k_dup, k_a = kept[m][5:8]
            sums = [Total(buf, m == 0) for buf in (s_up, s_down)]
            feed_grads(
                load(k_a, a_t), load(k_dup, dup), load(cot.at[m], pool["tok"][0]), load(k_hidden, hidden),
                *sums, b_t,
            )
            if line and m == 0:
                for step in firsts([scatters[CROSS]]):
                    step()
        if line:
            feed_sums()
            pair = [scatters[UP], scatters[DOWN]]
            queue.add(*in_groups(firsts(pair), 4), *seconds([scatters[CROSS]]), *seconds(pair))
        for m in range(micro):
            count[0] = base
            k_qkv, k_weights, k_mixed, _, k_dh1 = kept[m][:5]
            tgt, mixed, dy, dmixed, dq = pool["tok"][:5]
            dh1, grad, dk, dv = pool["tok32"]
            loads = [load(k_dh1, dh1), load(k_mixed, mixed), load(k_qkv, v_qkv), load(k_weights, v_weights)]
            sink = store(g_in.at[m], grad)
            sums = [Total(s_mats, m == 0), Total(s_table, m == 0), Total(s_gains, False)]
            self_back(
                loads[0], w_mats, *loads[1:], load(own.at[m], tgt), w_table, w_gains, sink, *sums, dy, a_t,
                b_t, dmixed, dq, dk, dv, queue,
            )
            finish([sink])
        if line:
            queue.flush()
            scatters[CROSS].finish(put_cross)
            hand.start()
            place.meet(ready.at[1])
            last_sums((TABLE, GAIN, MATS, OUT))
            hand.wait_send()
        for item in first:
            item()

    for m in range(micro):
        box(m).wait()
    if not line:
        copies = [
            pltpu.make_async_copy(buf, out, local.at[at])
            for at, (buf, out) in enumerate(zip((s_mats, s_cross, s_up, s_down, s_table, s_gains), results))
        ]
        for copy in copies:
            copy.start()
        for copy in copies:
            copy.wait()


def run_step(z, line, given, results, own, cot, segments, levels):
    micro, length = own.shape[:2]
    parts = length // TB
    args = [*given, own, cot, segments, levels]
    outs = [z["outputs"], z["g_in"], *results] + [z[name] for _ in range(micro) for name in KEPT]
    scratch = [z[name] for name in PERSISTENT]
    scratch += [z[name] for name, number in POOL for _ in range(number)]
    dma = pltpu.SemaphoreType.DMA
    sems = [dma((64,)), dma((micro, parts)), dma((micro, parts))]
    if line:
        per, width = given[0].shape[1:]
        slots = 4 * LINE
        own_scratch = [
            shape((slots, 4, per, width), BF), shape((slots,) + z["packed_gains"].shape[1:], BF),
            z["packed_gains"], shape((2, per, width), F32), shape((2, per, width), F32),
        ]
        sems_line = [dma((KINDS, LINE - 1))] * 2 + [dma((KINDS, LINE))] * 2 + [dma((KINDS, 2 * LINE))] * 2
        sems_line += [dma((KINDS, LINE - 1))] * 2 + [dma((KINDS, LINE))] * 2 + [dma((KINDS, LINE, 2))] * 2
        sems_line += [pltpu.SemaphoreType.REGULAR((2,)), dma((2,)), dma((2,))]
    in_vmem, anywhere = pl.BlockSpec(memory_space=pltpu.VMEM), pl.BlockSpec(memory_space=pl.ANY)
    edge = in_vmem if line else anywhere
    vmem = [pltpu.VMEM(s.shape, s.dtype) for s in scratch]
    if line:
        scratch_shapes = vmem + sems + [pltpu.VMEM(s.shape, s.dtype) for s in own_scratch] + sems_line
    else:
        scratch_shapes = vmem + sems
    outs = pl.pallas_call(
        partial(step_kernel, z, line),
        out_shape=outs,
        in_specs=[edge] * 6 + [anywhere] * 4,
        out_specs=[anywhere] * 2 + [edge] * 6 + [anywhere] * (len(outs) - 8),
        scratch_shapes=scratch_shapes,
        compiler_params=pltpu.CompilerParams(
            collective_id=0, has_side_effects=True, vmem_limit_bytes=VMEM_BYTES
        ),
        name="step",
    )(*args)
    return outs[:8]


def body(
    inputs,
    positions,
    projections,
    out_projections,
    ffn_up,
    ffn_down,
    norm_gains,
    segments,
    levels,
    cotangent,
):
    micro, _, length, width = inputs.shape[1:]
    ranks = lax.axis_size("dp")
    per, n_gains = width // ranks, norm_gains.shape[1]
    z = sizes(length, width, ffn_up.shape[2], micro, ranks)
    rows = (inputs[0, :, 0], cotangent[:, 0], segments, levels)
    line = ranks == 4 * LINE and per * 4 == PAIR and n_gains <= 8
    if line:
        gain = norm_gains.transpose(1, 0, 2)
        given = (projections[0], out_projections[0], ffn_up[0], ffn_down[0], positions[0].T, gain)
        results = [shape(item.shape, F32) for item in given]
        whole, g_in, d_proj, d_out, d_up, d_down, d_table, d_gain = run_step(z, True, given, results, *rows)
        d_table, d_gain = d_table.T[None], d_gain.transpose(1, 0, 2)
    else:
        every = lambda value, axis: lax.all_gather(value.astype(BF), "dp", axis=axis, tiled=True)
        part = lambda value, axis: lax.psum_scatter(value, "dp", scatter_dimension=axis, tiled=True)
        to_section = lambda value, source: lax.ppermute(value, "section", [(source, 1 - source)])
        proj, outp = projections[0].astype(BF), out_projections[0].astype(BF)
        mine = jnp.stack([proj[3], outp[1]])
        gains = every(norm_gains[0], 1).astype(F32)
        given = (
            every(jnp.stack([proj[0], proj[1], proj[2], outp[0]]), 1),
            every(jnp.concatenate([mine, to_section(mine, 0)]), 1),
            every(ffn_up[0], 0), every(ffn_down[0], 0), every(positions[0], 1),
            jnp.concatenate([gains, jnp.zeros((8 - n_gains, width), F32)]),
        )
        results = [z[name] for name in ("mats", "mats", "up", "down", "packed", "gains")]
        whole, g_in, d_mats, d_cross, d_up, d_down, d_table, d_gain = run_step(z, False, given, results, *rows)
        d_mats, d_cross = part(d_mats, 1).astype(F32), part(d_cross, 1)
        back = to_section(d_cross[2:], 1)
        more = jnp.where(lax.axis_index("section") == 0, back, d_cross[:2]).astype(F32)
        d_proj = jnp.concatenate([d_mats[:3], more[:1]])
        d_out = jnp.concatenate([d_mats[3:], more[1:]])
        d_up, d_down = part(d_up, 0).astype(F32), part(d_down, 0).astype(F32)
        d_table = part(d_table, 0)[0].astype(F32).T[None]
        d_gain = part(d_gain, 1)[None, :n_gains]
    return (
        whole[None, :, None],
        g_in[None, :, None],
        d_table,
        d_proj[None],
        d_out[None],
        d_up[None],
        d_down[None],
        d_gain,
    )


def solution(mesh):
    in_specs = (
        P("section", None, "dp", None, None),
        P("section", None, "dp"),
        P("section", None, "dp", None),
        P("section", None, "dp", None),
        P("section", "dp", None),
        P("section", "dp", None),
        P("section", None, "dp"),
        P(None, "dp", None),
        P(None, None, "dp", None),
        P(None, "dp", None, None),
    )
    out_specs = (
        P("section", None, "dp", None, None),
        P("section", None, "dp", None, None),
        P("section", None, "dp"),
        P("section", None, "dp", None),
        P("section", None, "dp", None),
        P("section", "dp", None),
        P("section", "dp", None),
        P("section", None, "dp"),
    )
    return jax.shard_map(body, mesh=mesh, in_specs=in_specs, out_specs=out_specs, check_vma=False)
```

```python
from functools import partial

import jax
import jax.numpy as jnp
from jax import lax
from jax.experimental import pallas as pl
from jax.experimental.pallas import tpu as pltpu
from jax.sharding import PartitionSpec as P

BF = jnp.bfloat16
F32 = jnp.float32
DH = 64
PAIR = 2 * DH
QB = 128
WIN = 256
TB = 256
MESH = pl.DeviceIdType.MESH
VMEM_BYTES = 62 * 1024 * 1024


def nn(left, right):
    return jnp.dot(left, right, preferred_element_type=F32)


def nt(left, right):
    return lax.dot_general(left, right, (((1,), (1,)), ((), ())), preferred_element_type=F32)


def tn(left, right):
    return lax.dot_general(left, right, (((0,), (0,)), ((), ())), preferred_element_type=F32)


def norm_parts(stream):
    centred = stream - jnp.mean(stream, axis=-1, keepdims=True)
    scale = lax.rsqrt(jnp.mean(centred * centred, axis=-1, keepdims=True) + 1e-05)
    return centred * scale, scale


def norm_back(grad, unit, scale, gain):
    inner = grad * gain
    first = jnp.mean(inner, axis=-1, keepdims=True)
    second = jnp.mean(inner * unit, axis=-1, keepdims=True)
    return scale * (inner - first - unit * second), jnp.sum(grad * unit, axis=0, keepdims=True)


def block_at(index, size):
    if isinstance(index, int):
        return pl.ds(index * size, size)
    return pl.ds(pl.multiple_of(index * size, size), size)


def lane_halves(scale=1.0):
    lane = lax.broadcasted_iota(jnp.int32, (1, PAIR), 1)
    low = jnp.where(lane < DH, scale, 0.0).astype(BF)
    high = jnp.where(lane < DH, 0.0, scale).astype(BF)
    return low, high


def both_heads(block, halves):
    return jnp.concatenate([block * halves[0], block * halves[1]], axis=0)


def join_heads(stacked):
    lane = lax.broadcasted_iota(jnp.int32, (QB, PAIR), 1)
    return jnp.where(lane < DH, stacked[:QB], stacked[QB:])


def window_start(index, length):
    return pl.multiple_of(jnp.clip(index * QB - DH, 0, length - WIN), DH)


def make_codes(segments, source_level, target_level, codes_ref, cols_ref):
    segment = segments[...]
    length = segment.shape[1]
    before = pltpu.roll(segment, 1, axis=1)
    lane = lax.broadcasted_iota(jnp.int32, (1, length), 1)
    first = (lane == 0) | (segment != before)
    usable = jnp.where(first | (source_level[...] > 0), segment, -1)
    row = lax.broadcasted_iota(jnp.int32, (8, length), 0)
    codes = jnp.where(row == 0, usable, jnp.where(row == 1, segment, target_level[...]))
    codes_ref[...] = codes
    cols_ref[...] = codes.T


def mask_bias(index, start, codes_ref, cols_ref, causal):
    keys = cols_ref[pl.ds(start, WIN), :]
    queries = codes_ref[:, block_at(index, QB)]
    query_segment = queries[1:2, :]
    if causal:
        key_id = start + lax.broadcasted_iota(jnp.int32, (WIN, QB), 0)
        query_id = index * QB + lax.broadcasted_iota(jnp.int32, (WIN, QB), 1)
        allowed = (keys[:, 1:2] == query_segment) & (
            (keys[:, 2:3] < queries[2:3, :]) | (key_id == query_id)
        )
    else:
        allowed = keys[:, 0:1] == query_segment
    bias = jnp.where(allowed, 0.0, -1e30)
    return jnp.concatenate([bias, bias], axis=1)


def attend_block(index, q_ref, k_ref, v_ref, codes_ref, cols_ref, weights_ref, mixed_ref, causal):
    length, width = q_ref.shape
    start = window_start(index, length)
    rows = block_at(index, QB)
    bias = mask_bias(index, start, codes_ref, cols_ref, causal)
    halves = lane_halves(DH ** -0.5)
    for pair in range(width // PAIR):
        lanes = slice(pair * PAIR, (pair + 1) * PAIR)
        queries = both_heads(q_ref[rows, lanes], halves)
        scores = nt(k_ref[pl.ds(start, WIN), lanes], queries) + bias
        shifted = jnp.exp(scores - jnp.max(scores, axis=0, keepdims=True))
        weights = (shifted * (1.0 / jnp.sum(shifted, axis=0, keepdims=True))).astype(BF)
        weights_ref[index, pair] = weights
        out = tn(weights, v_ref[pl.ds(start, WIN), lanes])
        mixed_ref[rows, lanes] = join_heads(out).astype(BF)


def attend_back_block(
    index, q_ref, k_ref, v_ref, weights_ref, mixed_ref, dmixed_ref, dq_ref, dk_ref, dv_ref
):
    length, width = q_ref.shape
    start = window_start(index, length)
    rows = block_at(index, QB)
    window = pl.ds(start, WIN)
    plain = lane_halves()
    halves = lane_halves(DH ** -0.5)
    ones = jnp.ones((WIN, PAIR), BF)
    for pair in range(width // PAIR):
        lanes = slice(pair * PAIR, (pair + 1) * PAIR)
        queries = both_heads(q_ref[rows, lanes], halves)
        keys = k_ref[window, lanes]
        values = v_ref[window, lanes]
        weights = weights_ref[index, pair]
        dmixed = dmixed_ref[rows, lanes]
        grads = both_heads(dmixed, plain)
        inner = (dmixed.astype(F32) * mixed_ref[rows, lanes].astype(F32) * -1.0).astype(BF)
        left = jnp.concatenate([values, ones], axis=1)
        right = jnp.concatenate([grads, both_heads(inner, plain)], axis=1)
        centred = nt(left, right)
        dscores = (weights.astype(F32) * centred).astype(BF)
        dv_ref[window, lanes] += nn(weights, grads)
        dk_ref[window, lanes] += nn(dscores, queries)
        dq = tn(dscores, keys) * (DH ** -0.5)
        dq_ref[rows, lanes] = join_heads(dq).astype(BF)


def gelu_parts(value):
    cdf = 0.5 + 0.5 * lax.erf(value * (0.5 ** 0.5))
    density = jnp.exp(value * value * -0.5) * 0.3989422804014327
    return value * cdf, cdf + value * density


def feed_block(normed, up_ref, down_ref, hidden_ref, slope_ref, rows):
    total = None
    width = up_ref.shape[1]
    step = 512
    for at in range(0, width, step):
        hidden, slope = gelu_parts(nn(normed, up_ref[:, at : at + step]))
        hidden = hidden.astype(BF)
        hidden_ref[rows, at : at + step] = hidden
        slope_ref[rows, at : at + step] = slope.astype(BF)
        term = nn(hidden, down_ref[at : at + step, :])
        total = term if total is None else total + term
    return total


def feed_back_block(grad, up_ref, down_ref, slope_ref, rows):
    total = None
    width = up_ref.shape[1]
    step = 512
    for at in range(0, width, step):
        dhidden = nt(grad, down_ref[at : at + step, :])
        dup = (dhidden * slope_ref[rows, at : at + step].astype(F32)).astype(BF)
        slope_ref[rows, at : at + step] = dup
        term = nt(dup, up_ref[:, at : at + step])
        total = term if total is None else total + term
    return total


class Queue:
    def __init__(self):
        self.steps = []

    def add(self, *groups):
        self.steps.extend(groups)

    def next(self):
        while self.steps and isinstance(self.steps[0], int):
            self.steps.pop(0)
        return self.steps.pop(0) if self.steps else None

    def flush(self, mark=None):
        if mark is not None and mark not in self.steps:
            return
        while self.steps:
            step = self.steps.pop(0)
            if step == mark and mark is not None:
                return
            if callable(step):
                step()


def loop(count, body, queue=None):
    hooks = [queue.next() if queue else None for _ in range(count)]

    def step(index, carry):
        body(index)
        for turn, hook in enumerate(hooks):
            if hook is not None:
                pl.when(index == turn)(hook)
        return carry

    lax.fori_loop(0, count, step, 0)


def put_grad(out, index, value):
    if out.prior is not None:
        value = value + out.buf[index].astype(F32)
    out.buf[index] = value.astype(BF)


def weight_grad(out, left_t_refs, right_refs, transposed):
    step = 512
    width = right_refs[0].shape[1]

    def slab(index):
        cols = block_at(index, step)
        value = None
        for left_t, right in zip(left_t_refs, right_refs):
            term = nn(left_t[...], right[:, cols])
            value = term if value is None else value + term
        if transposed:
            put_grad(out, (cols, slice(None)), value.T)
        else:
            put_grad(out, (slice(None), cols), value)

    loop(width // step, slab)


def put_table(out, rows, value):
    value = value.T.reshape(out.buf.shape[:2] + (value.shape[0],))
    put_grad(out, (slice(None), slice(None), rows), value)


def add_gain(out, row, value):
    out.buf[row : row + 1, :] += value


class Source:
    def __init__(self, hbm, buf, sem):
        self.buf, self.copy, self.here = buf, pltpu.make_async_copy(hbm, buf, sem), False
        self.copy.start()

    def __call__(self):
        if not self.here:
            self.copy.wait()
            self.here = True
        return self.buf


class Sink:
    def __init__(self, hbm, buf, sems, first, parts, axis, prior):
        self.hbm, self.buf, self.sems, self.first = hbm, buf, sems, first
        self.parts, self.axis, self.prior = parts, axis, prior

    def copy(self, part):
        view = [slice(None)] * len(self.buf.shape)
        size = self.buf.shape[self.axis] // self.parts
        view[self.axis] = block_at(part, size)
        view = tuple(view)
        return pltpu.make_async_copy(
            self.buf.at[view], self.hbm.at[view], self.sems.at[self.first + part]
        )

    def send(self, part=0):
        self.copy(part).start()

    def wait(self):
        for part in range(self.parts):
            self.copy(part).wait()


class Ready:
    def __init__(self, buf, before=None):
        self.buf, self.before = buf, before

    def __call__(self):
        if self.before is not None:
            self.before()
            self.before = None
        return self.buf


class Total:
    def __init__(self, buf, first):
        self.buf = buf
        self.prior = None if first else buf


class Link:
    def __init__(self, outbox, inbox, send, recv, parts):
        self.buf, self.inbox, self.sems, self.parts = outbox, inbox, (send, recv), parts

    def copy(self, part):
        size = self.buf.shape[0] // self.parts
        rows = block_at(part, size)
        return pltpu.make_async_remote_copy(
            src_ref=self.buf.at[rows, :], dst_ref=self.inbox.at[rows, :],
            send_sem=self.sems[0].at[part], recv_sem=self.sems[1].at[part],
            device_id={"section": 1 - lax.axis_index("section")}, device_id_type=MESH,
        )

    def send(self, part):
        self.copy(part).start()

    def wait(self):
        for part in range(self.parts):
            self.copy(part).wait_send()

    def come(self, part):
        self.copy(part).wait_recv()


def encode_attend(src, table, gains, segments, source_level, target_level, mats, qkv, weights, mixed, codes, cols, queue):
    length = src.buf.shape[0]
    make_codes(segments(), source_level(), target_level(), codes, cols)
    src, table, gains, mats = src(), table(), gains(), mats()

    def project(index):
        rows = block_at(index, TB)
        unit, _ = norm_parts(src[rows, :].astype(F32) + table[rows, :].astype(F32))
        normed = (unit * gains[0:1, :]).astype(BF)
        for which in range(3):
            qkv.buf[which, rows, :] = nn(normed, mats[which]).astype(BF)
        qkv.send(index)

    loop(length // TB, project, queue)

    def attend(index):
        for part in range(TB // QB):
            attend_block(
                index * (TB // QB) + part,
                qkv.buf.at[0], qkv.buf.at[1], qkv.buf.at[2], codes, cols, weights.buf, mixed.buf, False,
            )
        weights.send(index)
        mixed.send(index)

    loop(length // TB, attend, queue)


def encode_feed(src, mixed, table, gains, mats, up, down, mem, x1, x2, hidden, slope):
    length = src.buf.shape[0]
    table, gains, mats, up, down = table(), gains(), mats(), up(), down()
    src, mixed = src(), mixed()

    def rest(index):
        rows = block_at(index, TB)
        stream = src[rows, :].astype(F32) + table[rows, :].astype(F32)
        stream = stream + nn(mixed[rows, :], mats[3])
        x1.buf[rows, :] = stream
        x1.send(index)
        unit, _ = norm_parts(stream)
        normed = (unit * gains[1:2, :]).astype(BF)
        stream = stream + feed_block(normed, up, down, hidden.buf, slope.buf, rows)
        x2.buf[rows, :] = stream
        unit, _ = norm_parts(stream)
        mem.buf[rows, :] = (unit * gains[2:3, :]).astype(BF)
        for item in (mem, x2, hidden, slope):
            item.send(index)

    loop(length // TB, rest)


def encode_back(
    x2, dmem, gains, slope, down, up, x1, mats, hidden, mixed, qkv, weights, src, table,
    g_in, g_mats, g_up, g_down, g_table, g_gains,
    dy, dy_t, a_t, dx, dmixed, dq, dk, dv, queue, fed,
):
    length = src.buf.shape[0]
    if g_gains.prior is None:
        g_gains.buf[...] = jnp.zeros_like(g_gains.buf)
    x2, gains, slope, down, up, x1, mats = x2(), gains(), slope(), down(), up(), x1(), mats()

    def feed_step(index):
        rows = block_at(index, TB)
        dmem.come(index)
        unit, scale = norm_parts(x2[rows, :])
        grad, d_gain = norm_back(dmem.inbox[rows, :].astype(F32), unit, scale, gains[2:3, :])
        add_gain(g_gains, 2, d_gain)
        low = grad.astype(BF)
        dy_t[:, rows] = low.T
        dnormed = feed_back_block(low, up, down, slope, rows)
        unit, scale = norm_parts(x1[rows, :])
        a_t[:, rows] = (unit * gains[1:2, :]).astype(BF).T
        back, d_gain = norm_back(dnormed, unit, scale, gains[1:2, :])
        add_gain(g_gains, 1, d_gain)
        grad = grad + back
        dx[rows, :] = grad
        low = grad.astype(BF)
        dy[rows, :] = low
        dmixed[rows, :] = nt(low, mats[3]).astype(BF)

    loop(length // TB, feed_step)
    weight_grad(g_up, [a_t], [slope], False)
    weight_grad(g_down, [dy_t], [hidden()], True)
    mixed = mixed()
    put_grad(g_mats, 3, tn(mixed[...], dy[...]))
    fed()
    qkv, weights = qkv(), weights()
    dk[...] = jnp.zeros_like(dk)
    dv[...] = jnp.zeros_like(dv)

    def attend_step(index):
        attend_back_block(
            index, qkv.at[0], qkv.at[1], qkv.at[2], weights, mixed, dmixed, dq, dk, dv
        )

    loop(length // QB, attend_step, queue)
    src, table = src(), table()

    def project_step(index):
        rows = block_at(index, TB)
        unit, scale = norm_parts(src[rows, :].astype(F32) + table[rows, :].astype(F32))
        a_t[:, rows] = (unit * gains[0:1, :]).astype(BF).T
        dnormed = nt(dq[rows, :], mats[0])
        dnormed += nt(dk[rows, :].astype(BF), mats[1])
        dnormed += nt(dv[rows, :].astype(BF), mats[2])
        back, d_gain = norm_back(dnormed, unit, scale, gains[0:1, :])
        add_gain(g_gains, 0, d_gain)
        grad = dx[rows, :] + back
        g_in.buf[rows, :] = grad
        g_in.send(index)
        put_table(g_table, rows, grad)

    loop(length // TB, project_step, queue)
    put_grad(g_mats, 0, nn(a_t[...], dq[...]))
    put_grad(g_mats, 1, nn(a_t[...], dk[...].astype(BF)))
    put_grad(g_mats, 2, nn(a_t[...], dv[...].astype(BF)))


def self_forward(tgt, table, gains, segments, source_level, target_level, mats, qkv, weights, mixed, h1, codes, cols, queue):
    length = tgt.buf.shape[0]
    make_codes(segments(), source_level(), target_level(), codes, cols)
    tgt, table, gains, mats = tgt(), table(), gains(), mats()

    def project(index):
        rows = block_at(index, TB)
        stream = table[rows, :].astype(F32)
        unit, _ = norm_parts(stream)
        qkv.buf[0, rows, :] = nn((unit * gains[0:1, :]).astype(BF), mats[0]).astype(BF)
        unit, _ = norm_parts(tgt[rows, :].astype(F32) + stream)
        normed = (unit * gains[0:1, :]).astype(BF)
        for which in (1, 2):
            qkv.buf[which, rows, :] = nn(normed, mats[which]).astype(BF)
        qkv.send(index)

    loop(length // TB, project, queue)

    def rest(index):
        for part in range(TB // QB):
            attend_block(
                index * (TB // QB) + part,
                qkv.buf.at[0], qkv.buf.at[1], qkv.buf.at[2], codes, cols, weights.buf, mixed.buf, True,
            )
        rows = block_at(index, TB)
        h1.buf[rows, :] = table[rows, :].astype(F32) + nn(mixed.buf[rows, :], mats[3])
        for item in (weights, mixed, h1):
            item.send(index)

    loop(length // TB, rest, queue)


def self_back(
    dh1, mats, mixed, qkv, weights, tgt, table, gains,
    g_in, g_mats, g_table, g_gains,
    dy, a_t, b_t, dmixed, dq, dk, dv, queue,
):
    length = tgt.buf.shape[0]
    dk[...] = jnp.zeros_like(dk)
    dv[...] = jnp.zeros_like(dv)
    dh1, mats, mixed = dh1(), mats(), mixed()

    def out_step(index):
        rows = block_at(index, TB)
        low = dh1[rows, :].astype(BF)
        dy[rows, :] = low
        dmixed[rows, :] = nt(low, mats[3]).astype(BF)

    loop(length // TB, out_step)
    put_grad(g_mats, 3, tn(mixed[...], dy[...]))
    qkv, weights = qkv(), weights()

    def attend_step(index):
        attend_back_block(
            index, qkv.at[0], qkv.at[1], qkv.at[2], weights, mixed, dmixed, dq, dk, dv
        )

    loop(length // QB, attend_step, queue)
    tgt, table, gains = tgt(), table(), gains()

    def project_step(index):
        rows = block_at(index, TB)
        stream = table[rows, :].astype(F32)
        unit, scale = norm_parts(stream)
        a_t[:, rows] = (unit * gains[0:1, :]).astype(BF).T
        back, d_gain = norm_back(nt(dq[rows, :], mats[0]), unit, scale, gains[0:1, :])
        dtable = dh1[rows, :] + back
        unit, scale = norm_parts(tgt[rows, :].astype(F32) + stream)
        b_t[:, rows] = (unit * gains[0:1, :]).astype(BF).T
        dnormed = nt(dk[rows, :].astype(BF), mats[1])
        dnormed += nt(dv[rows, :].astype(BF), mats[2])
        back, d_gain_too = norm_back(dnormed, unit, scale, gains[0:1, :])
        add_gain(g_gains, 0, d_gain + d_gain_too)
        g_in.buf[rows, :] = back
        g_in.send(index)
        put_table(g_table, rows, dtable + back)

    loop(length // TB, project_step, queue)
    put_grad(g_mats, 0, nn(a_t[...], dq[...]))
    put_grad(g_mats, 1, nn(b_t[...], dk[...].astype(BF)))
    put_grad(g_mats, 2, nn(b_t[...], dv[...].astype(BF)))


def feed_grads(a_t, dup, cot, hidden, g_up, g_down, cot_t):
    cot_t[...] = cot()[...].T
    weight_grad(g_up, [a_t()], [dup()], False)
    weight_grad(g_down, [cot_t], [hidden()], True)


def cross(
    h1, gains, segments, source_level, target_level, mats, mem, up, down, cot,
    out, dmem, dh1, g_mats, g_gains, a_t, dup, hidden,
    codes, cols, qkv, weights, mixed, h2, dy, b_t, dmixed, dq, dk, dv,
):
    length = h1.buf.shape[0]
    make_codes(segments(), source_level(), target_level(), codes, cols)
    if g_gains.prior is None:
        g_gains.buf[...] = jnp.zeros_like(g_gains.buf)
    dk[...] = jnp.zeros_like(dk)
    dv[...] = jnp.zeros_like(dv)
    h1, gains, mats = h1(), gains(), mats()
    memory = mem.inbox

    def project(index):
        rows = block_at(index, TB)
        unit, _ = norm_parts(h1[rows, :])
        qkv[0, rows, :] = nn((unit * gains[1:2, :]).astype(BF), mats[0]).astype(BF)
        mem.come(index)
        qkv[1, rows, :] = nn(memory[rows, :], mats[2]).astype(BF)
        qkv[2, rows, :] = nn(memory[rows, :], mats[3]).astype(BF)

    loop(length // TB, project)
    up, down, cot = up(), down(), cot()

    def middle(index):
        for part in range(TB // QB):
            attend_block(
                index * (TB // QB) + part,
                qkv.at[0], qkv.at[1], qkv.at[2], codes, cols, weights, mixed, False,
            )
        rows = block_at(index, TB)
        stream = h1[rows, :] + nn(mixed[rows, :], mats[1])
        unit, scale = norm_parts(stream)
        normed = (unit * gains[2:3, :]).astype(BF)
        a_t.buf[:, rows] = normed.T
        fed = feed_block(normed, up, down, hidden.buf, dup.buf, rows)
        out.buf[rows, :] = (stream + fed).astype(BF)
        low = cot[rows, :]
        dnormed = feed_back_block(low, up, down, dup.buf, rows)
        back, d_gain = norm_back(dnormed, unit, scale, gains[2:3, :])
        add_gain(g_gains, 2, d_gain)
        grad = low.astype(F32) + back
        h2[rows, :] = grad
        low = grad.astype(BF)
        dy[rows, :] = low
        dmixed[rows, :] = nt(low, mats[1]).astype(BF)
        for item in (out, hidden, dup):
            item.send(index)

    loop(length // TB, middle)
    a_t.send()

    def attend_step(index):
        def one(at):
            attend_back_block(at, qkv.at[0], qkv.at[1], qkv.at[2], weights, mixed, dmixed, dq, dk, dv)

        steps = TB // QB
        last = length // TB - 1
        pl.when(index == 0)(lambda: one(0))
        for part in range(1, steps):
            one(index * steps + part)
        pl.when(index < last)(lambda: one((index + 1) * steps))
        rows = block_at(index, TB)
        dkeys = dk[rows, :].astype(BF)
        dvalues = dv[rows, :].astype(BF)
        dmem.buf[rows, :] = (nt(dkeys, mats[2]) + nt(dvalues, mats[3])).astype(BF)
        dmem.send(index)

    loop(length // TB, attend_step)

    def project_step(index):
        rows = block_at(index, TB)
        unit, scale = norm_parts(h1[rows, :])
        b_t[:, rows] = (unit * gains[1:2, :]).astype(BF).T
        back, d_gain = norm_back(nt(dq[rows, :], mats[0]), unit, scale, gains[1:2, :])
        add_gain(g_gains, 1, d_gain)
        dh1.buf[rows, :] = h2[rows, :] + back
        dh1.send(index)

    loop(length // TB, project_step)
    put_grad(g_mats, 0, nn(b_t[...], dq[...]))
    put_grad(g_mats, 1, tn(mixed[...], dy[...]))
    put_grad(g_mats, 2, tn(memory[...], dk[...].astype(BF)))
    put_grad(g_mats, 3, tn(memory[...], dv[...].astype(BF)))


def shape(dims, kind):
    return jax.ShapeDtypeStruct(dims, kind)


def sizes(length, width, ff, micro, ranks):
    blocks = length // QB
    pairs = width // PAIR
    return dict(
        tok=shape((length, width), BF),
        tok32=shape((length, width), F32),
        outputs=shape((micro, length, width), BF),
        g_in=shape((micro, length, width), F32),
        qkv=shape((3, length, width), BF),
        weights=shape((blocks, pairs, WIN, 2 * QB), BF),
        hidden=shape((length, ff), BF),
        tokt=shape((width, length), BF),
        packed=shape((ranks, width // ranks, length), BF),
        packed_gains=shape((ranks, 16, PAIR), BF),
        mats=shape((4, width, width), BF),
        up=shape((width, ff), BF),
        down=shape((ff, width), BF),
        gains=shape((8, width), F32),
        pair=shape((2, width, width), BF),
        row=shape((1, length), jnp.int32),
        codes=shape((8, length), jnp.int32),
        cols=shape((length, 8), jnp.int32),
    )


LINE = 4
AHEAD = (2, 1, 3, 0)
TABLE, GAIN, MATS, UP, DOWN, CROSS, OUT = range(7)
KINDS = 7


def rank_of(z, x, core):
    return z * 4 + x * 2 + core


def remote(src, dst, send, recv, to):
    return pltpu.make_async_remote_copy(
        src_ref=src, dst_ref=dst, send_sem=send, recv_sem=recv, device_id=to, device_id_type=MESH
    )


def rows_at(ref, per, rank):
    view = [slice(None)] * len(ref.shape)
    view[-2] = pl.ds(pl.multiple_of(rank * per, 16), per)
    return ref.at[tuple(view)]


class Place:
    def __init__(self):
        me = lax.axis_index("dp")
        self.z, self.x, self.core = me // 4, (me // 2) % 2, me % 2
        self.rank = me
        self.section = lax.axis_index("section")
        self.partner = {"section": 1 - self.section}
        self.across = {"dp": rank_of(self.z, 1 - self.x, self.core)}
        self.sibling = {"dp": rank_of(self.z, self.x, 1 - self.core)}

    def ahead(self, step):
        return (self.z + step) % LINE

    def on_line(self, step):
        return {"dp": rank_of(self.ahead(step), self.x, self.core)}

    def line(self, other):
        return 1 - self.x if other else self.x

    def meet(self, semaphore, also=()):
        devices = [self.across, self.sibling, *also] + [self.on_line(step) for step in range(1, LINE)]
        for device in devices:
            pl.semaphore_signal(semaphore, inc=1, device_id=device, device_id_type=MESH)
        pl.semaphore_wait(semaphore, len(devices))


class Gather:
    def __init__(self, place, kind, view, sems):
        self.place, self.kind, self.view = place, kind, view
        self.zsend, self.zrecv, self.xsend, self.xrecv, self.csend, self.crecv = sems

    def block(self, back, other):
        place = self.place
        return self.view(rank_of(place.ahead(LINE - back), place.line(other), place.core))

    def along(self, step):
        at, block = (self.kind, step - 1), self.block(0, 0)
        return remote(block, block, self.zsend.at[at], self.zrecv.at[at], self.place.on_line(step))

    def over(self, back):
        at, block = (self.kind, back), self.block(back, 0)
        return remote(block, block, self.xsend.at[at], self.xrecv.at[at], self.place.across)

    def beside(self, back, other):
        at, block = (self.kind, back + LINE * other), self.block(back, other)
        return remote(block, block, self.csend.at[at], self.crecv.at[at], self.place.sibling)

    def begin_along(self):
        for step in (1, 3, 2):
            self.along(step).start()

    def begin_over(self):
        self.over(0).start()
        self.beside(0, 0).start()

    def pass_on(self, back):
        self.along(back).wait_recv()
        self.over(back).start()
        self.beside(back, 0).start()

    def share(self, back):
        self.over(back).wait_recv()
        self.beside(back, 1).start()

    def finish(self):
        for step in range(1, LINE):
            self.along(step).wait_send()
        for back in range(LINE):
            self.over(back).wait_send()
            for other in range(2):
                copy = self.beside(back, other)
                copy.wait_send()
                copy.wait_recv()


def passing(arrays):
    return [partial(array.pass_on, back) for back in (1, 3, 2) for array in arrays]


def sharing(arrays):
    return [partial(array.share, back) for back in (0, 1, 3, 2) for array in arrays]


def in_groups(steps, size):
    def group(some):
        return lambda: [step() for step in some] and None

    return [group(steps[at : at + size]) for at in range(0, len(steps), size)]


class Scatter:
    def __init__(self, place, kind, view, slots, sems):
        self.place, self.kind, self.view, self.slots = place, kind, view, slots
        self.zsend, self.zrecv, self.xsend, self.xrecv, self.csend, self.crecv = sems

    def from_core(self, step, part):
        return self.slots(step * 2 + part)

    def from_x(self, step):
        return self.slots(2 * LINE + step)

    def from_z(self, step):
        return self.slots(3 * LINE + step - 1)

    def own(self, step, part, its_core):
        return self.view(rank_of(self.place.ahead(step), self.place.line(1 - part), its_core))

    def beside(self, step, part):
        at = (self.kind, step, part)
        return remote(
            self.own(step, part, 1 - self.place.core), self.from_core(step, part), self.csend.at[at],
            self.crecv.at[at], self.place.sibling,
        )

    def over(self, step):
        at = (self.kind, step)
        return remote(
            self.from_core(step, 0), self.from_x(step), self.xsend.at[at], self.xrecv.at[at],
            self.place.across,
        )

    def along(self, step):
        at = (self.kind, step - 1)
        return remote(
            self.from_core(step, 1), self.from_z(step), self.zsend.at[at], self.zrecv.at[at],
            self.place.on_line(step),
        )

    def total(self, *terms):
        value = terms[0][...].astype(F32)
        for term in terms[1:]:
            value = value + term[...].astype(F32)
        return value

    def begin(self):
        for part in range(2):
            for step in AHEAD:
                self.beside(step, part).start()

    def first(self, step):
        self.beside(step, 0).wait_recv()
        both = self.from_core(step, 0)
        both[...] = self.total(both, self.own(step, 0, self.place.core)).astype(BF)
        self.over(step).start()

    def second(self, step):
        self.beside(step, 1).wait_recv()
        self.over(step).wait_recv()
        four = self.from_core(step, 1)
        four[...] = self.total(four, self.own(step, 1, self.place.core), self.from_x(step)).astype(BF)
        if step:
            self.along(step).start()

    def finish(self, put):
        for step in range(1, LINE):
            self.along(step).wait_recv()
        put(self.total(self.from_core(0, 1), *[self.from_z(step) for step in range(1, LINE)]))
        for step in range(LINE):
            self.over(step).wait_send()
            if step:
                self.along(step).wait_send()
            for part in range(2):
                self.beside(step, part).wait_send()


def firsts(arrays):
    return [partial(array.first, step) for step in AHEAD for array in arrays]


def seconds(arrays):
    return [partial(array.second, step) for step in AHEAD for array in arrays]


POOL = (("row", 3), ("tok", 6), ("tok32", 4), ("tokt", 2), ("qkv", 1), ("weights", 1), ("hidden", 2))
KEPT = ("qkv", "weights", "tok", "tok32", "tok32", "hidden", "hidden", "tokt")
PERSISTENT = (
    "tok", "gains", "mats", "up", "down", "mats", "mats", "mats", "up", "down", "packed", "gains", "codes",
    "cols", "outputs", "outputs",
)


def step_kernel(z, line, *refs):
    refs = list(refs)
    take = lambda count: [refs.pop(0) for _ in range(count)]
    given, (own, cot, segments, levels) = take(6), take(4)
    whole, g_in = take(2)
    results = take(6)
    micro, length = own.shape[:2]
    parts = length // TB
    kept = [take(len(KEPT)) for _ in range(micro)]
    (
        v_table, v_gains, v_mats, v_up, v_down, v_cross, s_mats, s_cross, s_up, s_down, s_table, s_gains,
        codes, cols, inbox, outbox,
    ) = take(len(PERSISTENT))
    pool = {name: take(count) for name, count in POOL}
    local, ysend, yrecv = take(3)
    section = lax.axis_index("section")
    count = [0]

    def sems(number):
        count[0] += number
        return count[0] - number

    def load(hbm, buf):
        return Source(hbm, buf, local.at[sems(1)])

    def store(hbm, buf, axis=0, split=True):
        number = parts if split else 1
        return Sink(hbm, buf, local, sems(number), number, axis, None)

    def box(m):
        return Link(outbox.at[m], inbox.at[m], ysend.at[m], yrecv.at[m], parts)

    def code_loads(m):
        hbm = (segments.at[m], levels.at[0, m], levels.at[1, m])
        return [load(ref, buf) for ref, buf in zip(hbm, pool["row"])]

    queue = Queue()
    if line:
        o_proj, o_out, o_up, o_down, o_table, o_gain = results
        r_mats, r_gains, packed_gains, handing, handed = take(5)
        g_sems, s_sems = take(6), take(6)
        ready, shard_sems, hand_sems = refs
        place = Place()
        per, n_gains = o_table.shape[0], o_gain.shape[0]
        ranks = s_table.shape[0]
        rank, lent = place.rank, slice(2, 4)

        view_of = {
            TABLE: lambda at: s_table.at[at],
            GAIN: lambda at: packed_gains.at[at],
            MATS: lambda at: rows_at(v_mats, per, at),
            UP: lambda at: rows_at(v_up, per, at),
            DOWN: lambda at: rows_at(v_down, o_down.shape[0], at),
            CROSS: lambda at: rows_at(v_cross, per, at),
        }
        gathers = {kind: Gather(place, kind, view, g_sems) for kind, view in view_of.items()}
        sum_of = {
            TABLE: lambda at: s_table.at[at],
            GAIN: lambda at: packed_gains.at[at],
            MATS: lambda at: rows_at(s_mats.at[0:3], per, at),
            UP: lambda at: rows_at(s_up, per, at),
            DOWN: lambda at: rows_at(s_down, o_down.shape[0], at),
            CROSS: lambda at: rows_at(s_cross, per, at),
            OUT: lambda at: rows_at(s_mats.at[3], per, at),
        }
        width = v_mats.shape[-1]
        hidden_0, hidden_1 = pool["hidden"]
        slots = 4 * LINE

        def in_hidden(buf, first, tall, wide):
            across = buf.shape[1] // wide

            def slot(number):
                row, lane = first + number // across * tall, number % across * wide
                return buf.at[row : row + tall, lane : lane + wide]

            return slot

        slot_of = {
            TABLE: in_hidden(hidden_0, slots * per, per, length),
            GAIN: lambda number: r_gains.at[number],
            MATS: lambda number: r_mats.at[number, 0:3],
            UP: in_hidden(hidden_0, 0, per, hidden_0.shape[1]),
            DOWN: in_hidden(hidden_1, 0, o_down.shape[0], width),
            CROSS: lambda number: r_mats.at[number],
            OUT: lambda number: r_mats.at[number, 3],
        }
        scatters = {
            kind: Scatter(place, kind, view, slot_of[kind], s_sems) for kind, view in sum_of.items()
        }

        p_proj, p_out, p_up, p_down, p_pos, p_gain = given
        s_table[rank] = p_pos[...].astype(BF)
        gain = jnp.concatenate([p_gain[...].reshape(n_gains, per), jnp.zeros((16 - n_gains, per), F32)], axis=0)
        packed_gains[rank] = jnp.concatenate([gain, jnp.zeros((16, PAIR - per), F32)], axis=1).astype(BF)
        own_mats = rows_at(v_mats, per, rank)
        for to, shard in enumerate((p_proj.at[0], p_proj.at[1], p_proj.at[2], p_out.at[0])):
            own_mats[to] = shard[...].astype(BF)
        own_cross = rows_at(v_cross, per, rank)
        for to, shard in enumerate((p_proj.at[3], p_out.at[1])):
            low = shard[...].astype(BF)
            own_cross[to] = low
            r_mats[0, to] = low
        place.meet(pltpu.get_barrier_semaphore(), (place.partner,))
        early = [gathers[kind] for kind in (GAIN, TABLE, MATS)]
        for item in early:
            item.begin_along()
            item.begin_over()
        lend = remote(
            r_mats.at[0, 0:2], own_cross.at[lent], shard_sems.at[0], shard_sems.at[1], place.partner
        )
        pl.when(section == 0)(lambda: lend.start())
        rows_at(v_up, per, rank)[...] = p_up[...].astype(BF)
        rows_at(v_down, o_down.shape[0], rank)[...] = p_down[...].astype(BF)
        for kind in (UP, DOWN):
            gathers[kind].begin_over()
        for step in passing(early):
            step()
        pl.when(section == 0)(lambda: gathers[UP].begin_along())

        @pl.when(section == 1)
        def _():
            lend.wait_recv()
            gathers[CROSS].begin_along()
            gathers[CROSS].begin_over()

        for step in sharing(early):
            step()
        for item in early[:2]:
            item.finish()
        v_gains[...] = jnp.zeros_like(v_gains)
        group = PAIR // per
        for first in range(0, ranks, group):
            at = slice(first * per, (first + group) * per)
            v_table[:, at] = jnp.concatenate([s_table[one] for one in range(first, first + group)], axis=0).T
            v_gains[:n_gains, at] = jnp.concatenate(
                [packed_gains[one, :n_gains, :per] for one in range(first, first + group)], axis=1
            ).astype(F32)
        early[2].finish()

        def weights_ready(kinds):
            def before():
                queue.flush(kinds[-1])
                for kind in kinds:
                    gathers[kind].finish()

            return before

        def put_mats(value):
            o_proj[0:3] = value

        def put_out(value):
            o_out[0] = value

        def put_up(value):
            o_up[...] = value

        def put_down(value):
            o_down[...] = value

        def put_pos(value):
            o_table[...] = value

        def put_gain(value):
            o_gain[...] = value[:n_gains, :per].reshape(n_gains, 1, per)

        def put_cross(value):
            o_proj[3] = value[0]
            o_out[1] = value[1]
            handing[...] = value[2:4]

        hand = remote(handing, handed, hand_sems.at[0], hand_sems.at[1], place.partner)

        def feed_sums():
            place.meet(ready.at[0])
            for kind in (UP, DOWN):
                scatters[kind].begin()

        def last_sums(late):
            for at in range(ranks):
                gain = s_gains[:, at * per : (at + 1) * per]
                gain = jnp.concatenate([gain, jnp.zeros((8, per), F32)], axis=0)
                packed_gains[at] = jnp.concatenate([gain, jnp.zeros((16, PAIR - per), F32)], axis=1).astype(BF)
            items = [scatters[kind] for kind in late]
            for item in items:
                item.begin()
            for step in firsts(items):
                step()
            queue.flush()
            for step in seconds(items):
                step()
            puts = {
                UP: put_up, DOWN: put_down, OUT: put_out, MATS: put_mats, TABLE: put_pos, GAIN: put_gain,
            }
            for kind, put in puts.items():
                scatters[kind].finish(put)
    else:
        partner = {"section": 1 - section}
        barrier = pltpu.get_barrier_semaphore()
        pl.semaphore_signal(barrier, inc=1, device_id=partner, device_id_type=MESH)
        pl.semaphore_wait(barrier, 1)

    def persistent():
        if line:
            return [Ready(buf) for buf in (v_table, v_gains, v_mats, v_up, v_down, v_cross)]
        order = (4, 5, 0, 2, 3, 1)
        return [
            load(given[at], buf) for at, buf in zip(order, (v_table, v_gains, v_mats, v_up, v_down, v_cross))
        ]

    def finish(items):
        for item in items:
            item.wait()

    @pl.when(section == 0)
    def _():
        count[0] = 0
        w_table, w_gains, w_mats, w_up, w_down, _ = first = persistent()
        if line:
            gathers[DOWN].begin_along()
            pair = [gathers[UP], gathers[DOWN]]
            queue.add(None, *passing(pair[:1]), *passing(pair[1:]), *sharing(pair), DOWN)
            w_up.before = weights_ready((UP, DOWN))
        base = count[0]
        src, mixed, dy, dmixed, dq = pool["tok"][:5]
        x1, x2, dx, dv = pool["tok32"]
        hidden, slope = pool["hidden"]
        dy_t, a_t = pool["tokt"]
        v_qkv, v_weights = pool["qkv"][0], pool["weights"][0]
        for m in range(micro):
            count[0] = base
            k_qkv, k_weights, k_mixed = kept[m][:3]
            sinks = [store(k_qkv, v_qkv, axis=1), store(k_weights, v_weights), store(k_mixed, mixed)]
            encode_attend(
                load(own.at[m], src), w_table, w_gains, *code_loads(m), w_mats, *sinks, codes, cols, queue
            )
            finish(sinks)
            if line and m == 0:
                lend.wait_send()
            count[0] = base
            _, _, k_mixed, k_x1, k_x2, k_hidden, k_slope, _ = kept[m]
            sinks = [store(k_x1, x1), store(k_x2, x2), store(k_hidden, hidden), store(k_slope, slope)]
            encode_feed(
                load(own.at[m], src), load(k_mixed, mixed), w_table, w_gains, w_mats, w_up, w_down, box(m),
                *sinks,
            )
            memory = pltpu.make_async_copy(outbox.at[m], whole.at[m], local.at[sems(1)])
            memory.start()
            finish(sinks + [memory])
        for m in range(micro):
            count[0] = base
            last = line and m == micro - 1
            k_qkv, k_weights, k_mixed, k_x1, k_x2, k_hidden, k_slope, _ = kept[m]
            loads = [load(k_x2, x2), load(k_slope, slope), load(k_x1, x1), load(k_hidden, hidden)]
            late = [load(k_mixed, mixed), load(k_qkv, v_qkv), load(k_weights, v_weights), load(own.at[m], src)]
            sink = store(g_in.at[m], x2)
            sums = [Total(buf, m == 0) for buf in (s_mats, s_up, s_down, s_table, s_gains)]

            def fed():
                if last:
                    feed_sums()
                    scatters[OUT].begin()
                    up_steps, down_steps = seconds([scatters[UP]]), seconds([scatters[DOWN]])
                    queue.add(*in_groups(firsts([scatters[kind] for kind in (UP, DOWN, OUT)]), 4))
                    queue.add(None, None, up_steps[0], None, None, down_steps[0], None, None, up_steps[1])
                    rest = seconds([scatters[kind] for kind in (UP, DOWN, OUT)])
                    queue.add(rest[2], *rest[4:])

            encode_back(
                loads[0], box(m), w_gains, loads[1], w_down, w_up, loads[2], w_mats, loads[3], *late[:3],
                late[3], w_table, sink, *sums, dy, dy_t, a_t, dx, dmixed, dq, x1, dv,
                queue, fed,
            )
            finish([sink])
        if line:
            last_sums((TABLE, GAIN, MATS))
            hand.wait_recv()
            o_proj[3] = handed[0]
            o_out[1] = handed[1]
        for item in first:
            item()

    @pl.when(section == 1)
    def _():
        count[0] = 0
        w_table, w_gains, w_mats, w_up, w_down, w_cross = first = persistent()
        if line:
            gathers[UP].begin_along()
            gathers[DOWN].begin_along()
            one, two, three = [[gathers[kind]] for kind in (CROSS, UP, DOWN)]
            queue.add(*passing(one), None, *passing(two), *sharing(one), CROSS, *passing(three))
            queue.add(*sharing(two), UP, *sharing(three), DOWN)
            w_cross.before = weights_ready((CROSS,))
            w_up.before = weights_ready((UP, DOWN))
        base = count[0]
        hidden, dup = pool["hidden"]
        a_t, b_t = pool["tokt"]
        v_qkv, v_weights = pool["qkv"][0], pool["weights"][0]
        for m in range(micro):
            count[0] = base
            k_qkv, k_weights, k_mixed, k_h1 = kept[m][:4]
            tgt, mixed = pool["tok"][:2]
            sinks = [
                store(k_qkv, v_qkv, axis=1), store(k_weights, v_weights), store(k_mixed, mixed),
                store(k_h1, pool["tok32"][0]),
            ]
            self_forward(
                load(own.at[m], tgt), w_table, w_gains, *code_loads(m), w_mats, *sinks, codes, cols, queue
            )
            finish(sinks)
        for m in range(micro):
            count[0] = base
            k_h1, k_dh1, k_hidden, k_dup, k_a = kept[m][3:8]
            v_cot, out, mixed, dy, dmixed, dq = pool["tok"]
            h1, h2, dk, dv = pool["tok32"]
            sums = [Total(buf, m == 0) for buf in (s_cross, s_gains)]
            sinks = [store(whole.at[m], out), store(k_dh1, h2)]
            feeds = [store(k_a, a_t, split=False), store(k_dup, dup), store(k_hidden, hidden)]
            cross(
                load(k_h1, h1), w_gains, *code_loads(m), w_cross, box(m), w_up, w_down,
                load(cot.at[m], v_cot), sinks[0], box(m), sinks[1], *sums, *feeds, codes, cols, v_qkv,
                v_weights, mixed, h2, dy, b_t, dmixed, dq, dk, dv,
            )
            finish(sinks + feeds)
        if line:
            scatters[CROSS].begin()
        for m in range(micro):
            count[0] = base
            k_hidden, k_dup, k_a = kept[m][5:8]
            sums = [Total(buf, m == 0) for buf in (s_up, s_down)]
            feed_grads(
                load(k_a, a_t), load(k_dup, dup), load(cot.at[m], pool["tok"][0]), load(k_hidden, hidden),
                *sums, b_t,
            )
            if line and m == 0:
                for step in firsts([scatters[CROSS]]):
                    step()
        if line:
            feed_sums()
            pair = [scatters[UP], scatters[DOWN]]
            late = seconds(pair)
            queue.add(*in_groups(firsts(pair), 4), *seconds([scatters[CROSS]]), late[0], None, late[1], None)
            queue.add(late[2], None, late[3], late[4], late[5], None, None, late[6], None, None, late[7])
        for m in range(micro):
            count[0] = base
            k_qkv, k_weights, k_mixed, _, k_dh1 = kept[m][:5]
            tgt, mixed, dy, dmixed, dq = pool["tok"][:5]
            dh1, grad, dk, dv = pool["tok32"]
            loads = [load(k_dh1, dh1), load(k_mixed, mixed), load(k_qkv, v_qkv), load(k_weights, v_weights)]
            sink = store(g_in.at[m], grad)
            sums = [Total(s_mats, m == 0), Total(s_table, m == 0), Total(s_gains, False)]
            self_back(
                loads[0], w_mats, *loads[1:], load(own.at[m], tgt), w_table, w_gains, sink, *sums, dy, a_t,
                b_t, dmixed, dq, dk, dv, queue,
            )
            finish([sink])
        if line:
            queue.flush()
            scatters[CROSS].finish(put_cross)
            hand.start()
            place.meet(ready.at[1])
            last_sums((TABLE, GAIN, MATS, OUT))
            hand.wait_send()
        for item in first:
            item()

    for m in range(micro):
        box(m).wait()
    if not line:
        copies = [
            pltpu.make_async_copy(buf, out, local.at[at])
            for at, (buf, out) in enumerate(zip((s_mats, s_cross, s_up, s_down, s_table, s_gains), results))
        ]
        for copy in copies:
            copy.start()
        for copy in copies:
            copy.wait()


def run_step(z, line, given, results, own, cot, segments, levels):
    micro, length = own.shape[:2]
    parts = length // TB
    args = [*given, own, cot, segments, levels]
    outs = [z["outputs"], z["g_in"], *results] + [z[name] for _ in range(micro) for name in KEPT]
    scratch = [z[name] for name in PERSISTENT]
    scratch += [z[name] for name, number in POOL for _ in range(number)]
    dma = pltpu.SemaphoreType.DMA
    sems = [dma((64,)), dma((micro, parts)), dma((micro, parts))]
    if line:
        per, width = given[0].shape[1:]
        slots = 4 * LINE
        own_scratch = [
            shape((slots, 4, per, width), BF), shape((slots,) + z["packed_gains"].shape[1:], BF),
            z["packed_gains"], shape((2, per, width), F32), shape((2, per, width), F32),
        ]
        sems_line = [dma((KINDS, LINE - 1))] * 2 + [dma((KINDS, LINE))] * 2 + [dma((KINDS, 2 * LINE))] * 2
        sems_line += [dma((KINDS, LINE - 1))] * 2 + [dma((KINDS, LINE))] * 2 + [dma((KINDS, LINE, 2))] * 2
        sems_line += [pltpu.SemaphoreType.REGULAR((2,)), dma((2,)), dma((2,))]
    in_vmem, anywhere = pl.BlockSpec(memory_space=pltpu.VMEM), pl.BlockSpec(memory_space=pl.ANY)
    edge = in_vmem if line else anywhere
    vmem = [pltpu.VMEM(s.shape, s.dtype) for s in scratch]
    if line:
        scratch_shapes = vmem + sems + [pltpu.VMEM(s.shape, s.dtype) for s in own_scratch] + sems_line
    else:
        scratch_shapes = vmem + sems
    outs = pl.pallas_call(
        partial(step_kernel, z, line),
        out_shape=outs,
        in_specs=[edge] * 6 + [anywhere] * 4,
        out_specs=[anywhere] * 2 + [edge] * 6 + [anywhere] * (len(outs) - 8),
        scratch_shapes=scratch_shapes,
        compiler_params=pltpu.CompilerParams(
            collective_id=0, has_side_effects=True, vmem_limit_bytes=VMEM_BYTES
        ),
        name="step",
    )(*args)
    return outs[:8]


def body(
    inputs,
    positions,
    projections,
    out_projections,
    ffn_up,
    ffn_down,
    norm_gains,
    segments,
    levels,
    cotangent,
):
    micro, _, length, width = inputs.shape[1:]
    ranks = lax.axis_size("dp")
    per, n_gains = width // ranks, norm_gains.shape[1]
    z = sizes(length, width, ffn_up.shape[2], micro, ranks)
    rows = (inputs[0, :, 0], cotangent[:, 0], segments, levels)
    line = ranks == 4 * LINE and per * 4 == PAIR and n_gains <= 8
    if line:
        gain = norm_gains.transpose(1, 0, 2)
        given = (projections[0], out_projections[0], ffn_up[0], ffn_down[0], positions[0].T, gain)
        results = [shape(item.shape, F32) for item in given]
        whole, g_in, d_proj, d_out, d_up, d_down, d_table, d_gain = run_step(z, True, given, results, *rows)
        d_table, d_gain = d_table.T[None], d_gain.transpose(1, 0, 2)
    else:
        every = lambda value, axis: lax.all_gather(value.astype(BF), "dp", axis=axis, tiled=True)
        part = lambda value, axis: lax.psum_scatter(value, "dp", scatter_dimension=axis, tiled=True)
        to_section = lambda value, source: lax.ppermute(value, "section", [(source, 1 - source)])
        proj, outp = projections[0].astype(BF), out_projections[0].astype(BF)
        mine = jnp.stack([proj[3], outp[1]])
        gains = every(norm_gains[0], 1).astype(F32)
        given = (
            every(jnp.stack([proj[0], proj[1], proj[2], outp[0]]), 1),
            every(jnp.concatenate([mine, to_section(mine, 0)]), 1),
            every(ffn_up[0], 0), every(ffn_down[0], 0), every(positions[0], 1),
            jnp.concatenate([gains, jnp.zeros((8 - n_gains, width), F32)]),
        )
        results = [z[name] for name in ("mats", "mats", "up", "down", "packed", "gains")]
        whole, g_in, d_mats, d_cross, d_up, d_down, d_table, d_gain = run_step(z, False, given, results, *rows)
        d_mats, d_cross = part(d_mats, 1).astype(F32), part(d_cross, 1)
        back = to_section(d_cross[2:], 1)
        more = jnp.where(lax.axis_index("section") == 0, back, d_cross[:2]).astype(F32)
        d_proj = jnp.concatenate([d_mats[:3], more[:1]])
        d_out = jnp.concatenate([d_mats[3:], more[1:]])
        d_up, d_down = part(d_up, 0).astype(F32), part(d_down, 0).astype(F32)
        d_table = part(d_table, 0)[0].astype(F32).T[None]
        d_gain = part(d_gain, 1)[None, :n_gains]
    return (
        whole[None, :, None],
        g_in[None, :, None],
        d_table,
        d_proj[None],
        d_out[None],
        d_up[None],
        d_down[None],
        d_gain,
    )


def solution(mesh):
    in_specs = (
        P("section", None, "dp", None, None),
        P("section", None, "dp"),
        P("section", None, "dp", None),
        P("section", None, "dp", None),
        P("section", "dp", None),
        P("section", "dp", None),
        P("section", None, "dp"),
        P(None, "dp", None),
        P(None, None, "dp", None),
        P(None, "dp", None, None),
    )
    out_specs = (
        P("section", None, "dp", None, None),
        P("section", None, "dp", None, None),
        P("section", None, "dp"),
        P("section", None, "dp", None),
        P("section", None, "dp", None),
        P("section", "dp", None),
        P("section", "dp", None),
        P("section", None, "dp"),
    )
    return jax.shard_map(body, mesh=mesh, in_specs=in_specs, out_specs=out_specs, check_vma=False)
```

```python
from functools import partial

import jax
import jax.numpy as jnp
from jax import lax
from jax.experimental import pallas as pl
from jax.experimental.pallas import tpu as pltpu
from jax.sharding import PartitionSpec as P

BF = jnp.bfloat16
F32 = jnp.float32
DH = 64
PAIR = 2 * DH
QB = 128
WIN = 256
TB = 256
MESH = pl.DeviceIdType.MESH
VMEM_BYTES = 62 * 1024 * 1024


def nn(left, right):
    return jnp.dot(left, right, preferred_element_type=F32)


def nt(left, right):
    return lax.dot_general(left, right, (((1,), (1,)), ((), ())), preferred_element_type=F32)


def tn(left, right):
    return lax.dot_general(left, right, (((0,), (0,)), ((), ())), preferred_element_type=F32)


def norm_parts(stream):
    centred = stream - jnp.mean(stream, axis=-1, keepdims=True)
    scale = lax.rsqrt(jnp.mean(centred * centred, axis=-1, keepdims=True) + 1e-05)
    return centred * scale, scale


def norm_back(grad, unit, scale, gain):
    inner = grad * gain
    first = jnp.mean(inner, axis=-1, keepdims=True)
    second = jnp.mean(inner * unit, axis=-1, keepdims=True)
    return scale * (inner - first - unit * second), jnp.sum(grad * unit, axis=0, keepdims=True)


def block_at(index, size):
    if isinstance(index, int):
        return pl.ds(index * size, size)
    return pl.ds(pl.multiple_of(index * size, size), size)


def lane_halves(scale=1.0):
    lane = lax.broadcasted_iota(jnp.int32, (1, PAIR), 1)
    low = jnp.where(lane < DH, scale, 0.0).astype(BF)
    high = jnp.where(lane < DH, 0.0, scale).astype(BF)
    return low, high


def both_heads(block, halves):
    return jnp.concatenate([block * halves[0], block * halves[1]], axis=0)


def join_heads(stacked):
    lane = lax.broadcasted_iota(jnp.int32, (QB, PAIR), 1)
    return jnp.where(lane < DH, stacked[:QB], stacked[QB:])


def window_start(index, length):
    return pl.multiple_of(jnp.clip(index * QB - DH, 0, length - WIN), DH)


def make_codes(segments, source_level, target_level, codes_ref, cols_ref):
    segment = segments[...]
    length = segment.shape[1]
    before = pltpu.roll(segment, 1, axis=1)
    lane = lax.broadcasted_iota(jnp.int32, (1, length), 1)
    first = (lane == 0) | (segment != before)
    usable = jnp.where(first | (source_level[...] > 0), segment, -1)
    row = lax.broadcasted_iota(jnp.int32, (8, length), 0)
    codes = jnp.where(row == 0, usable, jnp.where(row == 1, segment, target_level[...]))
    codes_ref[...] = codes
    cols_ref[...] = codes.T


def mask_bias(index, start, codes_ref, cols_ref, causal):
    keys = cols_ref[pl.ds(start, WIN), :]
    queries = codes_ref[:, block_at(index, QB)]
    query_segment = queries[1:2, :]
    if causal:
        key_id = start + lax.broadcasted_iota(jnp.int32, (WIN, QB), 0)
        query_id = index * QB + lax.broadcasted_iota(jnp.int32, (WIN, QB), 1)
        allowed = (keys[:, 1:2] == query_segment) & (
            (keys[:, 2:3] < queries[2:3, :]) | (key_id == query_id)
        )
    else:
        allowed = keys[:, 0:1] == query_segment
    bias = jnp.where(allowed, 0.0, -1e30)
    return jnp.concatenate([bias, bias], axis=1)


def attend_block(index, q_ref, k_ref, v_ref, codes_ref, cols_ref, weights_ref, mixed_ref, causal):
    length, width = q_ref.shape
    start = window_start(index, length)
    rows = block_at(index, QB)
    bias = mask_bias(index, start, codes_ref, cols_ref, causal)
    halves = lane_halves(DH ** -0.5)
    for pair in range(width // PAIR):
        lanes = slice(pair * PAIR, (pair + 1) * PAIR)
        queries = both_heads(q_ref[rows, lanes], halves)
        scores = nt(k_ref[pl.ds(start, WIN), lanes], queries) + bias
        shifted = jnp.exp(scores - jnp.max(scores, axis=0, keepdims=True))
        weights = (shifted * (1.0 / jnp.sum(shifted, axis=0, keepdims=True))).astype(BF)
        weights_ref[index, pair] = weights
        out = tn(weights, v_ref[pl.ds(start, WIN), lanes])
        mixed_ref[rows, lanes] = join_heads(out).astype(BF)


def attend_back_block(
    index, q_ref, k_ref, v_ref, weights_ref, mixed_ref, dmixed_ref, dq_ref, dk_ref, dv_ref
):
    length, width = q_ref.shape
    start = window_start(index, length)
    rows = block_at(index, QB)
    window = pl.ds(start, WIN)
    plain = lane_halves()
    halves = lane_halves(DH ** -0.5)
    ones = jnp.ones((WIN, PAIR), BF)
    for pair in range(width // PAIR):
        lanes = slice(pair * PAIR, (pair + 1) * PAIR)
        queries = both_heads(q_ref[rows, lanes], halves)
        keys = k_ref[window, lanes]
        values = v_ref[window, lanes]
        weights = weights_ref[index, pair]
        dmixed = dmixed_ref[rows, lanes]
        grads = both_heads(dmixed, plain)
        inner = (dmixed.astype(F32) * mixed_ref[rows, lanes].astype(F32) * -1.0).astype(BF)
        left = jnp.concatenate([values, ones], axis=1)
        right = jnp.concatenate([grads, both_heads(inner, plain)], axis=1)
        centred = nt(left, right)
        dscores = (weights.astype(F32) * centred).astype(BF)
        dv_ref[window, lanes] += nn(weights, grads)
        dk_ref[window, lanes] += nn(dscores, queries)
        dq = tn(dscores, keys) * (DH ** -0.5)
        dq_ref[rows, lanes] = join_heads(dq).astype(BF)


def gelu_parts(value):
    cdf = 0.5 + 0.5 * lax.erf(value * (0.5 ** 0.5))
    density = jnp.exp(value * value * -0.5) * 0.3989422804014327
    return value * cdf, cdf + value * density


def feed_block(normed, up_ref, down_ref, hidden_ref, slope_ref, rows):
    total = None
    width, step = up_ref.shape[1], down_ref.shape[1]
    for at in range(0, width, step):
        hidden, slope = gelu_parts(nn(normed, up_ref[:, at : at + step]))
        hidden = hidden.astype(BF)
        hidden_ref[rows, at : at + step] = hidden
        slope_ref[rows, at : at + step] = slope.astype(BF)
        term = nn(hidden, down_ref[at // step])
        total = term if total is None else total + term
    return total


def feed_back_block(grad, up_ref, down_ref, slope_ref, rows):
    total = None
    width, step = up_ref.shape[1], down_ref.shape[1]
    for at in range(0, width, step):
        dhidden = nt(grad, down_ref[at // step])
        dup = (dhidden * slope_ref[rows, at : at + step].astype(F32)).astype(BF)
        slope_ref[rows, at : at + step] = dup
        term = nt(dup, up_ref[:, at : at + step])
        total = term if total is None else total + term
    return total


class Queue:
    def __init__(self):
        self.steps = []

    def add(self, *groups):
        self.steps.extend(groups)

    def next(self):
        while self.steps and isinstance(self.steps[0], int):
            self.steps.pop(0)
        return self.steps.pop(0) if self.steps else None

    def flush(self, mark=None):
        if mark is not None and mark not in self.steps:
            return
        while self.steps:
            step = self.steps.pop(0)
            if step == mark and mark is not None:
                return
            if callable(step):
                step()


def loop(count, body, queue=None):
    hooks = [queue.next() if queue else None for _ in range(count)]

    def step(index, carry):
        body(index)
        for turn, hook in enumerate(hooks):
            if hook is not None:
                pl.when(index == turn)(hook)
        return carry

    lax.fori_loop(0, count, step, 0)


def put_grad(out, index, value):
    if out.prior is not None:
        value = value + out.buf[index].astype(F32)
    out.buf[index] = value.astype(BF)


def weight_grad(out, left_t_refs, right_refs, transposed):
    step = 512
    width = right_refs[0].shape[1]

    def slab(index):
        cols = block_at(index, step)
        value = None
        for left_t, right in zip(left_t_refs, right_refs):
            term = nn(left_t[...], right[:, cols])
            value = term if value is None else value + term
        if transposed:
            put_grad(out, (cols, slice(None)), value.T)
        else:
            put_grad(out, (slice(None), cols), value)

    loop(width // step, slab)


def put_table(out, rows, value):
    value = value.T.reshape(out.buf.shape[:2] + (value.shape[0],))
    put_grad(out, (slice(None), slice(None), rows), value)


def add_gain(out, row, value):
    out.buf[row : row + 1, :] += value


class Source:
    def __init__(self, hbm, buf, sem):
        self.buf, self.copy, self.here = buf, pltpu.make_async_copy(hbm, buf, sem), False
        self.copy.start()

    def __call__(self):
        if not self.here:
            self.copy.wait()
            self.here = True
        return self.buf


class Sink:
    def __init__(self, hbm, buf, sems, first, parts, axis, prior):
        self.hbm, self.buf, self.sems, self.first = hbm, buf, sems, first
        self.parts, self.axis, self.prior = parts, axis, prior

    def copy(self, part):
        view = [slice(None)] * len(self.buf.shape)
        size = self.buf.shape[self.axis] // self.parts
        view[self.axis] = block_at(part, size)
        view = tuple(view)
        return pltpu.make_async_copy(
            self.buf.at[view], self.hbm.at[view], self.sems.at[self.first + part]
        )

    def send(self, part=0):
        self.copy(part).start()

    def wait(self):
        for part in range(self.parts):
            self.copy(part).wait()


class Ready:
    def __init__(self, buf, before=None):
        self.buf, self.before = buf, before

    def __call__(self):
        if self.before is not None:
            self.before()
            self.before = None
        return self.buf


class Total:
    def __init__(self, buf, first):
        self.buf = buf
        self.prior = None if first else buf


class Link:
    def __init__(self, outbox, inbox, send, recv, parts):
        self.buf, self.inbox, self.sems, self.parts = outbox, inbox, (send, recv), parts

    def copy(self, part):
        size = self.buf.shape[0] // self.parts
        rows = block_at(part, size)
        return pltpu.make_async_remote_copy(
            src_ref=self.buf.at[rows, :], dst_ref=self.inbox.at[rows, :],
            send_sem=self.sems[0].at[part], recv_sem=self.sems[1].at[part],
            device_id={"section": 1 - lax.axis_index("section")}, device_id_type=MESH,
        )

    def send(self, part):
        self.copy(part).start()

    def wait(self):
        for part in range(self.parts):
            self.copy(part).wait_send()

    def come(self, part):
        self.copy(part).wait_recv()


def encode_attend(src, table, gains, segments, source_level, target_level, mats, qkv, weights, mixed, codes, cols, queue):
    length = src.buf.shape[0]
    make_codes(segments(), source_level(), target_level(), codes, cols)
    src, table, gains, mats = src(), table(), gains(), mats()

    def project(index):
        rows = block_at(index, TB)
        unit, _ = norm_parts(src[rows, :].astype(F32) + table[rows, :].astype(F32))
        normed = (unit * gains[0:1, :]).astype(BF)
        for which in range(3):
            qkv.buf[which, rows, :] = nn(normed, mats[which]).astype(BF)
        qkv.send(index)

    loop(length // TB, project, queue)

    def attend(index):
        for part in range(TB // QB):
            attend_block(
                index * (TB // QB) + part,
                qkv.buf.at[0], qkv.buf.at[1], qkv.buf.at[2], codes, cols, weights.buf, mixed.buf, False,
            )
        weights.send(index)
        mixed.send(index)

    loop(length // TB, attend, queue)


def encode_feed(src, mixed, table, gains, mats, up, down, mem, x1, x2, hidden, slope):
    length = src.buf.shape[0]
    table, gains, mats, up, down = table(), gains(), mats(), up(), down()
    src, mixed = src(), mixed()

    def rest(index):
        rows = block_at(index, TB)
        stream = src[rows, :].astype(F32) + table[rows, :].astype(F32)
        stream = stream + nn(mixed[rows, :], mats[3])
        x1.buf[rows, :] = stream
        x1.send(index)
        unit, _ = norm_parts(stream)
        normed = (unit * gains[1:2, :]).astype(BF)
        stream = stream + feed_block(normed, up, down, hidden.buf, slope.buf, rows)
        x2.buf[rows, :] = stream
        unit, _ = norm_parts(stream)
        mem.buf[rows, :] = (unit * gains[2:3, :]).astype(BF)
        for item in (mem, x2, hidden, slope):
            item.send(index)

    loop(length // TB, rest)


def encode_back(
    x2, dmem, gains, slope, down, up, x1, mats, hidden, mixed, qkv, weights, src, table,
    g_in, g_mats, g_up, g_down, g_table, g_gains,
    dy, dy_t, a_t, dx, dmixed, dq, dk, dv, queue, fed, tabled, passed,
):
    length = src.buf.shape[0]
    if g_gains.prior is None:
        g_gains.buf[...] = jnp.zeros_like(g_gains.buf)
    x2, gains, slope, down, up, x1, mats = x2(), gains(), slope(), down(), up(), x1(), mats()

    def feed_step(index):
        rows = block_at(index, TB)
        dmem.come(index)
        unit, scale = norm_parts(x2[rows, :])
        grad, d_gain = norm_back(dmem.inbox[rows, :].astype(F32), unit, scale, gains[2:3, :])
        add_gain(g_gains, 2, d_gain)
        low = grad.astype(BF)
        dy_t[:, rows] = low.T
        dnormed = feed_back_block(low, up, down, slope, rows)
        unit, scale = norm_parts(x1[rows, :])
        a_t[:, rows] = (unit * gains[1:2, :]).astype(BF).T
        back, d_gain = norm_back(dnormed, unit, scale, gains[1:2, :])
        add_gain(g_gains, 1, d_gain)
        grad = grad + back
        dx[rows, :] = grad
        low = grad.astype(BF)
        dy[rows, :] = low
        dmixed[rows, :] = nt(low, mats[3]).astype(BF)

    loop(length // TB, feed_step)
    weight_grad(g_up, [a_t], [slope], False)
    weight_grad(g_down, [dy_t], [hidden()], True)
    mixed = mixed()
    put_grad(g_mats, 3, tn(mixed[...], dy[...]))
    fed()
    qkv, weights = qkv(), weights()
    dk[...] = jnp.zeros_like(dk)
    dv[...] = jnp.zeros_like(dv)

    def attend_step(index):
        attend_back_block(
            index, qkv.at[0], qkv.at[1], qkv.at[2], weights, mixed, dmixed, dq, dk, dv
        )

    loop(length // QB, attend_step, queue)
    src, table = src(), table()

    def project_step(index):
        rows = block_at(index, TB)
        unit, scale = norm_parts(src[rows, :].astype(F32) + table[rows, :].astype(F32))
        a_t[:, rows] = (unit * gains[0:1, :]).astype(BF).T
        dnormed = nt(dq[rows, :], mats[0])
        dnormed += nt(dk[rows, :].astype(BF), mats[1])
        dnormed += nt(dv[rows, :].astype(BF), mats[2])
        back, d_gain = norm_back(dnormed, unit, scale, gains[0:1, :])
        add_gain(g_gains, 0, d_gain)
        grad = dx[rows, :] + back
        g_in.buf[rows, :] = grad
        g_in.send(index)
        put_table(g_table, rows, grad)

    loop(length // TB, project_step, queue)
    tabled()
    put_grad(g_mats, 0, nn(a_t[...], dq[...]))
    passed()
    put_grad(g_mats, 1, nn(a_t[...], dk[...].astype(BF)))
    put_grad(g_mats, 2, nn(a_t[...], dv[...].astype(BF)))


def self_forward(tgt, table, gains, segments, source_level, target_level, mats, qkv, weights, mixed, h1, codes, cols, queue):
    length = tgt.buf.shape[0]
    make_codes(segments(), source_level(), target_level(), codes, cols)
    tgt, table, gains, mats = tgt(), table(), gains(), mats()

    def project(index):
        rows = block_at(index, TB)
        stream = table[rows, :].astype(F32)
        unit, _ = norm_parts(stream)
        qkv.buf[0, rows, :] = nn((unit * gains[0:1, :]).astype(BF), mats[0]).astype(BF)
        unit, _ = norm_parts(tgt[rows, :].astype(F32) + stream)
        normed = (unit * gains[0:1, :]).astype(BF)
        for which in (1, 2):
            qkv.buf[which, rows, :] = nn(normed, mats[which]).astype(BF)
        qkv.send(index)

    loop(length // TB, project, queue)

    def rest(index):
        for part in range(TB // QB):
            attend_block(
                index * (TB // QB) + part,
                qkv.buf.at[0], qkv.buf.at[1], qkv.buf.at[2], codes, cols, weights.buf, mixed.buf, True,
            )
        rows = block_at(index, TB)
        h1.buf[rows, :] = table[rows, :].astype(F32) + nn(mixed.buf[rows, :], mats[3])
        for item in (weights, mixed, h1):
            item.send(index)

    loop(length // TB, rest, queue)


def self_back(
    dh1, mats, mixed, qkv, weights, tgt, table, gains,
    g_in, g_mats, g_table, g_gains,
    dy, a_t, b_t, dmixed, dq, dk, dv, queue, mixed_done, tabled, passed,
):
    length = tgt.buf.shape[0]
    dk[...] = jnp.zeros_like(dk)
    dv[...] = jnp.zeros_like(dv)
    dh1, mats, mixed = dh1(), mats(), mixed()

    def out_step(index):
        rows = block_at(index, TB)
        low = dh1[rows, :].astype(BF)
        dy[rows, :] = low
        dmixed[rows, :] = nt(low, mats[3]).astype(BF)

    loop(length // TB, out_step)
    put_grad(g_mats, 3, tn(mixed[...], dy[...]))
    mixed_done()
    qkv, weights = qkv(), weights()

    def attend_step(index):
        attend_back_block(
            index, qkv.at[0], qkv.at[1], qkv.at[2], weights, mixed, dmixed, dq, dk, dv
        )

    loop(length // QB, attend_step, queue)
    tgt, table, gains = tgt(), table(), gains()

    def project_step(index):
        rows = block_at(index, TB)
        stream = table[rows, :].astype(F32)
        unit, scale = norm_parts(stream)
        a_t[:, rows] = (unit * gains[0:1, :]).astype(BF).T
        back, d_gain = norm_back(nt(dq[rows, :], mats[0]), unit, scale, gains[0:1, :])
        dtable = dh1[rows, :] + back
        unit, scale = norm_parts(tgt[rows, :].astype(F32) + stream)
        b_t[:, rows] = (unit * gains[0:1, :]).astype(BF).T
        dnormed = nt(dk[rows, :].astype(BF), mats[1])
        dnormed += nt(dv[rows, :].astype(BF), mats[2])
        back, d_gain_too = norm_back(dnormed, unit, scale, gains[0:1, :])
        add_gain(g_gains, 0, d_gain + d_gain_too)
        g_in.buf[rows, :] = back
        g_in.send(index)
        put_table(g_table, rows, dtable + back)

    loop(length // TB, project_step, queue)
    tabled()
    put_grad(g_mats, 0, nn(a_t[...], dq[...]))
    passed()
    put_grad(g_mats, 1, nn(b_t[...], dk[...].astype(BF)))
    put_grad(g_mats, 2, nn(b_t[...], dv[...].astype(BF)))


def feed_grads(a_t, dup, cot, hidden, g_up, g_down, cot_t):
    cot_t[...] = cot()[...].T
    weight_grad(g_up, [a_t()], [dup()], False)
    weight_grad(g_down, [cot_t], [hidden()], True)


def cross(
    h1, gains, segments, source_level, target_level, mats, mem, up, down, cot,
    out, dmem, dh1, g_mats, g_gains, a_t, dup, hidden,
    codes, cols, qkv, weights, mixed, h2, dy, b_t, dmixed, dq, dk, dv,
):
    length = h1.buf.shape[0]
    make_codes(segments(), source_level(), target_level(), codes, cols)
    if g_gains.prior is None:
        g_gains.buf[...] = jnp.zeros_like(g_gains.buf)
    dk[...] = jnp.zeros_like(dk)
    dv[...] = jnp.zeros_like(dv)
    h1, gains, mats = h1(), gains(), mats()
    memory = mem.inbox

    def project(index):
        rows = block_at(index, TB)
        unit, _ = norm_parts(h1[rows, :])
        qkv[0, rows, :] = nn((unit * gains[1:2, :]).astype(BF), mats[0]).astype(BF)
        mem.come(index)
        qkv[1, rows, :] = nn(memory[rows, :], mats[2]).astype(BF)
        qkv[2, rows, :] = nn(memory[rows, :], mats[3]).astype(BF)

    loop(length // TB, project)
    up, down, cot = up(), down(), cot()

    def attend(index):
        for part in range(TB // QB):
            attend_block(
                index * (TB // QB) + part,
                qkv.at[0], qkv.at[1], qkv.at[2], codes, cols, weights, mixed, False,
            )

    def feed(index):
        rows = block_at(index, TB)
        stream = h1[rows, :] + nn(mixed[rows, :], mats[1])
        unit, scale = norm_parts(stream)
        normed = (unit * gains[2:3, :]).astype(BF)
        a_t.buf[:, rows] = normed.T
        fed = feed_block(normed, up, down, hidden.buf, dup.buf, rows)
        out.buf[rows, :] = (stream + fed).astype(BF)
        low = cot[rows, :]
        dnormed = feed_back_block(low, up, down, dup.buf, rows)
        back, d_gain = norm_back(dnormed, unit, scale, gains[2:3, :])
        add_gain(g_gains, 2, d_gain)
        grad = low.astype(F32) + back
        h2[rows, :] = grad
        low = grad.astype(BF)
        dy[rows, :] = low
        dmixed[rows, :] = nt(low, mats[1]).astype(BF)
        for item in (out, hidden, dup):
            item.send(index)

    attend(0)

    def middle(index):
        feed(index)
        attend(index + 1)

    loop(length // TB - 1, middle)
    feed(length // TB - 1)
    a_t.send()

    def attend_step(index):
        def one(at):
            attend_back_block(at, qkv.at[0], qkv.at[1], qkv.at[2], weights, mixed, dmixed, dq, dk, dv)

        steps = TB // QB
        last = length // TB - 1
        pl.when(index == 0)(lambda: one(0))
        for part in range(1, steps):
            one(index * steps + part)
        pl.when(index < last)(lambda: one((index + 1) * steps))
        rows = block_at(index, TB)
        dkeys = dk[rows, :].astype(BF)
        dvalues = dv[rows, :].astype(BF)
        dmem.buf[rows, :] = (nt(dkeys, mats[2]) + nt(dvalues, mats[3])).astype(BF)
        dmem.send(index)

    loop(length // TB, attend_step)

    def project_step(index):
        rows = block_at(index, TB)
        unit, scale = norm_parts(h1[rows, :])
        b_t[:, rows] = (unit * gains[1:2, :]).astype(BF).T
        back, d_gain = norm_back(nt(dq[rows, :], mats[0]), unit, scale, gains[1:2, :])
        add_gain(g_gains, 1, d_gain)
        dh1.buf[rows, :] = h2[rows, :] + back
        dh1.send(index)

    loop(length // TB, project_step)
    put_grad(g_mats, 0, nn(b_t[...], dq[...]))
    put_grad(g_mats, 1, tn(mixed[...], dy[...]))
    put_grad(g_mats, 2, tn(memory[...], dk[...].astype(BF)))
    put_grad(g_mats, 3, tn(memory[...], dv[...].astype(BF)))


def shape(dims, kind):
    return jax.ShapeDtypeStruct(dims, kind)


def sizes(length, width, ff, micro, ranks):
    blocks = length // QB
    pairs = width // PAIR
    return dict(
        tok=shape((length, width), BF),
        tok32=shape((length, width), F32),
        outputs=shape((micro, length, width), BF),
        g_in=shape((micro, length, width), F32),
        qkv=shape((3, length, width), BF),
        weights=shape((blocks, pairs, WIN, 2 * QB), BF),
        hidden=shape((length, ff), BF),
        tokt=shape((width, length), BF),
        packed=shape((ranks, width // ranks, length), BF),
        packed_gains=shape((ranks, 16, PAIR), BF),
        mats=shape((4, width, width), BF),
        up=shape((width, ff), BF),
        down=shape((ff, width), BF),
        down_parts=shape((ff // width, width, width), BF),
        gains=shape((8, width), F32),
        pair=shape((2, width, width), BF),
        row=shape((1, length), jnp.int32),
        codes=shape((8, length), jnp.int32),
        cols=shape((length, 8), jnp.int32),
    )


LINE = 4
AHEAD = (2, 1, 3, 0)
TABLE, GAIN, MATS, UP, DOWN, CROSS, OUT = range(7)
KINDS = 7


def rank_of(z, x, core):
    return z * 4 + x * 2 + core


def remote(src, dst, send, recv, to):
    return pltpu.make_async_remote_copy(
        src_ref=src, dst_ref=dst, send_sem=send, recv_sem=recv, device_id=to, device_id_type=MESH
    )


def rows_at(ref, per, rank):
    view = [slice(None)] * len(ref.shape)
    view[-2] = pl.ds(pl.multiple_of(rank * per, 16), per)
    return ref.at[tuple(view)]


class Place:
    def __init__(self):
        me = lax.axis_index("dp")
        self.z, self.x, self.core = me // 4, (me // 2) % 2, me % 2
        self.rank = me
        self.section = lax.axis_index("section")
        self.partner = {"section": 1 - self.section}
        self.across = {"dp": rank_of(self.z, 1 - self.x, self.core)}
        self.sibling = {"dp": rank_of(self.z, self.x, 1 - self.core)}

    def ahead(self, step):
        return (self.z + step) % LINE

    def on_line(self, step):
        return {"dp": rank_of(self.ahead(step), self.x, self.core)}

    def line(self, other):
        return 1 - self.x if other else self.x

    def meet(self, semaphore, also=()):
        devices = [self.across, self.sibling, *also] + [self.on_line(step) for step in range(1, LINE)]
        for device in devices:
            pl.semaphore_signal(semaphore, inc=1, device_id=device, device_id_type=MESH)
        pl.semaphore_wait(semaphore, len(devices))


class Gather:
    def __init__(self, place, kind, view, sems):
        self.place, self.kind, self.view = place, kind, view
        self.zsend, self.zrecv, self.xsend, self.xrecv, self.csend, self.crecv = sems

    def block(self, back, other):
        place = self.place
        return self.view(rank_of(place.ahead(LINE - back), place.line(other), place.core))

    def along(self, step):
        at, block = (self.kind, step - 1), self.block(0, 0)
        return remote(block, block, self.zsend.at[at], self.zrecv.at[at], self.place.on_line(step))

    def over(self, back):
        at, block = (self.kind, back), self.block(back, 0)
        return remote(block, block, self.xsend.at[at], self.xrecv.at[at], self.place.across)

    def beside(self, back, other):
        at, block = (self.kind, back + LINE * other), self.block(back, other)
        return remote(block, block, self.csend.at[at], self.crecv.at[at], self.place.sibling)

    def begin_along(self):
        for step in (1, 3, 2):
            self.along(step).start()

    def begin_over(self):
        self.over(0).start()
        self.beside(0, 0).start()

    def pass_on(self, back):
        self.along(back).wait_recv()
        self.over(back).start()
        self.beside(back, 0).start()

    def share(self, back):
        self.over(back).wait_recv()
        self.beside(back, 1).start()

    def finish(self):
        for step in range(1, LINE):
            self.along(step).wait_send()
        for back in range(LINE):
            self.over(back).wait_send()
            for other in range(2):
                copy = self.beside(back, other)
                copy.wait_send()
                copy.wait_recv()


def passing(arrays):
    return [partial(array.pass_on, back) for back in (1, 3, 2) for array in arrays]


def sharing(arrays):
    return [partial(array.share, back) for back in (0, 1, 3, 2) for array in arrays]


def in_groups(steps, size):
    def group(some):
        return lambda: [step() for step in some] and None

    return [group(steps[at : at + size]) for at in range(0, len(steps), size)]


class Scatter:
    def __init__(self, place, kind, view, slots, sems):
        self.place, self.kind, self.view, self.slots = place, kind, view, slots
        self.zsend, self.zrecv, self.xsend, self.xrecv, self.csend, self.crecv = sems

    def from_core(self, step, part):
        return self.slots(step * 2 + part)

    def from_x(self, step):
        return self.slots(2 * LINE + step)

    def from_z(self, step):
        return self.slots(3 * LINE + step - 1)

    def own(self, step, part, its_core):
        return self.view(rank_of(self.place.ahead(step), self.place.line(1 - part), its_core))

    def beside(self, step, part):
        at = (self.kind, step, part)
        return remote(
            self.own(step, part, 1 - self.place.core), self.from_core(step, part), self.csend.at[at],
            self.crecv.at[at], self.place.sibling,
        )

    def over(self, step):
        at = (self.kind, step)
        return remote(
            self.from_core(step, 0), self.from_x(step), self.xsend.at[at], self.xrecv.at[at],
            self.place.across,
        )

    def along(self, step):
        at = (self.kind, step - 1)
        return remote(
            self.from_core(step, 1), self.from_z(step), self.zsend.at[at], self.zrecv.at[at],
            self.place.on_line(step),
        )

    def total(self, *terms):
        value = terms[0][...].astype(F32)
        for term in terms[1:]:
            value = value + term[...].astype(F32)
        return value

    def begin(self):
        for part in range(2):
            for step in AHEAD:
                self.beside(step, part).start()

    def first(self, step):
        self.beside(step, 0).wait_recv()
        both = self.from_core(step, 0)
        both[...] = self.total(both, self.own(step, 0, self.place.core)).astype(BF)
        self.over(step).start()

    def second(self, step):
        self.beside(step, 1).wait_recv()
        self.over(step).wait_recv()
        four = self.from_core(step, 1)
        four[...] = self.total(four, self.own(step, 1, self.place.core), self.from_x(step)).astype(BF)
        if step:
            self.along(step).start()

    def finish(self, put):
        for step in range(1, LINE):
            self.along(step).wait_recv()
        put(self.total(self.from_core(0, 1), *[self.from_z(step) for step in range(1, LINE)]))
        for step in range(LINE):
            self.over(step).wait_send()
            if step:
                self.along(step).wait_send()
            for part in range(2):
                self.beside(step, part).wait_send()


def firsts(arrays):
    return [partial(array.first, step) for step in AHEAD for array in arrays]


def seconds(arrays):
    return [partial(array.second, step) for step in AHEAD for array in arrays]


POOL = (("row", 3), ("tok", 6), ("tok32", 4), ("tokt", 2), ("qkv", 1), ("weights", 1), ("hidden", 2))
KEPT = ("qkv", "weights", "tok", "tok32", "tok32", "hidden", "hidden", "tokt")
PERSISTENT = (
    "tok", "gains", "mats", "up", "down_parts", "mats", "mats", "mats", "up", "down", "packed", "gains", "codes",
    "cols", "outputs", "outputs",
)


def nothing():
    return None


def step_kernel(z, line, *refs):
    refs = list(refs)
    take = lambda count: [refs.pop(0) for _ in range(count)]
    given, (own, cot, segments, levels) = take(6), take(4)
    whole, g_in = take(2)
    results = take(6)
    micro, length = own.shape[:2]
    parts = length // TB
    kept = [take(len(KEPT)) for _ in range(micro)]
    (
        v_table, v_gains, v_mats, v_up, v_down, v_cross, s_mats, s_cross, s_up, s_down, s_table, s_gains,
        codes, cols, inbox, outbox,
    ) = take(len(PERSISTENT))
    pool = {name: take(count) for name, count in POOL}
    local, ysend, yrecv = take(3)
    section = lax.axis_index("section")
    count = [0]

    def sems(number):
        count[0] += number
        return count[0] - number

    def load(hbm, buf):
        return Source(hbm, buf, local.at[sems(1)])

    def store(hbm, buf, axis=0, split=True):
        number = parts if split else 1
        return Sink(hbm, buf, local, sems(number), number, axis, None)

    def box(m):
        return Link(outbox.at[m], inbox.at[m], ysend.at[m], yrecv.at[m], parts)

    def code_loads(m):
        hbm = (segments.at[m], levels.at[0, m], levels.at[1, m])
        return [load(ref, buf) for ref, buf in zip(hbm, pool["row"])]

    queue = Queue()
    if line:
        o_proj, o_out, o_up, o_down, o_table, o_gain = results
        r_gains, packed_gains, handing, handed = take(4)
        g_sems, s_sems = take(6), take(6)
        ready, shard_sems, hand_sems = refs
        place = Place()
        per, n_gains = o_table.shape[0], o_gain.shape[0]
        ranks = s_table.shape[0]
        rank, lent = place.rank, slice(2, 4)

        def down_shard(at):
            tall = o_down.shape[0]
            inside = v_down.shape[1] // tall
            return v_down.at[at // inside, pl.ds(pl.multiple_of(at % inside * tall, 16), tall), :]

        view_of = {
            TABLE: lambda at: s_table.at[at],
            GAIN: lambda at: packed_gains.at[at],
            MATS: lambda at: rows_at(v_mats, per, at),
            UP: lambda at: rows_at(v_up, per, at),
            DOWN: down_shard,
            CROSS: lambda at: rows_at(v_cross, per, at),
        }
        gathers = {kind: Gather(place, kind, view, g_sems) for kind, view in view_of.items()}
        sum_of = {
            TABLE: lambda at: s_table.at[at],
            GAIN: lambda at: packed_gains.at[at],
            MATS: lambda at: rows_at(s_mats.at[0:3], per, at),
            UP: lambda at: rows_at(s_up, per, at),
            DOWN: lambda at: rows_at(s_down, o_down.shape[0], at),
            CROSS: lambda at: rows_at(s_cross, per, at),
            OUT: lambda at: rows_at(s_mats.at[3], per, at),
        }
        width = v_mats.shape[-1]
        hidden_0, hidden_1 = pool["hidden"]
        slots = 4 * LINE

        def in_hidden(buf, first, tall, wide):
            across = buf.shape[1] // wide

            def slot(number):
                row, lane = first + number // across * tall, number % across * wide
                return buf.at[row : row + tall, lane : lane + wide]

            return slot

        slot_of = {
            TABLE: in_hidden(hidden_0, slots * per, per, length),
            GAIN: lambda number: r_gains.at[number],
            MATS: lambda number: v_down.at[0:3, number * per : (number + 1) * per, :],
            UP: in_hidden(hidden_0, 0, per, hidden_0.shape[1]),
            DOWN: in_hidden(hidden_1, 0, o_down.shape[0], width),
            CROSS: lambda number: v_cross.at[:, number * per : (number + 1) * per, :],
            OUT: in_hidden(hidden_1, slots // (hidden_1.shape[1] // width) * o_down.shape[0], per, width),
        }
        scatters = {
            kind: Scatter(place, kind, view, slot_of[kind], s_sems) for kind, view in sum_of.items()
        }

        p_proj, p_out, p_up, p_down, p_pos, p_gain = given
        s_table[rank] = p_pos[...].astype(BF)
        gain = jnp.concatenate([p_gain[...].reshape(n_gains, per), jnp.zeros((16 - n_gains, per), F32)], axis=0)
        packed_gains[rank] = jnp.concatenate([gain, jnp.zeros((16, PAIR - per), F32)], axis=1).astype(BF)
        own_mats = rows_at(v_mats, per, rank)
        for to, shard in enumerate((p_proj.at[0], p_proj.at[1], p_proj.at[2], p_out.at[0])):
            own_mats[to] = shard[...].astype(BF)
        own_cross = rows_at(v_cross, per, rank)
        for to, shard in enumerate((p_proj.at[3], p_out.at[1])):
            own_cross[to] = shard[...].astype(BF)
        place.meet(pltpu.get_barrier_semaphore(), (place.partner,))
        early = [gathers[kind] for kind in (GAIN, TABLE, MATS)]
        for item in early:
            item.begin_along()
            item.begin_over()
        lend = remote(
            own_cross.at[0:2], own_cross.at[lent], shard_sems.at[0], shard_sems.at[1], place.partner
        )
        pl.when(section == 0)(lambda: lend.start())
        rows_at(v_up, per, rank)[...] = p_up[...].astype(BF)
        down_shard(rank)[...] = p_down[...].astype(BF)
        for kind in (UP, DOWN):
            gathers[kind].begin_over()
        for step in passing(early):
            step()
        pl.when(section == 0)(lambda: gathers[UP].begin_along())

        @pl.when(section == 1)
        def _():
            lend.wait_recv()
            gathers[CROSS].begin_along()
            gathers[CROSS].begin_over()

        for step in sharing(early):
            step()
        for item in early[:2]:
            item.finish()
        v_gains[...] = jnp.zeros_like(v_gains)
        group = PAIR // per
        for first in range(0, ranks, group):
            at = slice(first * per, (first + group) * per)
            v_table[:, at] = jnp.concatenate([s_table[one] for one in range(first, first + group)], axis=0).T
            v_gains[:n_gains, at] = jnp.concatenate(
                [packed_gains[one, :n_gains, :per] for one in range(first, first + group)], axis=1
            ).astype(F32)
        early[2].finish()

        def weights_ready(kinds):
            def before():
                queue.flush(kinds[-1])
                for kind in kinds:
                    gathers[kind].finish()

            return before

        def put_mats(value):
            o_proj[0:3] = value

        def put_out(value):
            o_out[0] = value

        def put_up(value):
            o_up[...] = value

        def put_down(value):
            o_down[...] = value

        def put_pos(value):
            o_table[...] = value

        def put_gain(value):
            o_gain[...] = value[:n_gains, :per].reshape(n_gains, 1, per)

        def put_cross(value):
            o_proj[3] = value[0]
            o_out[1] = value[1]
            handing[...] = value[2:4]

        hand = remote(handing, handed, hand_sems.at[0], hand_sems.at[1], place.partner)

        def feed_sums():
            place.meet(ready.at[0])
            for kind in (UP, DOWN):
                scatters[kind].begin()

        def table_sums():
            scatters[TABLE].begin()
            for at in range(ranks):
                gain = s_gains[:, at * per : (at + 1) * per]
                gain = jnp.concatenate([gain, jnp.zeros((8, per), F32)], axis=0)
                packed_gains[at] = jnp.concatenate([gain, jnp.zeros((16, PAIR - per), F32)], axis=1).astype(BF)
            scatters[GAIN].begin()

        def table_on():
            for step in firsts([scatters[TABLE], scatters[GAIN]]):
                step()

        def last_sums(also=()):
            scatters[MATS].begin()
            pair = [scatters[TABLE], scatters[GAIN]]
            for step in firsts([scatters[MATS]]):
                step()
            queue.flush()
            if also:
                scatters[CROSS].finish(put_cross)
                hand.start()
            for step in seconds(also) + seconds(pair) + seconds([scatters[MATS]]):
                step()
            puts = {
                UP: put_up, DOWN: put_down, OUT: put_out, MATS: put_mats, TABLE: put_pos, GAIN: put_gain,
            }
            for kind, put in puts.items():
                scatters[kind].finish(put)
    else:
        partner = {"section": 1 - section}
        barrier = pltpu.get_barrier_semaphore()
        pl.semaphore_signal(barrier, inc=1, device_id=partner, device_id_type=MESH)
        pl.semaphore_wait(barrier, 1)

    def persistent():
        if line:
            return [Ready(buf) for buf in (v_table, v_gains, v_mats, v_up, v_down, v_cross)]
        order = (4, 5, 0, 2, 3, 1)
        return [
            load(given[at], buf) for at, buf in zip(order, (v_table, v_gains, v_mats, v_up, v_down, v_cross))
        ]

    def finish(items):
        for item in items:
            item.wait()

    @pl.when(section == 0)
    def _():
        count[0] = 0
        w_table, w_gains, w_mats, w_up, w_down, _ = first = persistent()
        if line:
            gathers[DOWN].begin_along()
            pair = [gathers[UP], gathers[DOWN]]
            queue.add(None, *passing(pair[:1]), *passing(pair[1:]), *sharing(pair), DOWN)
            w_up.before = weights_ready((UP, DOWN))
        base = count[0]
        src, mixed, dy, dmixed, dq = pool["tok"][:5]
        x1, x2, dx, dv = pool["tok32"]
        hidden, slope = pool["hidden"]
        dy_t, a_t = pool["tokt"]
        v_qkv, v_weights = pool["qkv"][0], pool["weights"][0]
        for m in range(micro):
            count[0] = base
            k_qkv, k_weights, k_mixed = kept[m][:3]
            sinks = [store(k_qkv, v_qkv, axis=1), store(k_weights, v_weights), store(k_mixed, mixed)]
            encode_attend(
                load(own.at[m], src), w_table, w_gains, *code_loads(m), w_mats, *sinks, codes, cols, queue
            )
            if line and m == 0:
                lend.wait_send()
            early_sinks = sinks
            _, _, _, k_x1, k_x2, k_hidden, k_slope, _ = kept[m]
            sinks = [store(k_x1, x1), store(k_x2, x2), store(k_hidden, hidden), store(k_slope, slope)]
            encode_feed(
                Ready(src), Ready(mixed), w_table, w_gains, w_mats, w_up, w_down, box(m), *sinks,
            )
            memory = pltpu.make_async_copy(outbox.at[m], whole.at[m], local.at[sems(1)])
            memory.start()
            finish(early_sinks + sinks + [memory])
        for m in range(micro):
            count[0] = base
            last = line and m == micro - 1
            k_qkv, k_weights, k_mixed, k_x1, k_x2, k_hidden, k_slope, _ = kept[m]
            loads = [load(k_x2, x2), load(k_slope, slope), load(k_x1, x1), load(k_hidden, hidden)]
            late = [load(k_mixed, mixed), load(k_qkv, v_qkv), load(k_weights, v_weights), load(own.at[m], src)]
            sink = store(g_in.at[m], x2)
            sums = [Total(buf, m == 0) for buf in (s_mats, s_up, s_down, s_table, s_gains)]

            def fed():
                if last:
                    feed_sums()
                    scatters[OUT].begin()
                    up_steps, down_steps = seconds([scatters[UP]]), seconds([scatters[DOWN]])
                    queue.add(*in_groups(firsts([scatters[kind] for kind in (UP, DOWN, OUT)]), 4))
                    queue.add(None, None, up_steps[0], None, None, down_steps[0], None, None, up_steps[1])
                    rest = seconds([scatters[kind] for kind in (UP, DOWN, OUT)])
                    queue.add(rest[2], *rest[4:])

            encode_back(
                loads[0], box(m), w_gains, loads[1], w_down, w_up, loads[2], w_mats, loads[3], *late[:3],
                late[3], w_table, sink, *sums, dy, dy_t, a_t, dx, dmixed, dq, x1, dv,
                queue, fed, *((table_sums, table_on) if last else (nothing, nothing)),
            )
            finish([sink])
        if line:
            last_sums()
            hand.wait_recv()
            o_proj[3] = handed[0]
            o_out[1] = handed[1]
        for item in first:
            item()

    @pl.when(section == 1)
    def _():
        count[0] = 0
        w_table, w_gains, w_mats, w_up, w_down, w_cross = first = persistent()
        if line:
            gathers[UP].begin_along()
            gathers[DOWN].begin_along()
            one, two, three = [[gathers[kind]] for kind in (CROSS, UP, DOWN)]
            queue.add(*passing(one), None, *passing(two), *sharing(one), CROSS, *passing(three))
            queue.add(*sharing(two), UP, *sharing(three), DOWN)
            w_cross.before = weights_ready((CROSS,))
            w_up.before = weights_ready((UP, DOWN))
        base = count[0]
        hidden, dup = pool["hidden"]
        a_t, b_t = pool["tokt"]
        v_qkv, v_weights = pool["qkv"][0], pool["weights"][0]
        for m in range(micro):
            count[0] = base
            k_qkv, k_weights, k_mixed, k_h1 = kept[m][:4]
            tgt, mixed = pool["tok"][:2]
            sinks = [
                store(k_qkv, v_qkv, axis=1), store(k_weights, v_weights), store(k_mixed, mixed),
                store(k_h1, pool["tok32"][0]),
            ]
            self_forward(
                load(own.at[m], tgt), w_table, w_gains, *code_loads(m), w_mats, *sinks, codes, cols, queue
            )
            finish(sinks)
        for m in range(micro):
            count[0] = base
            k_h1, k_dh1, k_hidden, k_dup, k_a = kept[m][3:8]
            v_cot, out, mixed, dy, dmixed, dq = pool["tok"]
            h1, h2, dk, dv = pool["tok32"]
            sums = [Total(buf, m == 0) for buf in (s_cross, s_gains)]
            sinks = [store(whole.at[m], out), store(k_dh1, h2)]
            feeds = [store(k_a, a_t, split=False), store(k_dup, dup), store(k_hidden, hidden)]
            cross(
                load(k_h1, h1), w_gains, *code_loads(m), w_cross, box(m), w_up, w_down,
                load(cot.at[m], v_cot), sinks[0], box(m), sinks[1], *sums, *feeds, codes, cols, v_qkv,
                v_weights, mixed, h2, dy, b_t, dmixed, dq, dk, dv,
            )
            finish(sinks + feeds)
        for m in range(micro):
            count[0] = base
            k_hidden, k_dup, k_a = kept[m][5:8]
            sums = [Total(buf, m == 0) for buf in (s_up, s_down)]
            feed_grads(
                load(k_a, a_t), load(k_dup, dup), load(cot.at[m], pool["tok"][0]), load(k_hidden, hidden),
                *sums, b_t,
            )
        if line:
            feed_sums()
            pair = [scatters[UP], scatters[DOWN]]
            scatters[CROSS].begin()
            steps, late = seconds([scatters[CROSS]]), seconds(pair)
            queue.add(*in_groups(firsts([scatters[CROSS]]) + firsts(pair), 4), None, None, steps[0], None, None)
            queue.add(steps[1], None, steps[2], None, steps[3], late[0], late[1], None, None, late[2], None)
            queue.add(late[3], None, None, late[4], None, *late[5:])
        for m in range(micro):
            count[0] = base
            k_qkv, k_weights, k_mixed, _, k_dh1 = kept[m][:5]
            tgt, mixed, dy, dmixed, dq = pool["tok"][:5]
            dh1, grad, dk, dv = pool["tok32"]
            loads = [load(k_dh1, dh1), load(k_mixed, mixed), load(k_qkv, v_qkv), load(k_weights, v_weights)]
            sink = store(g_in.at[m], grad)
            sums = [Total(s_mats, m == 0), Total(s_table, m == 0), Total(s_gains, False)]
            last = line and m == micro - 1

            def mixed_done():
                if last:
                    scatters[OUT].begin()
                    queue.steps = in_groups(firsts([scatters[OUT]]), 4) + queue.steps

            self_back(
                loads[0], w_mats, *loads[1:], load(own.at[m], tgt), w_table, w_gains, sink, *sums, dy, a_t,
                b_t, dmixed, dq, dk, dv, queue, mixed_done,
                *((table_sums, table_on) if last else (nothing, nothing)),
            )
            finish([sink])
        if line:
            last_sums([scatters[OUT]])
            hand.wait_send()
        for item in first:
            item()

    for m in range(micro):
        box(m).wait()
    if not line:
        copies = [
            pltpu.make_async_copy(buf, out, local.at[at])
            for at, (buf, out) in enumerate(zip((s_mats, s_cross, s_up, s_down, s_table, s_gains), results))
        ]
        for copy in copies:
            copy.start()
        for copy in copies:
            copy.wait()


def run_step(z, line, given, results, own, cot, segments, levels):
    micro, length = own.shape[:2]
    parts = length // TB
    args = [*given, own, cot, segments, levels]
    outs = [z["outputs"], z["g_in"], *results] + [z[name] for _ in range(micro) for name in KEPT]
    scratch = [z[name] for name in PERSISTENT]
    scratch += [z[name] for name, number in POOL for _ in range(number)]
    dma = pltpu.SemaphoreType.DMA
    sems = [dma((64,)), dma((micro, parts)), dma((micro, parts))]
    if line:
        per, width = given[0].shape[1:]
        slots = 4 * LINE
        own_scratch = [
            shape((slots,) + z["packed_gains"].shape[1:], BF),
            z["packed_gains"], shape((2, per, width), F32), shape((2, per, width), F32),
        ]
        sems_line = [dma((KINDS, LINE - 1))] * 2 + [dma((KINDS, LINE))] * 2 + [dma((KINDS, 2 * LINE))] * 2
        sems_line += [dma((KINDS, LINE - 1))] * 2 + [dma((KINDS, LINE))] * 2 + [dma((KINDS, LINE, 2))] * 2
        sems_line += [pltpu.SemaphoreType.REGULAR((1,)), dma((2,)), dma((2,))]
    in_vmem, anywhere = pl.BlockSpec(memory_space=pltpu.VMEM), pl.BlockSpec(memory_space=pl.ANY)
    edge = in_vmem if line else anywhere
    vmem = [pltpu.VMEM(s.shape, s.dtype) for s in scratch]
    if line:
        scratch_shapes = vmem + sems + [pltpu.VMEM(s.shape, s.dtype) for s in own_scratch] + sems_line
    else:
        scratch_shapes = vmem + sems
    outs = pl.pallas_call(
        partial(step_kernel, z, line),
        out_shape=outs,
        in_specs=[edge] * 6 + [anywhere] * 4,
        out_specs=[anywhere] * 2 + [edge] * 6 + [anywhere] * (len(outs) - 8),
        scratch_shapes=scratch_shapes,
        compiler_params=pltpu.CompilerParams(
            collective_id=0, has_side_effects=True, vmem_limit_bytes=VMEM_BYTES
        ),
        name="step",
    )(*args)
    return place_outputs(outs[:8]) if line else outs[:8]


def place_kernel(count, *refs):
    ins, outs, bufs, sems = refs[:count], refs[count : 2 * count], refs[2 * count : 3 * count], refs[-1]
    pieces = []
    for src, dst, buf in zip(ins, outs, bufs):
        parts = 4 if src.shape[-2] % 64 == 0 else 1
        rows = src.shape[-2] // parts
        for part in range(parts):
            view = (slice(None),) * (len(src.shape) - 2) + (slice(part * rows, (part + 1) * rows),)
            pieces.append((src.at[view], buf.at[view], dst.at[view]))
    first = [pltpu.make_async_copy(src, buf, sems.at[0, at]) for at, (src, buf, _) in enumerate(pieces)]
    second = [pltpu.make_async_copy(buf, dst, sems.at[1, at]) for at, (_, buf, dst) in enumerate(pieces)]
    for copy in first:
        copy.start()
    for one, other in zip(first, second):
        one.wait()
        other.start()
    for copy in second:
        copy.wait()


def place_outputs(arrays):
    anywhere = pl.BlockSpec(memory_space=pl.ANY)
    kinds = [shape(array.shape, array.dtype) for array in arrays]
    return pl.pallas_call(
        partial(place_kernel, len(arrays)),
        out_shape=kinds,
        in_specs=[anywhere] * len(arrays),
        out_specs=[anywhere] * len(arrays),
        scratch_shapes=[pltpu.VMEM(kind.shape, kind.dtype) for kind in kinds]
        + [pltpu.SemaphoreType.DMA((2, 4 * len(arrays)))],
        compiler_params=pltpu.CompilerParams(vmem_limit_bytes=VMEM_BYTES),
        name="place",
    )(*arrays)


def body(
    inputs,
    positions,
    projections,
    out_projections,
    ffn_up,
    ffn_down,
    norm_gains,
    segments,
    levels,
    cotangent,
):
    micro, _, length, width = inputs.shape[1:]
    ranks = lax.axis_size("dp")
    per, n_gains = width // ranks, norm_gains.shape[1]
    z = sizes(length, width, ffn_up.shape[2], micro, ranks)
    rows = (inputs[0, :, 0], cotangent[:, 0], segments, levels)
    line = ranks == 4 * LINE and per * 4 == PAIR and n_gains <= 8
    if line:
        gain = norm_gains.transpose(1, 0, 2)
        given = (projections[0], out_projections[0], ffn_up[0], ffn_down[0], positions[0].T, gain)
        results = [shape(item.shape, F32) for item in given]
        whole, g_in, d_proj, d_out, d_up, d_down, d_table, d_gain = run_step(z, True, given, results, *rows)
        d_table, d_gain = d_table.T[None], d_gain.transpose(1, 0, 2)
    else:
        every = lambda value, axis: lax.all_gather(value.astype(BF), "dp", axis=axis, tiled=True)
        part = lambda value, axis: lax.psum_scatter(value, "dp", scatter_dimension=axis, tiled=True)
        to_section = lambda value, source: lax.ppermute(value, "section", [(source, 1 - source)])
        proj, outp = projections[0].astype(BF), out_projections[0].astype(BF)
        mine = jnp.stack([proj[3], outp[1]])
        gains = every(norm_gains[0], 1).astype(F32)
        given = (
            every(jnp.stack([proj[0], proj[1], proj[2], outp[0]]), 1),
            every(jnp.concatenate([mine, to_section(mine, 0)]), 1),
            every(ffn_up[0], 0), every(ffn_down[0], 0).reshape(z["down_parts"].shape), every(positions[0], 1),
            jnp.concatenate([gains, jnp.zeros((8 - n_gains, width), F32)]),
        )
        results = [z[name] for name in ("mats", "mats", "up", "down", "packed", "gains")]
        whole, g_in, d_mats, d_cross, d_up, d_down, d_table, d_gain = run_step(z, False, given, results, *rows)
        d_mats, d_cross = part(d_mats, 1).astype(F32), part(d_cross, 1)
        back = to_section(d_cross[2:], 1)
        more = jnp.where(lax.axis_index("section") == 0, back, d_cross[:2]).astype(F32)
        d_proj = jnp.concatenate([d_mats[:3], more[:1]])
        d_out = jnp.concatenate([d_mats[3:], more[1:]])
        d_up, d_down = part(d_up, 0).astype(F32), part(d_down, 0).astype(F32)
        d_table = part(d_table, 0)[0].astype(F32).T[None]
        d_gain = part(d_gain, 1)[None, :n_gains]
    return (
        whole[None, :, None],
        g_in[None, :, None],
        d_table,
        d_proj[None],
        d_out[None],
        d_up[None],
        d_down[None],
        d_gain,
    )


def solution(mesh):
    in_specs = (
        P("section", None, "dp", None, None),
        P("section", None, "dp"),
        P("section", None, "dp", None),
        P("section", None, "dp", None),
        P("section", "dp", None),
        P("section", "dp", None),
        P("section", None, "dp"),
        P(None, "dp", None),
        P(None, None, "dp", None),
        P(None, "dp", None, None),
    )
    out_specs = (
        P("section", None, "dp", None, None),
        P("section", None, "dp", None, None),
        P("section", None, "dp"),
        P("section", None, "dp", None),
        P("section", None, "dp", None),
        P("section", "dp", None),
        P("section", "dp", None),
        P("section", None, "dp"),
    )
    return jax.shard_map(body, mesh=mesh, in_specs=in_specs, out_specs=out_specs, check_vma=False)
```

```python
from functools import partial

import jax
import jax.numpy as jnp
from jax import lax
from jax.experimental import pallas as pl
from jax.experimental.pallas import tpu as pltpu
from jax.sharding import PartitionSpec as P

BF = jnp.bfloat16
F32 = jnp.float32
DH = 64
PAIR = 2 * DH
QB = 128
WIN = 256
TB = 256
MESH = pl.DeviceIdType.MESH
VMEM_BYTES = 62 * 1024 * 1024


def nn(left, right):
    return jnp.dot(left, right, preferred_element_type=F32)


def nt(left, right):
    return lax.dot_general(left, right, (((1,), (1,)), ((), ())), preferred_element_type=F32)


def tn(left, right):
    return lax.dot_general(left, right, (((0,), (0,)), ((), ())), preferred_element_type=F32)


def norm_parts(stream):
    centred = stream - jnp.mean(stream, axis=-1, keepdims=True)
    scale = lax.rsqrt(jnp.mean(centred * centred, axis=-1, keepdims=True) + 1e-05)
    return centred * scale, scale


def norm_back(grad, unit, scale, gain):
    inner = grad * gain
    first = jnp.mean(inner, axis=-1, keepdims=True)
    second = jnp.mean(inner * unit, axis=-1, keepdims=True)
    return scale * (inner - first - unit * second), jnp.sum(grad * unit, axis=0, keepdims=True)


def block_at(index, size):
    if isinstance(index, int):
        return pl.ds(index * size, size)
    return pl.ds(pl.multiple_of(index * size, size), size)


def lane_halves(scale=1.0):
    lane = lax.broadcasted_iota(jnp.int32, (1, PAIR), 1)
    low = jnp.where(lane < DH, scale, 0.0).astype(BF)
    high = jnp.where(lane < DH, 0.0, scale).astype(BF)
    return low, high


def both_heads(block, halves):
    return jnp.concatenate([block * halves[0], block * halves[1]], axis=0)


def join_heads(stacked):
    lane = lax.broadcasted_iota(jnp.int32, (QB, PAIR), 1)
    return jnp.where(lane < DH, stacked[:QB], stacked[QB:])


def window_start(index, length):
    return pl.multiple_of(jnp.clip(index * QB - DH, 0, length - WIN), DH)


def make_codes(segments, source_level, target_level, codes_ref, cols_ref):
    segment = segments[...]
    length = segment.shape[1]
    before = pltpu.roll(segment, 1, axis=1)
    lane = lax.broadcasted_iota(jnp.int32, (1, length), 1)
    first = (lane == 0) | (segment != before)
    usable = jnp.where(first | (source_level[...] > 0), segment, -1)
    row = lax.broadcasted_iota(jnp.int32, (8, length), 0)
    codes = jnp.where(row == 0, usable, jnp.where(row == 1, segment, target_level[...]))
    codes_ref[...] = codes
    cols_ref[...] = codes.T


def mask_bias(index, start, codes_ref, cols_ref, causal):
    keys = cols_ref[pl.ds(start, WIN), :]
    queries = codes_ref[:, block_at(index, QB)]
    query_segment = queries[1:2, :]
    if causal:
        key_id = start + lax.broadcasted_iota(jnp.int32, (WIN, QB), 0)
        query_id = index * QB + lax.broadcasted_iota(jnp.int32, (WIN, QB), 1)
        allowed = (keys[:, 1:2] == query_segment) & (
            (keys[:, 2:3] < queries[2:3, :]) | (key_id == query_id)
        )
    else:
        allowed = keys[:, 0:1] == query_segment
    bias = jnp.where(allowed, 0.0, -1e30)
    return jnp.concatenate([bias, bias], axis=1)


def attend_block(index, q_ref, k_ref, v_ref, codes_ref, cols_ref, weights_ref, mixed_ref, causal):
    length, width = q_ref.shape
    start = window_start(index, length)
    rows = block_at(index, QB)
    bias = mask_bias(index, start, codes_ref, cols_ref, causal)
    halves = lane_halves(DH ** -0.5)
    for pair in range(width // PAIR):
        lanes = slice(pair * PAIR, (pair + 1) * PAIR)
        queries = both_heads(q_ref[rows, lanes], halves)
        scores = nt(k_ref[pl.ds(start, WIN), lanes], queries) + bias
        shifted = jnp.exp(scores - jnp.max(scores, axis=0, keepdims=True))
        weights = (shifted * (1.0 / jnp.sum(shifted, axis=0, keepdims=True))).astype(BF)
        weights_ref[index, pair] = weights
        out = tn(weights, v_ref[pl.ds(start, WIN), lanes])
        mixed_ref[rows, lanes] = join_heads(out).astype(BF)


def attend_back_block(
    index, q_ref, k_ref, v_ref, weights_ref, mixed_ref, dmixed_ref, dq_ref, dk_ref, dv_ref
):
    length, width = q_ref.shape
    start = window_start(index, length)
    rows = block_at(index, QB)
    window = pl.ds(start, WIN)
    plain = lane_halves()
    halves = lane_halves(DH ** -0.5)
    ones = jnp.ones((WIN, PAIR), BF)
    for pair in range(width // PAIR):
        lanes = slice(pair * PAIR, (pair + 1) * PAIR)
        queries = both_heads(q_ref[rows, lanes], halves)
        keys = k_ref[window, lanes]
        values = v_ref[window, lanes]
        weights = weights_ref[index, pair]
        dmixed = dmixed_ref[rows, lanes]
        grads = both_heads(dmixed, plain)
        inner = (dmixed.astype(F32) * mixed_ref[rows, lanes].astype(F32) * -1.0).astype(BF)
        left = jnp.concatenate([values, ones], axis=1)
        right = jnp.concatenate([grads, both_heads(inner, plain)], axis=1)
        centred = nt(left, right)
        dscores = (weights.astype(F32) * centred).astype(BF)
        dv_ref[window, lanes] += nn(weights, grads)
        dk_ref[window, lanes] += nn(dscores, queries)
        dq = tn(dscores, keys) * (DH ** -0.5)
        dq_ref[rows, lanes] = join_heads(dq).astype(BF)


def gelu_parts(value):
    cdf = 0.5 + 0.5 * lax.erf(value * (0.5 ** 0.5))
    density = jnp.exp(value * value * -0.5) * 0.3989422804014327
    return value * cdf, cdf + value * density


def feed_block(normed, up_ref, down_ref, hidden_ref, slope_ref, rows):
    total = None
    width, step = up_ref.shape[1], down_ref.shape[1]
    for at in range(0, width, step):
        hidden, slope = gelu_parts(nn(normed, up_ref[:, at : at + step]))
        hidden = hidden.astype(BF)
        hidden_ref[rows, at : at + step] = hidden
        slope_ref[rows, at : at + step] = slope.astype(BF)
        term = nn(hidden, down_ref[at // step])
        total = term if total is None else total + term
    return total


def feed_back_block(grad, up_ref, down_ref, slope_ref, rows):
    total = None
    width, step = up_ref.shape[1], down_ref.shape[1]
    for at in range(0, width, step):
        dhidden = nt(grad, down_ref[at // step])
        dup = (dhidden * slope_ref[rows, at : at + step].astype(F32)).astype(BF)
        slope_ref[rows, at : at + step] = dup
        term = nt(dup, up_ref[:, at : at + step])
        total = term if total is None else total + term
    return total


class Queue:
    def __init__(self):
        self.steps = []

    def add(self, *groups):
        self.steps.extend(groups)

    def next(self):
        while self.steps and isinstance(self.steps[0], int):
            self.steps.pop(0)
        return self.steps.pop(0) if self.steps else None

    def flush(self, mark=None):
        if mark is not None and mark not in self.steps:
            return
        while self.steps:
            step = self.steps.pop(0)
            if step == mark and mark is not None:
                return
            if callable(step):
                step()


def loop(count, body, queue=None):
    hooks = [queue.next() if queue else None for _ in range(count)]

    def step(index, carry):
        body(index)
        for turn, hook in enumerate(hooks):
            if hook is not None:
                pl.when(index == turn)(hook)
        return carry

    lax.fori_loop(0, count, step, 0)


def put_grad(out, index, value):
    if out.prior is not None:
        value = value + out.buf[index].astype(F32)
    out.buf[index] = value.astype(BF)


def weight_grad(out, left_t_refs, right_refs, transposed):
    step = 512
    width = right_refs[0].shape[1]

    def slab(index):
        cols = block_at(index, step)
        value = None
        for left_t, right in zip(left_t_refs, right_refs):
            term = nn(left_t[...], right[:, cols])
            value = term if value is None else value + term
        if transposed:
            put_grad(out, (cols, slice(None)), value.T)
        else:
            put_grad(out, (slice(None), cols), value)

    loop(width // step, slab)


def put_table(out, rows, value):
    value = value.T.reshape(out.buf.shape[:2] + (value.shape[0],))
    put_grad(out, (slice(None), slice(None), rows), value)


def add_gain(out, row, value):
    out.buf[row : row + 1, :] += value


class Source:
    def __init__(self, hbm, buf, sem):
        self.buf, self.copy, self.here = buf, pltpu.make_async_copy(hbm, buf, sem), False
        self.copy.start()

    def __call__(self):
        if not self.here:
            self.copy.wait()
            self.here = True
        return self.buf


class Sink:
    def __init__(self, hbm, buf, sems, first, parts, axis, prior):
        self.hbm, self.buf, self.sems, self.first = hbm, buf, sems, first
        self.parts, self.axis, self.prior = parts, axis, prior

    def copy(self, part):
        view = [slice(None)] * len(self.buf.shape)
        size = self.buf.shape[self.axis] // self.parts
        view[self.axis] = block_at(part, size)
        view = tuple(view)
        return pltpu.make_async_copy(
            self.buf.at[view], self.hbm.at[view], self.sems.at[self.first + part]
        )

    def send(self, part=0):
        self.copy(part).start()

    def wait(self):
        for part in range(self.parts):
            self.copy(part).wait()


class Ready:
    def __init__(self, buf, before=None):
        self.buf, self.before = buf, before

    def __call__(self):
        if self.before is not None:
            self.before()
            self.before = None
        return self.buf


class Total:
    def __init__(self, buf, first):
        self.buf = buf
        self.prior = None if first else buf


class Link:
    def __init__(self, outbox, inbox, send, recv, parts):
        self.buf, self.inbox, self.sems, self.parts = outbox, inbox, (send, recv), parts

    def copy(self, part):
        size = self.buf.shape[0] // self.parts
        rows = block_at(part, size)
        return pltpu.make_async_remote_copy(
            src_ref=self.buf.at[rows, :], dst_ref=self.inbox.at[rows, :],
            send_sem=self.sems[0].at[part], recv_sem=self.sems[1].at[part],
            device_id={"section": 1 - lax.axis_index("section")}, device_id_type=MESH,
        )

    def send(self, part):
        self.copy(part).start()

    def wait(self):
        for part in range(self.parts):
            self.copy(part).wait_send()

    def come(self, part):
        self.copy(part).wait_recv()


def encode_attend(src, table, gains, segments, source_level, target_level, mats, qkv, weights, mixed, codes, cols, queue):
    length = src.buf.shape[0]
    make_codes(segments(), source_level(), target_level(), codes, cols)
    src, table, gains, mats = src(), table(), gains(), mats()

    def project(index):
        rows = block_at(index, TB)
        unit, _ = norm_parts(src[rows, :].astype(F32) + table[rows, :].astype(F32))
        normed = (unit * gains[0:1, :]).astype(BF)
        for which in range(3):
            qkv.buf[which, rows, :] = nn(normed, mats[which]).astype(BF)
        qkv.send(index)

    loop(length // TB, project, queue)

    def attend(index):
        for part in range(TB // QB):
            attend_block(
                index * (TB // QB) + part,
                qkv.buf.at[0], qkv.buf.at[1], qkv.buf.at[2], codes, cols, weights.buf, mixed.buf, False,
            )
        weights.send(index)
        mixed.send(index)

    loop(length // TB, attend, queue)


def encode_feed(src, mixed, table, gains, mats, up, down, mem, x1, x2, hidden, slope):
    length = src.buf.shape[0]
    table, gains, mats, up, down = table(), gains(), mats(), up(), down()
    src, mixed = src(), mixed()

    def rest(index):
        rows = block_at(index, TB)
        stream = src[rows, :].astype(F32) + table[rows, :].astype(F32)
        stream = stream + nn(mixed[rows, :], mats[3])
        x1.buf[rows, :] = stream
        x1.send(index)
        unit, _ = norm_parts(stream)
        normed = (unit * gains[1:2, :]).astype(BF)
        stream = stream + feed_block(normed, up, down, hidden.buf, slope.buf, rows)
        x2.buf[rows, :] = stream
        unit, _ = norm_parts(stream)
        mem.buf[rows, :] = (unit * gains[2:3, :]).astype(BF)
        for item in (mem, x2, hidden, slope):
            item.send(index)

    loop(length // TB, rest)


def encode_back(
    x2, dmem, gains, slope, down, up, x1, mats, hidden, mixed, qkv, weights, src, table,
    g_in, g_mats, g_up, g_down, g_table, g_gains,
    dy, dy_t, a_t, dx, dmixed, dq, dk, dv, queue, fed, tabled, passed,
):
    length = src.buf.shape[0]
    if g_gains.prior is None:
        g_gains.buf[...] = jnp.zeros_like(g_gains.buf)
    x2, gains, slope, down, up, x1, mats = x2(), gains(), slope(), down(), up(), x1(), mats()

    def feed_step(index):
        rows = block_at(index, TB)
        dmem.come(index)
        unit, scale = norm_parts(x2[rows, :])
        grad, d_gain = norm_back(dmem.inbox[rows, :].astype(F32), unit, scale, gains[2:3, :])
        add_gain(g_gains, 2, d_gain)
        low = grad.astype(BF)
        dy_t[:, rows] = low.T
        dnormed = feed_back_block(low, up, down, slope, rows)
        unit, scale = norm_parts(x1[rows, :])
        a_t[:, rows] = (unit * gains[1:2, :]).astype(BF).T
        back, d_gain = norm_back(dnormed, unit, scale, gains[1:2, :])
        add_gain(g_gains, 1, d_gain)
        grad = grad + back
        dx[rows, :] = grad
        low = grad.astype(BF)
        dy[rows, :] = low
        dmixed[rows, :] = nt(low, mats[3]).astype(BF)

    loop(length // TB, feed_step)
    weight_grad(g_up, [a_t], [slope], False)
    weight_grad(g_down, [dy_t], [hidden()], True)
    mixed = mixed()
    put_grad(g_mats, 3, tn(mixed[...], dy[...]))
    fed()
    qkv, weights = qkv(), weights()
    dk[...] = jnp.zeros_like(dk)
    dv[...] = jnp.zeros_like(dv)

    def attend_step(index):
        attend_back_block(
            index, qkv.at[0], qkv.at[1], qkv.at[2], weights, mixed, dmixed, dq, dk, dv
        )

    loop(length // QB, attend_step, queue)
    src, table = src(), table()

    def project_step(index):
        rows = block_at(index, TB)
        unit, scale = norm_parts(src[rows, :].astype(F32) + table[rows, :].astype(F32))
        a_t[:, rows] = (unit * gains[0:1, :]).astype(BF).T
        dnormed = nt(dq[rows, :], mats[0])
        dnormed += nt(dk[rows, :].astype(BF), mats[1])
        dnormed += nt(dv[rows, :].astype(BF), mats[2])
        back, d_gain = norm_back(dnormed, unit, scale, gains[0:1, :])
        add_gain(g_gains, 0, d_gain)
        grad = dx[rows, :] + back
        g_in.buf[rows, :] = grad
        g_in.send(index)
        put_table(g_table, rows, grad)

    loop(length // TB, project_step, queue)
    tabled()
    put_grad(g_mats, 0, nn(a_t[...], dq[...]))
    passed()
    put_grad(g_mats, 1, nn(a_t[...], dk[...].astype(BF)))
    put_grad(g_mats, 2, nn(a_t[...], dv[...].astype(BF)))


def self_forward(tgt, table, gains, segments, source_level, target_level, mats, qkv, weights, mixed, h1, codes, cols, queue):
    length = tgt.buf.shape[0]
    make_codes(segments(), source_level(), target_level(), codes, cols)
    tgt, table, gains, mats = tgt(), table(), gains(), mats()

    def project(index):
        rows = block_at(index, TB)
        stream = table[rows, :].astype(F32)
        unit, _ = norm_parts(stream)
        qkv.buf[0, rows, :] = nn((unit * gains[0:1, :]).astype(BF), mats[0]).astype(BF)
        unit, _ = norm_parts(tgt[rows, :].astype(F32) + stream)
        normed = (unit * gains[0:1, :]).astype(BF)
        for which in (1, 2):
            qkv.buf[which, rows, :] = nn(normed, mats[which]).astype(BF)
        qkv.send(index)

    loop(length // TB, project, queue)

    def rest(index):
        for part in range(TB // QB):
            attend_block(
                index * (TB // QB) + part,
                qkv.buf.at[0], qkv.buf.at[1], qkv.buf.at[2], codes, cols, weights.buf, mixed.buf, True,
            )
        rows = block_at(index, TB)
        h1.buf[rows, :] = table[rows, :].astype(F32) + nn(mixed.buf[rows, :], mats[3])
        for item in (weights, mixed, h1):
            item.send(index)

    loop(length // TB, rest, queue)


def self_back(
    dh1, mats, mixed, qkv, weights, tgt, table, gains,
    g_in, g_mats, g_table, g_gains,
    dy, a_t, b_t, dmixed, dq, dk, dv, queue, mixed_done, tabled, passed,
):
    length = tgt.buf.shape[0]
    dk[...] = jnp.zeros_like(dk)
    dv[...] = jnp.zeros_like(dv)
    dh1, mats, mixed = dh1(), mats(), mixed()

    def out_step(index):
        rows = block_at(index, TB)
        low = dh1[rows, :].astype(BF)
        dy[rows, :] = low
        dmixed[rows, :] = nt(low, mats[3]).astype(BF)

    loop(length // TB, out_step)
    put_grad(g_mats, 3, tn(mixed[...], dy[...]))
    mixed_done()
    qkv, weights = qkv(), weights()

    def attend_step(index):
        attend_back_block(
            index, qkv.at[0], qkv.at[1], qkv.at[2], weights, mixed, dmixed, dq, dk, dv
        )

    loop(length // QB, attend_step, queue)
    tgt, table, gains = tgt(), table(), gains()

    def project_step(index):
        rows = block_at(index, TB)
        stream = table[rows, :].astype(F32)
        unit, scale = norm_parts(stream)
        a_t[:, rows] = (unit * gains[0:1, :]).astype(BF).T
        back, d_gain = norm_back(nt(dq[rows, :], mats[0]), unit, scale, gains[0:1, :])
        dtable = dh1[rows, :] + back
        unit, scale = norm_parts(tgt[rows, :].astype(F32) + stream)
        b_t[:, rows] = (unit * gains[0:1, :]).astype(BF).T
        dnormed = nt(dk[rows, :].astype(BF), mats[1])
        dnormed += nt(dv[rows, :].astype(BF), mats[2])
        back, d_gain_too = norm_back(dnormed, unit, scale, gains[0:1, :])
        add_gain(g_gains, 0, d_gain + d_gain_too)
        g_in.buf[rows, :] = back
        g_in.send(index)
        put_table(g_table, rows, dtable + back)

    loop(length // TB, project_step, queue)
    tabled()
    put_grad(g_mats, 0, nn(a_t[...], dq[...]))
    passed()
    put_grad(g_mats, 1, nn(b_t[...], dk[...].astype(BF)))
    put_grad(g_mats, 2, nn(b_t[...], dv[...].astype(BF)))


def feed_grads(a_t, dup, cot, hidden, g_up, g_down, cot_t):
    cot_t[...] = cot()[...].T
    weight_grad(g_up, [a_t()], [dup()], False)
    weight_grad(g_down, [cot_t], [hidden()], True)


def cross(
    h1, gains, segments, source_level, target_level, mats, mem, up, down, cot,
    out, dmem, dh1, g_mats, g_gains, a_t, dup, hidden,
    codes, cols, qkv, weights, mixed, h2, dy, b_t, dmixed, dq, dk, dv,
):
    length = h1.buf.shape[0]
    make_codes(segments(), source_level(), target_level(), codes, cols)
    if g_gains.prior is None:
        g_gains.buf[...] = jnp.zeros_like(g_gains.buf)
    dk[...] = jnp.zeros_like(dk)
    dv[...] = jnp.zeros_like(dv)
    h1, gains, mats = h1(), gains(), mats()
    memory = mem.inbox

    def project(index):
        rows = block_at(index, TB)
        unit, _ = norm_parts(h1[rows, :])
        qkv[0, rows, :] = nn((unit * gains[1:2, :]).astype(BF), mats[0]).astype(BF)
        mem.come(index)
        qkv[1, rows, :] = nn(memory[rows, :], mats[2]).astype(BF)
        qkv[2, rows, :] = nn(memory[rows, :], mats[3]).astype(BF)

    loop(length // TB, project)
    up, down, cot = up(), down(), cot()

    def attend(index):
        for part in range(TB // QB):
            attend_block(
                index * (TB // QB) + part,
                qkv.at[0], qkv.at[1], qkv.at[2], codes, cols, weights, mixed, False,
            )

    def feed(index):
        rows = block_at(index, TB)
        stream = h1[rows, :] + nn(mixed[rows, :], mats[1])
        unit, scale = norm_parts(stream)
        normed = (unit * gains[2:3, :]).astype(BF)
        a_t.buf[:, rows] = normed.T
        fed = feed_block(normed, up, down, hidden.buf, dup.buf, rows)
        out.buf[rows, :] = (stream + fed).astype(BF)
        low = cot[rows, :]
        dnormed = feed_back_block(low, up, down, dup.buf, rows)
        back, d_gain = norm_back(dnormed, unit, scale, gains[2:3, :])
        add_gain(g_gains, 2, d_gain)
        grad = low.astype(F32) + back
        h2[rows, :] = grad
        low = grad.astype(BF)
        dy[rows, :] = low
        dmixed[rows, :] = nt(low, mats[1]).astype(BF)
        for item in (out, hidden, dup):
            item.send(index)

    attend(0)

    def middle(index):
        feed(index)
        attend(index + 1)

    loop(length // TB - 1, middle)
    feed(length // TB - 1)
    a_t.send()

    def attend_step(index):
        def one(at):
            attend_back_block(at, qkv.at[0], qkv.at[1], qkv.at[2], weights, mixed, dmixed, dq, dk, dv)

        steps = TB // QB
        last = length // TB - 1
        pl.when(index == 0)(lambda: one(0))
        for part in range(1, steps):
            one(index * steps + part)
        pl.when(index < last)(lambda: one((index + 1) * steps))
        rows = block_at(index, TB)
        dkeys = dk[rows, :].astype(BF)
        dvalues = dv[rows, :].astype(BF)
        dmem.buf[rows, :] = (nt(dkeys, mats[2]) + nt(dvalues, mats[3])).astype(BF)
        dmem.send(index)

    loop(length // TB, attend_step)

    def project_step(index):
        rows = block_at(index, TB)
        unit, scale = norm_parts(h1[rows, :])
        b_t[:, rows] = (unit * gains[1:2, :]).astype(BF).T
        back, d_gain = norm_back(nt(dq[rows, :], mats[0]), unit, scale, gains[1:2, :])
        add_gain(g_gains, 1, d_gain)
        dh1.buf[rows, :] = h2[rows, :] + back
        dh1.send(index)

    loop(length // TB, project_step)
    put_grad(g_mats, 0, nn(b_t[...], dq[...]))
    put_grad(g_mats, 1, tn(mixed[...], dy[...]))
    put_grad(g_mats, 2, tn(memory[...], dk[...].astype(BF)))
    put_grad(g_mats, 3, tn(memory[...], dv[...].astype(BF)))


def shape(dims, kind):
    return jax.ShapeDtypeStruct(dims, kind)


def sizes(length, width, ff, micro, ranks):
    blocks = length // QB
    pairs = width // PAIR
    return dict(
        tok=shape((length, width), BF),
        tok32=shape((length, width), F32),
        outputs=shape((micro, length, width), BF),
        g_in=shape((micro, length, width), F32),
        qkv=shape((3, length, width), BF),
        weights=shape((blocks, pairs, WIN, 2 * QB), BF),
        hidden=shape((length, ff), BF),
        tokt=shape((width, length), BF),
        packed=shape((ranks, width // ranks, length), BF),
        packed_gains=shape((ranks, 16, PAIR), BF),
        mats=shape((4, width, width), BF),
        up=shape((width, ff), BF),
        down=shape((ff, width), BF),
        down_parts=shape((ff // width, width, width), BF),
        gains=shape((8, width), F32),
        pair=shape((2, width, width), BF),
        row=shape((1, length), jnp.int32),
        codes=shape((8, length), jnp.int32),
        cols=shape((length, 8), jnp.int32),
    )


LINE = 4
AHEAD = (2, 1, 3, 0)
TABLE, GAIN, MATS, UP, DOWN, CROSS, OUT = range(7)
KINDS = 7


def rank_of(z, x, core):
    return z * 4 + x * 2 + core


def remote(src, dst, send, recv, to):
    return pltpu.make_async_remote_copy(
        src_ref=src, dst_ref=dst, send_sem=send, recv_sem=recv, device_id=to, device_id_type=MESH
    )


def rows_at(ref, per, rank):
    view = [slice(None)] * len(ref.shape)
    view[-2] = pl.ds(pl.multiple_of(rank * per, 16), per)
    return ref.at[tuple(view)]


class Place:
    def __init__(self):
        me = lax.axis_index("dp")
        self.z, self.x, self.core = me // 4, (me // 2) % 2, me % 2
        self.rank = me
        self.section = lax.axis_index("section")
        self.partner = {"section": 1 - self.section}
        self.across = {"dp": rank_of(self.z, 1 - self.x, self.core)}
        self.sibling = {"dp": rank_of(self.z, self.x, 1 - self.core)}

    def ahead(self, step):
        return (self.z + step) % LINE

    def on_line(self, step):
        return {"dp": rank_of(self.ahead(step), self.x, self.core)}

    def line(self, other):
        return 1 - self.x if other else self.x

    def meet(self, semaphore, also=()):
        devices = [self.across, self.sibling, *also] + [self.on_line(step) for step in range(1, LINE)]
        for device in devices:
            pl.semaphore_signal(semaphore, inc=1, device_id=device, device_id_type=MESH)
        pl.semaphore_wait(semaphore, len(devices))


class Gather:
    def __init__(self, place, kind, view, sems):
        self.place, self.kind, self.view = place, kind, view
        self.zsend, self.zrecv, self.xsend, self.xrecv, self.csend, self.crecv = sems

    def block(self, back, other):
        place = self.place
        return self.view(rank_of(place.ahead(LINE - back), place.line(other), place.core))

    def along(self, step):
        at, block = (self.kind, step - 1), self.block(0, 0)
        return remote(block, block, self.zsend.at[at], self.zrecv.at[at], self.place.on_line(step))

    def over(self, back):
        at, block = (self.kind, back), self.block(back, 0)
        return remote(block, block, self.xsend.at[at], self.xrecv.at[at], self.place.across)

    def beside(self, back, other):
        at, block = (self.kind, back + LINE * other), self.block(back, other)
        return remote(block, block, self.csend.at[at], self.crecv.at[at], self.place.sibling)

    def begin_along(self):
        for step in (1, 3, 2):
            self.along(step).start()

    def begin_over(self):
        self.over(0).start()
        self.beside(0, 0).start()

    def pass_on(self, back):
        self.along(back).wait_recv()
        self.over(back).start()
        self.beside(back, 0).start()

    def share(self, back):
        self.over(back).wait_recv()
        self.beside(back, 1).start()

    def finish(self):
        for step in range(1, LINE):
            self.along(step).wait_send()
        for back in range(LINE):
            self.over(back).wait_send()
            for other in range(2):
                copy = self.beside(back, other)
                copy.wait_send()
                copy.wait_recv()


def passing(arrays):
    return [partial(array.pass_on, back) for back in (1, 3, 2) for array in arrays]


def sharing(arrays):
    return [partial(array.share, back) for back in (0, 1, 3, 2) for array in arrays]


def in_groups(steps, size):
    def group(some):
        return lambda: [step() for step in some] and None

    return [group(steps[at : at + size]) for at in range(0, len(steps), size)]


class Scatter:
    def __init__(self, place, kind, view, slots, sems):
        self.place, self.kind, self.view, self.slots = place, kind, view, slots
        self.zsend, self.zrecv, self.xsend, self.xrecv, self.csend, self.crecv = sems

    def from_core(self, step, part):
        return self.slots(step * 2 + part)

    def from_x(self, step):
        return self.slots(2 * LINE + step)

    def from_z(self, step):
        return self.slots(3 * LINE + step - 1)

    def own(self, step, part, its_core):
        return self.view(rank_of(self.place.ahead(step), self.place.line(1 - part), its_core))

    def beside(self, step, part):
        at = (self.kind, step, part)
        return remote(
            self.own(step, part, 1 - self.place.core), self.from_core(step, part), self.csend.at[at],
            self.crecv.at[at], self.place.sibling,
        )

    def over(self, step):
        at = (self.kind, step)
        return remote(
            self.from_core(step, 0), self.from_x(step), self.xsend.at[at], self.xrecv.at[at],
            self.place.across,
        )

    def along(self, step):
        at = (self.kind, step - 1)
        return remote(
            self.from_core(step, 1), self.from_z(step), self.zsend.at[at], self.zrecv.at[at],
            self.place.on_line(step),
        )

    def total(self, *terms):
        value = terms[0][...].astype(F32)
        for term in terms[1:]:
            value = value + term[...].astype(F32)
        return value

    def begin(self):
        for part in range(2):
            for step in AHEAD:
                self.beside(step, part).start()

    def first(self, step):
        self.beside(step, 0).wait_recv()
        both = self.from_core(step, 0)
        both[...] = self.total(both, self.own(step, 0, self.place.core)).astype(BF)
        self.over(step).start()

    def second(self, step):
        self.beside(step, 1).wait_recv()
        self.over(step).wait_recv()
        four = self.from_core(step, 1)
        four[...] = self.total(four, self.own(step, 1, self.place.core), self.from_x(step)).astype(BF)
        if step:
            self.along(step).start()

    def finish(self, put):
        for step in range(1, LINE):
            self.along(step).wait_recv()
        put(self.total(self.from_core(0, 1), *[self.from_z(step) for step in range(1, LINE)]))
        for step in range(LINE):
            self.over(step).wait_send()
            if step:
                self.along(step).wait_send()
            for part in range(2):
                self.beside(step, part).wait_send()


def firsts(arrays):
    return [partial(array.first, step) for step in AHEAD for array in arrays]


def seconds(arrays):
    return [partial(array.second, step) for step in AHEAD for array in arrays]


POOL = (("row", 3), ("tok", 6), ("tok32", 4), ("tokt", 2), ("qkv", 1), ("weights", 1), ("hidden", 2))
KEPT = ("qkv", "weights", "tok", "tok32", "tok32", "hidden", "hidden", "tokt")
PERSISTENT = (
    "tok", "gains", "mats", "up", "down_parts", "mats", "mats", "mats", "up", "down", "packed", "gains", "codes",
    "cols", "outputs", "outputs",
)


def nothing():
    return None


def step_kernel(z, line, *refs):
    refs = list(refs)
    take = lambda count: [refs.pop(0) for _ in range(count)]
    given, (own, cot, segments, levels) = take(6), take(4)
    whole, g_in = take(2)
    results = take(6)
    micro, length = own.shape[:2]
    parts = length // TB
    kept = [take(len(KEPT)) for _ in range(micro)]
    (
        v_table, v_gains, v_mats, v_up, v_down, v_cross, s_mats, s_cross, s_up, s_down, s_table, s_gains,
        codes, cols, inbox, outbox,
    ) = take(len(PERSISTENT))
    pool = {name: take(count) for name, count in POOL}
    local, ysend, yrecv = take(3)
    section = lax.axis_index("section")
    count = [0]

    def sems(number):
        count[0] += number
        return count[0] - number

    def load(hbm, buf):
        return Source(hbm, buf, local.at[sems(1)])

    def store(hbm, buf, axis=0, split=True):
        number = parts if split else 1
        return Sink(hbm, buf, local, sems(number), number, axis, None)

    def box(m):
        return Link(outbox.at[m], inbox.at[m], ysend.at[m], yrecv.at[m], parts)

    def code_loads(m):
        hbm = (segments.at[m], levels.at[0, m], levels.at[1, m])
        return [load(ref, buf) for ref, buf in zip(hbm, pool["row"])]

    queue = Queue()
    if line:
        o_proj, o_out, o_up, o_down, o_table, o_gain = results
        r_gains, packed_gains, handing, handed = take(4)
        g_sems, s_sems = take(6), take(6)
        ready, shard_sems, hand_sems = refs
        place = Place()
        per, n_gains = o_table.shape[0], o_gain.shape[0]
        ranks = s_table.shape[0]
        rank, lent = place.rank, slice(2, 4)

        def down_shard(at):
            tall = o_down.shape[0]
            inside = v_down.shape[1] // tall
            return v_down.at[at // inside, pl.ds(pl.multiple_of(at % inside * tall, 16), tall), :]

        view_of = {
            TABLE: lambda at: s_table.at[at],
            GAIN: lambda at: packed_gains.at[at],
            MATS: lambda at: rows_at(v_mats, per, at),
            UP: lambda at: rows_at(v_up, per, at),
            DOWN: down_shard,
            CROSS: lambda at: rows_at(v_cross, per, at),
        }
        gathers = {kind: Gather(place, kind, view, g_sems) for kind, view in view_of.items()}
        sum_of = {
            TABLE: lambda at: s_table.at[at],
            GAIN: lambda at: packed_gains.at[at],
            MATS: lambda at: rows_at(s_mats.at[0:3], per, at),
            UP: lambda at: rows_at(s_up, per, at),
            DOWN: lambda at: rows_at(s_down, o_down.shape[0], at),
            CROSS: lambda at: rows_at(s_cross, per, at),
            OUT: lambda at: rows_at(s_mats.at[3], per, at),
        }
        width = v_mats.shape[-1]
        hidden_0, hidden_1 = pool["hidden"]
        slots = 4 * LINE

        def in_hidden(buf, first, tall, wide):
            across = buf.shape[1] // wide

            def slot(number):
                row, lane = first + number // across * tall, number % across * wide
                return buf.at[row : row + tall, lane : lane + wide]

            return slot

        slot_of = {
            TABLE: in_hidden(hidden_0, slots * per, per, length),
            GAIN: lambda number: r_gains.at[number],
            MATS: lambda number: v_down.at[0:3, number * per : (number + 1) * per, :],
            UP: in_hidden(hidden_0, 0, per, hidden_0.shape[1]),
            DOWN: in_hidden(hidden_1, 0, o_down.shape[0], width),
            CROSS: lambda number: v_cross.at[:, number * per : (number + 1) * per, :],
            OUT: in_hidden(hidden_1, slots // (hidden_1.shape[1] // width) * o_down.shape[0], per, width),
        }
        scatters = {
            kind: Scatter(place, kind, view, slot_of[kind], s_sems) for kind, view in sum_of.items()
        }

        p_proj, p_out, p_up, p_down, p_pos, p_gain = given
        s_table[rank] = p_pos[...].astype(BF)
        gain = jnp.concatenate([p_gain[...].reshape(n_gains, per), jnp.zeros((16 - n_gains, per), F32)], axis=0)
        packed_gains[rank] = jnp.concatenate([gain, jnp.zeros((16, PAIR - per), F32)], axis=1).astype(BF)
        own_mats = rows_at(v_mats, per, rank)
        for to, shard in enumerate((p_proj.at[0], p_proj.at[1], p_proj.at[2], p_out.at[0])):
            own_mats[to] = shard[...].astype(BF)
        own_cross = rows_at(v_cross, per, rank)
        for to, shard in enumerate((p_proj.at[3], p_out.at[1])):
            own_cross[to] = shard[...].astype(BF)
        place.meet(pltpu.get_barrier_semaphore(), (place.partner,))
        early = [gathers[kind] for kind in (GAIN, TABLE, MATS)]
        for item in early:
            item.begin_along()
            item.begin_over()
        lend = remote(
            own_cross.at[0:2], own_cross.at[lent], shard_sems.at[0], shard_sems.at[1], place.partner
        )
        pl.when(section == 0)(lambda: lend.start())
        rows_at(v_up, per, rank)[...] = p_up[...].astype(BF)
        down_shard(rank)[...] = p_down[...].astype(BF)
        for kind in (UP, DOWN):
            gathers[kind].begin_over()
        for step in passing(early):
            step()
        pl.when(section == 0)(lambda: gathers[UP].begin_along())

        @pl.when(section == 1)
        def _():
            lend.wait_recv()
            gathers[CROSS].begin_along()
            gathers[CROSS].begin_over()

        for step in sharing(early):
            step()
        for item in early[:2]:
            item.finish()
        v_gains[...] = jnp.zeros_like(v_gains)
        group = PAIR // per
        for first in range(0, ranks, group):
            at = slice(first * per, (first + group) * per)
            v_table[:, at] = jnp.concatenate([s_table[one] for one in range(first, first + group)], axis=0).T
            v_gains[:n_gains, at] = jnp.concatenate(
                [packed_gains[one, :n_gains, :per] for one in range(first, first + group)], axis=1
            ).astype(F32)
        early[2].finish()

        def weights_ready(kinds):
            def before():
                queue.flush(kinds[-1])
                for kind in kinds:
                    gathers[kind].finish()

            return before

        def put_mats(value):
            o_proj[0:3] = value

        def put_out(value):
            o_out[0] = value

        def put_up(value):
            o_up[...] = value

        def put_down(value):
            o_down[...] = value

        def put_pos(value):
            o_table[...] = value

        def put_gain(value):
            o_gain[...] = value[:n_gains, :per].reshape(n_gains, 1, per)

        def put_cross(value):
            o_proj[3] = value[0]
            o_out[1] = value[1]
            handing[...] = value[2:4]

        hand = remote(handing, handed, hand_sems.at[0], hand_sems.at[1], place.partner)

        def feed_sums():
            place.meet(ready.at[0])
            for kind in (UP, DOWN):
                scatters[kind].begin()

        def table_sums():
            scatters[TABLE].begin()
            for at in range(ranks):
                gain = s_gains[:, at * per : (at + 1) * per]
                gain = jnp.concatenate([gain, jnp.zeros((8, per), F32)], axis=0)
                packed_gains[at] = jnp.concatenate([gain, jnp.zeros((16, PAIR - per), F32)], axis=1).astype(BF)
            scatters[GAIN].begin()

        def table_on(ready_steps):
            for step in firsts([scatters[TABLE], scatters[GAIN]]):
                step()
            for _ in range(min(ready_steps, len(queue.steps))):
                step = queue.next()
                if step is not None:
                    step()

        def last_sums(also=()):
            scatters[MATS].begin()
            pair = [scatters[TABLE], scatters[GAIN]]
            for step in firsts([scatters[MATS]]):
                step()
            queue.flush()
            if also:
                scatters[CROSS].finish(put_cross)
                hand.start()
            for step in seconds(also) + seconds(pair) + seconds([scatters[MATS]]):
                step()
            puts = {
                UP: put_up, DOWN: put_down, OUT: put_out, MATS: put_mats, TABLE: put_pos, GAIN: put_gain,
            }
            for kind, put in puts.items():
                scatters[kind].finish(put)
    else:
        partner = {"section": 1 - section}
        barrier = pltpu.get_barrier_semaphore()
        pl.semaphore_signal(barrier, inc=1, device_id=partner, device_id_type=MESH)
        pl.semaphore_wait(barrier, 1)

    def persistent():
        if line:
            return [Ready(buf) for buf in (v_table, v_gains, v_mats, v_up, v_down, v_cross)]
        order = (4, 5, 0, 2, 3, 1)
        return [
            load(given[at], buf) for at, buf in zip(order, (v_table, v_gains, v_mats, v_up, v_down, v_cross))
        ]

    def finish(items):
        for item in items:
            item.wait()

    @pl.when(section == 0)
    def _():
        count[0] = 0
        w_table, w_gains, w_mats, w_up, w_down, _ = first = persistent()
        if line:
            gathers[DOWN].begin_along()
            pair = [gathers[UP], gathers[DOWN]]
            queue.add(None, *passing(pair[:1]), *passing(pair[1:]), *sharing(pair), DOWN)
            w_up.before = weights_ready((UP, DOWN))
        base = count[0]
        src, mixed, dy, dmixed, dq = pool["tok"][:5]
        x1, x2, dx, dv = pool["tok32"]
        hidden, slope = pool["hidden"]
        dy_t, a_t = pool["tokt"]
        v_qkv, v_weights = pool["qkv"][0], pool["weights"][0]
        for m in range(micro):
            count[0] = base
            k_qkv, k_weights, k_mixed = kept[m][:3]
            sinks = [store(k_qkv, v_qkv, axis=1), store(k_weights, v_weights), store(k_mixed, mixed)]
            encode_attend(
                load(own.at[m], src), w_table, w_gains, *code_loads(m), w_mats, *sinks, codes, cols, queue
            )
            if line and m == 0:
                lend.wait_send()
            early_sinks = sinks
            _, _, _, k_x1, k_x2, k_hidden, k_slope, _ = kept[m]
            sinks = [store(k_x1, x1), store(k_x2, x2), store(k_hidden, hidden), store(k_slope, slope)]
            encode_feed(
                Ready(src), Ready(mixed), w_table, w_gains, w_mats, w_up, w_down, box(m), *sinks,
            )
            memory = pltpu.make_async_copy(outbox.at[m], whole.at[m], local.at[sems(1)])
            memory.start()
            finish(early_sinks + sinks + [memory])
        for m in range(micro):
            count[0] = base
            last = line and m == micro - 1
            k_qkv, k_weights, k_mixed, k_x1, k_x2, k_hidden, k_slope, _ = kept[m]
            loads = [load(k_x2, x2), load(k_slope, slope), load(k_x1, x1), load(k_hidden, hidden)]
            late = [load(k_mixed, mixed), load(k_qkv, v_qkv), load(k_weights, v_weights), load(own.at[m], src)]
            sink = store(g_in.at[m], x2)
            sums = [Total(buf, m == 0) for buf in (s_mats, s_up, s_down, s_table, s_gains)]

            def fed():
                if last:
                    feed_sums()
                    scatters[OUT].begin()
                    up_steps, down_steps = seconds([scatters[UP]]), seconds([scatters[DOWN]])
                    queue.add(*in_groups(firsts([scatters[kind] for kind in (UP, DOWN, OUT)]), 4))
                    queue.add(None, None, up_steps[0], None, None, down_steps[0], None, None, up_steps[1])
                    rest = seconds([scatters[kind] for kind in (UP, DOWN, OUT)])
                    queue.add(rest[2], *rest[4:])

            encode_back(
                loads[0], box(m), w_gains, loads[1], w_down, w_up, loads[2], w_mats, loads[3], *late[:3],
                late[3], w_table, sink, *sums, dy, dy_t, a_t, dx, dmixed, dq, x1, dv,
                queue, fed, *((table_sums, partial(table_on, 3)) if last else (nothing, nothing)),
            )
            finish([sink])
        if line:
            last_sums()
            hand.wait_recv()
            o_proj[3] = handed[0]
            o_out[1] = handed[1]
        for item in first:
            item()

    @pl.when(section == 1)
    def _():
        count[0] = 0
        w_table, w_gains, w_mats, w_up, w_down, w_cross = first = persistent()
        if line:
            gathers[UP].begin_along()
            gathers[DOWN].begin_along()
            one, two, three = [[gathers[kind]] for kind in (CROSS, UP, DOWN)]
            queue.add(*passing(one), None, *passing(two), *sharing(one), CROSS, *passing(three))
            queue.add(*sharing(two), UP, *sharing(three), DOWN)
            w_cross.before = weights_ready((CROSS,))
            w_up.before = weights_ready((UP, DOWN))
        base = count[0]
        hidden, dup = pool["hidden"]
        a_t, b_t = pool["tokt"]
        v_qkv, v_weights = pool["qkv"][0], pool["weights"][0]
        for m in range(micro):
            count[0] = base
            k_qkv, k_weights, k_mixed, k_h1 = kept[m][:4]
            tgt, mixed = pool["tok"][:2]
            sinks = [
                store(k_qkv, v_qkv, axis=1), store(k_weights, v_weights), store(k_mixed, mixed),
                store(k_h1, pool["tok32"][0]),
            ]
            self_forward(
                load(own.at[m], tgt), w_table, w_gains, *code_loads(m), w_mats, *sinks, codes, cols, queue
            )
            finish(sinks)
        for m in range(micro):
            count[0] = base
            k_h1, k_dh1, k_hidden, k_dup, k_a = kept[m][3:8]
            v_cot, out, mixed, dy, dmixed, dq = pool["tok"]
            h1, h2, dk, dv = pool["tok32"]
            sums = [Total(buf, m == 0) for buf in (s_cross, s_gains)]
            sinks = [store(whole.at[m], out), store(k_dh1, h2)]
            feeds = [store(k_a, a_t, split=False), store(k_dup, dup), store(k_hidden, hidden)]
            cross(
                load(k_h1, h1), w_gains, *code_loads(m), w_cross, box(m), w_up, w_down,
                load(cot.at[m], v_cot), sinks[0], box(m), sinks[1], *sums, *feeds, codes, cols, v_qkv,
                v_weights, mixed, h2, dy, b_t, dmixed, dq, dk, dv,
            )
            finish(sinks + feeds)
        for m in range(micro):
            count[0] = base
            k_hidden, k_dup, k_a = kept[m][5:8]
            sums = [Total(buf, m == 0) for buf in (s_up, s_down)]
            feed_grads(
                load(k_a, a_t), load(k_dup, dup), load(cot.at[m], pool["tok"][0]), load(k_hidden, hidden),
                *sums, b_t,
            )
        if line:
            feed_sums()
            pair = [scatters[UP], scatters[DOWN]]
            scatters[CROSS].begin()
            steps, late = seconds([scatters[CROSS]]), seconds(pair)
            queue.add(*in_groups(firsts([scatters[CROSS]]) + firsts(pair), 4), None, None, steps[0], None, None)
            queue.add(steps[1], None, steps[2], None, steps[3], late[0], late[1], None, None, late[2], None)
            queue.add(late[3], None, None, late[4], None, *late[5:])
        for m in range(micro):
            count[0] = base
            k_qkv, k_weights, k_mixed, _, k_dh1 = kept[m][:5]
            tgt, mixed, dy, dmixed, dq = pool["tok"][:5]
            dh1, grad, dk, dv = pool["tok32"]
            loads = [load(k_dh1, dh1), load(k_mixed, mixed), load(k_qkv, v_qkv), load(k_weights, v_weights)]
            sink = store(g_in.at[m], grad)
            sums = [Total(s_mats, m == 0), Total(s_table, m == 0), Total(s_gains, False)]
            last = line and m == micro - 1

            def mixed_done():
                if last:
                    scatters[OUT].begin()
                    queue.steps = in_groups(firsts([scatters[OUT]]), 4) + queue.steps

            self_back(
                loads[0], w_mats, *loads[1:], load(own.at[m], tgt), w_table, w_gains, sink, *sums, dy, a_t,
                b_t, dmixed, dq, dk, dv, queue, mixed_done,
                *((table_sums, partial(table_on, 100)) if last else (nothing, nothing)),
            )
            finish([sink])
        if line:
            last_sums([scatters[OUT]])
            hand.wait_send()
        for item in first:
            item()

    for m in range(micro):
        box(m).wait()
    if not line:
        copies = [
            pltpu.make_async_copy(buf, out, local.at[at])
            for at, (buf, out) in enumerate(zip((s_mats, s_cross, s_up, s_down, s_table, s_gains), results))
        ]
        for copy in copies:
            copy.start()
        for copy in copies:
            copy.wait()


def run_step(z, line, given, results, own, cot, segments, levels):
    micro, length = own.shape[:2]
    parts = length // TB
    args = [*given, own, cot, segments, levels]
    outs = [z["outputs"], z["g_in"], *results] + [z[name] for _ in range(micro) for name in KEPT]
    scratch = [z[name] for name in PERSISTENT]
    scratch += [z[name] for name, number in POOL for _ in range(number)]
    dma = pltpu.SemaphoreType.DMA
    sems = [dma((64,)), dma((micro, parts)), dma((micro, parts))]
    if line:
        per, width = given[0].shape[1:]
        slots = 4 * LINE
        own_scratch = [
            shape((slots,) + z["packed_gains"].shape[1:], BF),
            z["packed_gains"], shape((2, per, width), F32), shape((2, per, width), F32),
        ]
        sems_line = [dma((KINDS, LINE - 1))] * 2 + [dma((KINDS, LINE))] * 2 + [dma((KINDS, 2 * LINE))] * 2
        sems_line += [dma((KINDS, LINE - 1))] * 2 + [dma((KINDS, LINE))] * 2 + [dma((KINDS, LINE, 2))] * 2
        sems_line += [pltpu.SemaphoreType.REGULAR((1,)), dma((2,)), dma((2,))]
    in_vmem, anywhere = pl.BlockSpec(memory_space=pltpu.VMEM), pl.BlockSpec(memory_space=pl.ANY)
    edge = in_vmem if line else anywhere
    vmem = [pltpu.VMEM(s.shape, s.dtype) for s in scratch]
    if line:
        scratch_shapes = vmem + sems + [pltpu.VMEM(s.shape, s.dtype) for s in own_scratch] + sems_line
    else:
        scratch_shapes = vmem + sems
    outs = pl.pallas_call(
        partial(step_kernel, z, line),
        out_shape=outs,
        in_specs=[edge] * 6 + [anywhere] * 4,
        out_specs=[anywhere] * 2 + [edge] * 6 + [anywhere] * (len(outs) - 8),
        scratch_shapes=scratch_shapes,
        compiler_params=pltpu.CompilerParams(
            collective_id=0, has_side_effects=True, vmem_limit_bytes=VMEM_BYTES
        ),
        name="step",
    )(*args)
    return place_outputs(outs[:8]) if line else outs[:8]


def place_kernel(count, *refs):
    ins, outs, bufs, sems = refs[:count], refs[count : 2 * count], refs[2 * count : 3 * count], refs[-1]
    pieces = []
    for src, dst, buf in zip(ins, outs, bufs):
        parts = 4 if src.shape[-2] % 64 == 0 else 1
        rows = src.shape[-2] // parts
        for part in range(parts):
            view = (slice(None),) * (len(src.shape) - 2) + (slice(part * rows, (part + 1) * rows),)
            pieces.append((src.at[view], buf.at[view], dst.at[view]))
    first = [pltpu.make_async_copy(src, buf, sems.at[0, at]) for at, (src, buf, _) in enumerate(pieces)]
    second = [pltpu.make_async_copy(buf, dst, sems.at[1, at]) for at, (_, buf, dst) in enumerate(pieces)]
    for copy in first:
        copy.start()
    for one, other in zip(first, second):
        one.wait()
        other.start()
    for copy in second:
        copy.wait()


def place_outputs(arrays):
    anywhere = pl.BlockSpec(memory_space=pl.ANY)
    kinds = [shape(array.shape, array.dtype) for array in arrays]
    return pl.pallas_call(
        partial(place_kernel, len(arrays)),
        out_shape=kinds,
        in_specs=[anywhere] * len(arrays),
        out_specs=[anywhere] * len(arrays),
        scratch_shapes=[pltpu.VMEM(kind.shape, kind.dtype) for kind in kinds]
        + [pltpu.SemaphoreType.DMA((2, 4 * len(arrays)))],
        compiler_params=pltpu.CompilerParams(vmem_limit_bytes=VMEM_BYTES),
        name="place",
    )(*arrays)


def body(
    inputs,
    positions,
    projections,
    out_projections,
    ffn_up,
    ffn_down,
    norm_gains,
    segments,
    levels,
    cotangent,
):
    micro, _, length, width = inputs.shape[1:]
    ranks = lax.axis_size("dp")
    per, n_gains = width // ranks, norm_gains.shape[1]
    z = sizes(length, width, ffn_up.shape[2], micro, ranks)
    rows = (inputs[0, :, 0], cotangent[:, 0], segments, levels)
    line = ranks == 4 * LINE and per * 4 == PAIR and n_gains <= 8
    if line:
        gain = norm_gains.transpose(1, 0, 2)
        given = (projections[0], out_projections[0], ffn_up[0], ffn_down[0], positions[0].T, gain)
        results = [shape(item.shape, F32) for item in given]
        whole, g_in, d_proj, d_out, d_up, d_down, d_table, d_gain = run_step(z, True, given, results, *rows)
        d_table, d_gain = d_table.T[None], d_gain.transpose(1, 0, 2)
    else:
        every = lambda value, axis: lax.all_gather(value.astype(BF), "dp", axis=axis, tiled=True)
        part = lambda value, axis: lax.psum_scatter(value, "dp", scatter_dimension=axis, tiled=True)
        to_section = lambda value, source: lax.ppermute(value, "section", [(source, 1 - source)])
        proj, outp = projections[0].astype(BF), out_projections[0].astype(BF)
        mine = jnp.stack([proj[3], outp[1]])
        gains = every(norm_gains[0], 1).astype(F32)
        given = (
            every(jnp.stack([proj[0], proj[1], proj[2], outp[0]]), 1),
            every(jnp.concatenate([mine, to_section(mine, 0)]), 1),
            every(ffn_up[0], 0), every(ffn_down[0], 0).reshape(z["down_parts"].shape), every(positions[0], 1),
            jnp.concatenate([gains, jnp.zeros((8 - n_gains, width), F32)]),
        )
        results = [z[name] for name in ("mats", "mats", "up", "down", "packed", "gains")]
        whole, g_in, d_mats, d_cross, d_up, d_down, d_table, d_gain = run_step(z, False, given, results, *rows)
        d_mats, d_cross = part(d_mats, 1).astype(F32), part(d_cross, 1)
        back = to_section(d_cross[2:], 1)
        more = jnp.where(lax.axis_index("section") == 0, back, d_cross[:2]).astype(F32)
        d_proj = jnp.concatenate([d_mats[:3], more[:1]])
        d_out = jnp.concatenate([d_mats[3:], more[1:]])
        d_up, d_down = part(d_up, 0).astype(F32), part(d_down, 0).astype(F32)
        d_table = part(d_table, 0)[0].astype(F32).T[None]
        d_gain = part(d_gain, 1)[None, :n_gains]
    return (
        whole[None, :, None],
        g_in[None, :, None],
        d_table,
        d_proj[None],
        d_out[None],
        d_up[None],
        d_down[None],
        d_gain,
    )


def solution(mesh):
    in_specs = (
        P("section", None, "dp", None, None),
        P("section", None, "dp"),
        P("section", None, "dp", None),
        P("section", None, "dp", None),
        P("section", "dp", None),
        P("section", "dp", None),
        P("section", None, "dp"),
        P(None, "dp", None),
        P(None, None, "dp", None),
        P(None, "dp", None, None),
    )
    out_specs = (
        P("section", None, "dp", None, None),
        P("section", None, "dp", None, None),
        P("section", None, "dp"),
        P("section", None, "dp", None),
        P("section", None, "dp", None),
        P("section", "dp", None),
        P("section", "dp", None),
        P("section", None, "dp"),
    )
    return jax.shard_map(body, mesh=mesh, in_specs=in_specs, out_specs=out_specs, check_vma=False)
```
